512 devices in a mesh: dp: 32 (over y, x), context: 16 (over z, core).
Axes of the slice: x: 4, y: 8, z: 8, core: 2. Of those that a mesh axis runs over, the one named last changes fastest.
Arguments:
- queries: bfloat16 [32, 2048, 4096], P('dp', 'context'), may hold values from -152 to 152
- keys: bfloat16 [32, 2048, 512], P('dp', 'context'), may hold values from -8 to 8
- values: bfloat16 [32, 2048, 512], P('dp', 'context'), may hold values from -6 to 6
- out_grad: bfloat16 [32, 2048, 4096], P('dp', 'context'), may hold values from -6 to 6
- layer_input: bfloat16 [32, 2048, 8192], P('dp', 'context'), may hold values from -0.1875 to 0.1875
- doc_blocks: int32 [32, 5], P('dp'), may hold values from 1 to 8, 16 in all within a row
Outputs:
- key_grad: bfloat16 [32, 2048, 512], P('dp', 'context')
- wv_grad: float32 [8192, 512], P(('dp', 'context'))
The draws below stay inside these ranges and needn't reach their ends.
Inputs may be any that keep to these rules, and one draw needn't show every extreme that they name: `doc_blocks`: each row lists, in mask blocks of 128 tokens, the lengths of the documents packed one after another into that sequence; they sum to 16, and the longest has exactly 8 blocks.
All inputs are finite; a program needn't handle non-finite values.
Results may differ from the reference program's by a relative error of at most 0.035.
Values may be sent and summed in bfloat16 or wider, within the bound.
A program may use at most 64 MiB of HBM per device.

```python
import math
import jax
import jax.numpy as jnp
import numpy as np
from jax import lax

D = 8192
HQ = 32
KEY_VALUE_HEADS = 4
HEAD_SIZE = 128
QUERY_PER_GROUP = 8
BLK = 128
TOKENS_ON_CARD = 128
PACKED_COUNT = 32
SEQUENCE_LENGTH = 2048
NBLK = 16
MOST = 8
NDOCS = 5
WIDTH = 8
N_DP = 32
N_CONTEXT = 16


def draw_queries(key, part):
    key = jax.random.fold_in(key, 3)
    return jnp.clip(jax.random.normal(key, (PACKED_COUNT, SEQUENCE_LENGTH, HQ * HEAD_SIZE), jnp.float32), -4.0, 4.0).astype(jnp.bfloat16)


def draw_keys(key, part):
    key = jax.random.fold_in(key, 5)
    return jnp.clip(jax.random.normal(key, (PACKED_COUNT, SEQUENCE_LENGTH, KEY_VALUE_HEADS * HEAD_SIZE), jnp.float32), -4.0, 4.0).astype(jnp.bfloat16)


def strengthened(values, stream_key, source, target, shards_of, factor):
    def block_of(dim):
        return (jnp.arange(values.shape[dim]) // (values.shape[dim] // shards_of)).reshape((-1,) + (1,) * (values.ndim - 1 - dim))

    one_side = jax.random.permutation(stream_key, shards_of)[block_of(target)]
    other_side = (block_of(target) + shards_of // 2) % shards_of
    return jnp.where((block_of(source) == one_side) | (block_of(source) == other_side), factor * values, values)


def level_of(stream_key, extent, cuts, low, top_value):
    def one(position, parts):
        draws = jax.random.uniform(jax.random.fold_in(jax.random.fold_in(stream_key, 6), position), (parts,), jnp.float32, low / len(cuts), top_value / len(cuts))
        return jnp.repeat(jnp.exp(draws), extent[position] // parts).reshape((-1,) + (1,) * (len(extent) - position - 1))

    factor_of = one(*cuts[0])
    for cut in cuts[1:]:
        factor_of = factor_of * one(*cut)
    return factor_of


def split_up(count, total, most, slope):
    portions = [(1 << 20) // math.isqrt(rank ** slope) + 1 for rank in range(2, count + 1)]
    surplus, given = total - most - (count - 1), [1] * (count - 1)
    while surplus > 0:
        movable = [i for i in range(count - 1) if given[i] < most]
        mass, left = sum([portions[i] for i in movable]), surplus
        for i in movable:
            more = min(most - given[i], max(1, left * portions[i] // mass), surplus)
            given[i] = given[i] + more
            surplus = surplus - more
    return np.array([most] + given)


def ragged(rng, number_of, total, limit, skew):
    if number_of == 2:
        one = jax.random.randint(rng, (), max(1, total - limit), min(limit, total - 1) + 1)
        return jnp.stack([one, total - one])
    sizes = jnp.asarray(split_up(number_of, total, limit, skew), jnp.int32)
    pairs = (number_of - 1) // 2
    giver, taker = sizes[1:1 + 2 * pairs:2], sizes[2:2 + 2 * pairs:2]
    room = jnp.minimum(giver - 1, limit - taker)
    passed = jax.random.randint(jax.random.fold_in(rng, 1), (pairs,), 0, 1 << 20) % (room + 1)
    sizes = sizes.at[1:1 + 2 * pairs:2].set(giver - passed).at[2:2 + 2 * pairs:2].set(taker + passed)
    return sizes[jax.random.permutation(jax.random.fold_in(rng, 2), number_of)]


def bell_draw(key, extent, deviation, bound, split=(), kind=jnp.bfloat16):
    entries = jax.random.normal(key, extent, jnp.float32) * deviation
    if len(split) > 0:
        entries = level_of(key, extent, split, -0.22, 0.18) * entries
    return jnp.clip(entries, min=-bound, max=bound).astype(kind)


def gaussian_with(rng, shape, scale, limit, split, heavy, held_as=jnp.bfloat16):
    array = scale * jax.random.normal(rng, shape, jnp.float32)
    if split:
        array = array * level_of(rng, shape, split, -0.22, 0.18)
    return jnp.clip(strengthened(array, jax.random.fold_in(rng, 3), *heavy), -limit, limit).astype(held_as)


def setup_inputs(seed: int = 0) -> dict:
    seeds = jax.random.split(jax.random.key(seed), 7)
    queries = draw_queries(jax.random.fold_in(seeds[6], 71), 0)
    keys = draw_keys(jax.random.fold_in(seeds[6], 71), 0)
    values = bell_draw(seeds[2], (PACKED_COUNT, SEQUENCE_LENGTH, KEY_VALUE_HEADS * HEAD_SIZE), 1.0, 6.0, ((0, 32), (1, 16)))
    out_grad = bell_draw(seeds[3], (PACKED_COUNT, SEQUENCE_LENGTH, HQ * HEAD_SIZE), 1.0, 6.0, ((0, 32), (1, 16)))
    layer_input = gaussian_with(seeds[4], (PACKED_COUNT, SEQUENCE_LENGTH, D), (4.0 * (N_DP * SEQUENCE_LENGTH) ** -0.5), 0.1875, ((0, 32), (1, 16)), (0, 2, 32, 2.75))
    doc_blocks = jax.vmap(lambda own: ragged(own, NDOCS, NBLK, MOST, 2))(jax.random.split(seeds[5], PACKED_COUNT)).reshape((PACKED_COUNT, NDOCS)).astype(jnp.int32)
    return dict(queries=queries, keys=keys, values=values, out_grad=out_grad, layer_input=layer_input, doc_blocks=doc_blocks)


MASKED = -1e+30

def block_documents(lengths):
    doc_ends = jnp.cumsum(lengths, dtype=jnp.int32)
    block_index = jnp.arange(NBLK, dtype=jnp.int32)
    return lax.optimization_barrier(jnp.sum((block_index[:, None] >= doc_ends[None, :]).astype(jnp.int32), axis=1, dtype=jnp.int32))

def sequence_grads(query_sequence, key_sequence, value_sequence, gradient_sequence, lengths):
    scale = 1.0 / math.sqrt(HEAD_SIZE)
    leading_dims = (WIDTH - 1) * TOKENS_ON_CARD
    span_length = WIDTH * TOKENS_ON_CARD
    token_doc = jnp.repeat(block_documents(lengths), BLK)
    padded_doc = jnp.concatenate([jnp.full((leading_dims,), -1, jnp.int32), token_doc.astype(jnp.int32)])
    key_padded_rows = jnp.concatenate([jnp.zeros((leading_dims, KEY_VALUE_HEADS * HEAD_SIZE), jnp.bfloat16), key_sequence])
    value_padded_rows = jnp.concatenate([jnp.zeros((leading_dims, KEY_VALUE_HEADS * HEAD_SIZE), jnp.bfloat16), value_sequence])

    def per_device(carry, device):
        key_overall, value_overall = carry
        start_offset = (device * TOKENS_ON_CARD).astype(jnp.int32)
        key_region = lax.dynamic_slice_in_dim(key_padded_rows, start_offset, span_length, 0).reshape(span_length, KEY_VALUE_HEADS, HEAD_SIZE)
        value_region = lax.dynamic_slice_in_dim(value_padded_rows, start_offset, span_length, 0).reshape(span_length, KEY_VALUE_HEADS, HEAD_SIZE)
        key_doc = lax.dynamic_slice_in_dim(padded_doc, start_offset, span_length, 0)
        query_tile_rows = lax.dynamic_slice_in_dim(query_sequence, start_offset, TOKENS_ON_CARD, 0).reshape(TOKENS_ON_CARD, KEY_VALUE_HEADS, QUERY_PER_GROUP, HEAD_SIZE)
        gradient_block = lax.dynamic_slice_in_dim(gradient_sequence, start_offset, TOKENS_ON_CARD, 0).reshape(TOKENS_ON_CARD, KEY_VALUE_HEADS, QUERY_PER_GROUP, HEAD_SIZE)
        query_doc = lax.dynamic_slice_in_dim(token_doc.astype(jnp.int32), start_offset, TOKENS_ON_CARD, 0)
        query_pos = start_offset + jnp.arange(TOKENS_ON_CARD, dtype=jnp.int32)
        key_pos = start_offset - leading_dims + jnp.arange(span_length, dtype=jnp.int32)
        allowed = (key_pos[None, :] <= query_pos[:, None]) & (key_doc[None, :] == query_doc[:, None])
        scores = jnp.einsum('tghd,sgd->ghts', query_tile_rows.astype(jnp.float32), key_region.astype(jnp.float32)) * scale
        scores = jnp.where(allowed[None, None], scores, MASKED)
        row_max = lax.optimization_barrier(jnp.max(scores, axis=3, keepdims=True))
        exponent = jnp.where(allowed[None, None], jnp.exp(scores - row_max), 0.0)
        probability = exponent / lax.optimization_barrier(jnp.sum(exponent, axis=3, keepdims=True))
        weights = probability.astype(jnp.bfloat16)
        attended = jnp.einsum('ghts,sgd->tghd', weights.astype(jnp.float32), value_region.astype(jnp.float32)).astype(jnp.bfloat16)
        delta = lax.optimization_barrier(jnp.sum(gradient_block.astype(jnp.float32) * attended.astype(jnp.float32), axis=3))
        prob_grad = jnp.einsum('tghd,sgd->ghts', gradient_block.astype(jnp.float32), value_region.astype(jnp.float32))
        score_grad = (probability * (prob_grad - jnp.transpose(delta, (1, 2, 0))[..., None])).astype(jnp.bfloat16)
        value_portion = jnp.einsum('ghts,tghd->sgd', weights.astype(jnp.float32), gradient_block.astype(jnp.float32))
        key_portion = jnp.einsum('ghts,tghd->sgd', score_grad.astype(jnp.float32), query_tile_rows.astype(jnp.float32)) * scale
        key_overall = lax.dynamic_update_slice_in_dim(key_overall, lax.dynamic_slice_in_dim(key_overall, start_offset, span_length, 0) + key_portion.reshape(span_length, KEY_VALUE_HEADS * HEAD_SIZE), start_offset, 0)
        value_overall = lax.dynamic_update_slice_in_dim(value_overall, lax.dynamic_slice_in_dim(value_overall, start_offset, span_length, 0) + value_portion.reshape(span_length, KEY_VALUE_HEADS * HEAD_SIZE), start_offset, 0)
        return ((key_overall, value_overall), None)
    empty_result = jnp.zeros((leading_dims + SEQUENCE_LENGTH, KEY_VALUE_HEADS * HEAD_SIZE), jnp.float32)
    (key_overall, value_overall), _ = lax.scan(per_device, (empty_result, empty_result), jnp.arange(N_CONTEXT, dtype=jnp.int32))
    return (key_overall[leading_dims:], value_overall[leading_dims:])

def reference(queries, keys, values, out_grad, layer_input, doc_blocks):

    def one_sequence(pieces):
        return sequence_grads(*pieces)
    key_sum, value_sum = lax.map(one_sequence, (queries, keys, values, out_grad, doc_blocks))
    value_gradient = value_sum.astype(jnp.bfloat16)
    flat_input = layer_input.reshape(PACKED_COUNT * SEQUENCE_LENGTH, D)
    flattened_value = value_gradient.reshape(PACKED_COUNT * SEQUENCE_LENGTH, KEY_VALUE_HEADS * HEAD_SIZE)
    wv_grad = lax.dot_general(flat_input, flattened_value, (((0,), (0,)), ((), ())), preferred_element_type=jnp.float32)
    return (key_sum.astype(jnp.bfloat16), wv_grad)
```

```python
import math

import jax
import jax.numpy as jnp
from jax import lax
from jax.experimental import pallas as pl
from jax.experimental.pallas import tpu as pltpu
from jax.sharding import PartitionSpec as P

HEAD = 128
BLK = 128
NX, NY, NZ = 4, 8, 8
HOPS = 4
ROWS = 1152
MASKED = -1e30
SCALE = 1.0 / math.sqrt(HEAD)
MESH = pl.DeviceIdType.MESH
F32 = jnp.float32
BF16 = jnp.bfloat16


def place():
    d = lax.axis_index("dp")
    c = lax.axis_index("context")
    return lax.rem(d, NX), lax.div(d, NX), lax.div(c, 2), lax.rem(c, 2)


def device(x, y, z, h):
    return (y * NX + x, z * 2 + h)


def around(i, by, n):
    return lax.rem(i + (by + n), n)


class Copies:
    def __init__(self, send, recv):
        self.send, self.recv, self.used, self.all = send, recv, 0, []

    def remote(self, src, dst, target):
        i = self.used
        self.used += 1
        copy = pltpu.make_async_remote_copy(
            src_ref=src,
            dst_ref=dst,
            send_sem=self.send.at[i],
            recv_sem=self.recv.at[i],
            device_id=target,
            device_id_type=MESH,
        )
        copy.start()
        self.all.append(copy)
        return copy

    def local(self, src, dst):
        i = self.used
        self.used += 1
        copy = pltpu.make_async_copy(src, dst, self.send.at[i])
        copy.start()
        return copy

    def wait_sends(self):
        for copy in self.all:
            copy.wait_send()


def greet(targets):
    barrier = pltpu.get_barrier_semaphore()
    for target in targets:
        pl.semaphore_signal(barrier, inc=1, device_id=target, device_id_type=MESH)
    pl.semaphore_wait(barrier, len(targets))


def lanes(start, size):
    return pl.ds(pl.multiple_of(start, 128), size)


def rows_at(start, size):
    return pl.ds(pl.multiple_of(start, 128), size)


def gather_kernel(q, g, k, v, xin, qg, kv, xg, send, recv):
    x, y, z, h = place()
    sib = device(x, y, z, 1 - h)
    up = device(x, y, around(z, 1, NZ), h)
    down = device(x, y, around(z, -1, NZ), h)
    across = [device(around(x, dx, NX), y, z, h) for dx in range(1, NX)]
    greet([sib, up, down] + across)
    copies = Copies(send, recv)
    mine = rows_at(h * BLK, BLK)

    first = []
    for a in range(2):
        for j, src in enumerate((k, v)):
            theirs = src.at[:, lanes((2 * (1 - h) + a) * HEAD, HEAD)]
            own = src.at[:, lanes((2 * h + a) * HEAD, HEAD)]
            first.append(
                (
                    copies.remote(theirs, kv.at[a, j, mine], sib),
                    copies.local(own, kv.at[a, j, mine]),
                )
            )
    exchange = []
    for j, src in enumerate((q, g)):
        exchange.append(copies.remote(src.at[:, lanes((1 - h) * 2048, 2048)], qg.at[j, mine], sib))
    hops = [[], []]
    for a in range(2):
        for remote, local in first[2 * a : 2 * a + 2]:
            remote.wait_recv()
            local.wait()
        hops[a].append(copies.remote(kv.at[a, :, pl.ds(0, 256)], kv.at[a, :, pl.ds(256, 256)], up))
    spread = [[] for _ in range(NX)]
    for dx in (1, 3, 2):
        to = around(x, dx, NX)
        for c in range(NY):
            spread[dx].append(
                copies.remote(
                    xin.at[:, lanes(c * 1024 + to * 256, 256)],
                    xg.at[dx, mine, pl.ds(c * 256, 256)],
                    across[dx - 1],
                )
            )
    own_x = [
        copies.local(
            xin.at[:, lanes(c * 1024 + x * 256, 256)], xg.at[0, mine, pl.ds(c * 256, 256)]
        )
        for c in range(NY)
    ]
    own_q = [
        copies.local(src.at[:, lanes(h * 2048, 2048)], qg.at[j, mine])
        for j, src in enumerate((q, g))
    ]
    for s in range(1, HOPS):
        for a in range(2):
            hops[a][s - 1].wait_recv()
            lo = s * 256 + (128 if s == 3 else 0)
            size = 128 if s == 3 else 256
            hops[a].append(
                copies.remote(
                    kv.at[a, :, pl.ds(lo, size)], kv.at[a, :, pl.ds((s + 1) * 256, size)], up
                )
            )
    for copy in own_x:
        copy.wait()
    passed = [copies.remote(xg.at[0, mine], xg.at[0, mine], sib)]
    for dx in (1, 3, 2):
        for copy in spread[dx]:
            copy.wait_recv()
        passed.append(copies.remote(xg.at[dx, mine], xg.at[dx, mine], sib))
    for a in range(2):
        hops[a][3].wait_recv()
    for copy in exchange + passed:
        copy.wait_recv()
    for copy in own_q:
        copy.wait()
    copies.wait_sends()


def attend_kernel(docs, q, g, kv, dk, dv, bias):
    _, _, z, _ = place()

    @pl.when(pl.program_id(0) == 0)
    def _():
        ends = []
        total = docs[0, 0]
        for i in range(5):
            ends.append(total)
            if i < 4:
                total = total + docs[0, i + 1]

        def doc(b):
            return sum((b >= e).astype(jnp.int32) for e in ends)

        key = lax.broadcasted_iota(jnp.int32, (BLK, BLK), 0)
        query = lax.broadcasted_iota(jnp.int32, (BLK, BLK), 1)
        for j in range(2):
            qb = 2 * z + j
            for i in range(9):
                kb = 2 * z - 2 * (i // 2) + (1 if i == 8 else i % 2)
                if i < 2 and i == j:
                    block = jnp.where(key <= query, 0.0, MASKED)
                elif i == 1 and j == 0:
                    block = jnp.full((BLK, BLK), MASKED, F32)
                else:
                    same = (kb >= 0) & (doc(kb) == doc(qb))
                    block = jnp.full((BLK, BLK), jnp.where(same, 0.0, MASKED), F32)
                bias[pl.ds(i * BLK, BLK), pl.ds(j * BLK, BLK)] = block

    keys = kv[0, 0]
    values = kv[0, 1]
    dk[0] = jnp.zeros((ROWS, HEAD), F32)
    dv[0] = jnp.zeros((ROWS, HEAD), F32)

    def one(head):
        col = lanes(head * HEAD, HEAD)
        qh = q[0, :, col]
        gh = g[0, :, col]
        contract = (((1,), (1,)), ((), ()))
        s = lax.dot_general(keys, qh, contract, preferred_element_type=F32)
        dp = lax.dot_general(values, gh, contract, preferred_element_type=F32)
        t = s * (SCALE * math.log2(math.e)) + bias[...]
        m = jnp.max(t, axis=0, keepdims=True)
        e = jnp.exp2(t - m)
        p = e * (1.0 / jnp.sum(e, axis=0, keepdims=True))
        delta = jnp.sum(p * dp, axis=0, keepdims=True)
        ds = (p * (dp - delta)).astype(BF16)
        dv[0] += jnp.dot(p.astype(BF16), gh, preferred_element_type=F32)
        dk[0] += jnp.dot(ds, qh, preferred_element_type=F32)

    @pl.loop(0, 4)
    def _(i):
        one(2 * i)
        one(2 * i + 1)


def reduce_kernel(
    dk, dv, xg, key_grad, wv_grad, xs, csend, crecv, dvt, part, ysend, yrecv, zsend, zrecv, kswap, send, recv
):
    x, y, z, h = place()
    sib = device(x, y, z, 1 - h)
    up = device(x, y, around(z, 1, NZ), h)
    down = device(x, y, around(z, -1, NZ), h)
    across = [device(around(x, dx, NX), y, z, h) for dx in range(1, NX)]
    ahead = device(x, around(y, 1, NY), z, h)
    behind = device(x, around(y, -1, NY), z, h)
    ctx = z * 2 + h
    column = [(y * NX + x, around(ctx, o, 16)) for o in range(1, 16)]
    copies = Copies(send, recv)
    load = copies.local(xg, xs)
    greet(column + across + [ahead, behind])

    parts = (dv, dk)
    chain = {}

    def chain_step(w, a, step):
        i = 2 * w + a
        if step > 1:
            chain[i].wait_recv()
        if step == 1:
            csend[i, 0, pl.ds(0, 128)] = parts[w][a, pl.ds(1024, 128)].astype(BF16)
            src, dst = csend.at[i, 0, pl.ds(0, 128)], crecv.at[i, 0, pl.ds(0, 128)]
        else:
            slot = 5 - step
            here = parts[w][a, pl.ds(slot * 256, 256)]
            if step == 2:
                csend[i, 1, pl.ds(0, 128)] = here[:128].astype(BF16)
                csend[i, 1, pl.ds(128, 128)] = (
                    here[128:] + crecv[i, 0, pl.ds(0, 128)].astype(F32)
                ).astype(BF16)
            else:
                csend[i, step - 1] = (here + crecv[i, step - 2].astype(F32)).astype(BF16)
            src, dst = csend.at[i, step - 1], crecv.at[i, step - 1]
        chain[i] = copies.remote(src, dst, down)

    def chain_end(w, a):
        i = 2 * w + a
        chain[i].wait_recv()
        return parts[w][a, pl.ds(0, 256)] + crecv[i, 3].astype(F32)

    for step in range(1, 5):
        for a in range(2):
            chain_step(0, a, step)
    for a in range(2):
        chain_step(1, a, 1)
    spread = {}
    for a in range(2):
        dvt[a, 0] = chain_end(0, a).T.astype(BF16)
        for dx in (2, 1, 3):
            spread[a, dx] = copies.remote(dvt.at[a, 0], dvt.at[a, dx], across[dx - 1])
    for a in range(2):
        chain_step(1, a, 2)
    load.wait()

    def product(a, c):
        cols = lanes(c * 256, 256)
        total = jnp.dot(dvt[a, 0], xs[0, :, cols], preferred_element_type=F32)
        for dx in range(1, NX):
            total += jnp.dot(dvt[a, dx], xs[dx, :, cols], preferred_element_type=F32)
        return total

    lengths = {(0, 0): 4, (0, 1): 3, (1, 0): 3, (1, 1): 4}
    ring = {}
    for a in range(2):
        for dx in range(1, NX):
            spread[a, dx].wait_recv()

        @pl.loop(0, NY)
        def _(c):
            part[a, c] = product(a, c)

        for way, target in ((0, ahead), (1, behind)):
            sign = 1 - 2 * way
            n = lengths[a, way]
            ysend[a, way, 0] = part[a, around(y, sign * n, NY)].astype(BF16)
            ring[a, way] = copies.remote(ysend.at[a, way, 0], yrecv.at[a, way, 0], target)
    for step in range(2, 5):
        for a in range(2):
            for way, target in ((0, ahead), (1, behind)):
                sign = 1 - 2 * way
                n = lengths[a, way]
                if step > n:
                    continue
                ring[a, way].wait_recv()
                ysend[a, way, step - 1] = (
                    part[a, around(y, sign * (n - step + 1), NY)]
                    + yrecv[a, way, step - 2].astype(F32)
                ).astype(BF16)
                ring[a, way] = copies.remote(
                    ysend.at[a, way, step - 1], yrecv.at[a, way, step - 1], target
                )
        if step < 4:
            for a in range(2):
                chain_step(1, a, step + 1)
    for a in range(2):
        for way in range(2):
            ring[a, way].wait_recv()
        total = (
            part[a, y]
            + yrecv[a, 0, lengths[a, 0] - 1].astype(F32)
            + yrecv[a, 1, lengths[a, 1] - 1].astype(F32)
        )
        zsend[:, a * HEAD : (a + 1) * HEAD] = total.T.astype(BF16)
    direct = []
    for o in range(1, 16):
        to = around(ctx, o, 16)
        direct.append(
            copies.remote(zsend.at[pl.ds(pl.multiple_of(to * 16, 16), 16)], zrecv.at[o], column[o - 1])
        )
    for a in range(2):
        kswap[0, :, a * HEAD : (a + 1) * HEAD] = (chain_end(1, a) * SCALE).astype(BF16)
    swap = copies.remote(
        kswap.at[0, rows_at((1 - h) * BLK, BLK)], kswap.at[1, pl.ds(0, BLK)], sib
    )
    key_grad[:, lanes(h * 256, 256)] = kswap[0, rows_at(h * BLK, BLK), :]
    sums = [zsend[pl.ds(pl.multiple_of(ctx * 16, 16), 16), :].astype(F32), None]
    for o in range(1, 16):
        direct[o - 1].wait_recv()
        got = zrecv[o].astype(F32)
        sums[o % 2] = got if sums[o % 2] is None else sums[o % 2] + got
    wv_grad[:, lanes(h * 256, 256)] = sums[0]
    wv_grad[:, lanes((1 - h) * 256, 256)] = sums[1]
    swap.wait_recv()
    key_grad[:, lanes((1 - h) * 256, 256)] = kswap[1, pl.ds(0, BLK), :]
    copies.wait_sends()


def on_device(queries, keys, values, out_grad, layer_input, doc_blocks):
    anywhere = pl.BlockSpec(memory_space=pl.ANY)
    in_vmem = pl.BlockSpec(memory_space=pltpu.VMEM)
    qg, kv, xg = pl.pallas_call(
        gather_kernel,
        out_shape=(
            jax.ShapeDtypeStruct((2, 256, 2048), BF16),
            jax.ShapeDtypeStruct((2, 2, ROWS, HEAD), BF16),
            jax.ShapeDtypeStruct((NX, 256, 2048), BF16),
        ),
        in_specs=[anywhere] * 5,
        out_specs=(anywhere,) * 3,
        scratch_shapes=[pltpu.SemaphoreType.DMA((64,)), pltpu.SemaphoreType.DMA((64,))],
        compiler_params=pltpu.CompilerParams(collective_id=0, has_side_effects=True),
        name="gather",
    )(queries[0], out_grad[0], keys[0], values[0], layer_input[0])
    dk, dv = pl.pallas_call(
        attend_kernel,
        grid=(2,),
        out_shape=(jax.ShapeDtypeStruct((2, ROWS, HEAD), F32),) * 2,
        in_specs=[
            pl.BlockSpec(memory_space=pltpu.SMEM),
            pl.BlockSpec((1, 256, 1024), lambda a: (0, 0, a)),
            pl.BlockSpec((1, 256, 1024), lambda a: (1, 0, a)),
            pl.BlockSpec((1, 2, ROWS, HEAD), lambda a: (a, 0, 0, 0)),
        ],
        out_specs=(pl.BlockSpec((1, ROWS, HEAD), lambda a: (a, 0, 0)),) * 2,
        scratch_shapes=[pltpu.VMEM((ROWS, 256), F32)],
        compiler_params=pltpu.CompilerParams(vmem_limit_bytes=40 << 20),
        name="attend",
    )(doc_blocks, qg, qg, kv)
    key_grad, wv_grad = pl.pallas_call(
        reduce_kernel,
        out_shape=(
            jax.ShapeDtypeStruct((BLK, 512), BF16),
            jax.ShapeDtypeStruct((16, 512), F32),
        ),
        in_specs=[in_vmem, in_vmem, anywhere],
        out_specs=(in_vmem, in_vmem),
        scratch_shapes=[
            pltpu.VMEM((NX, 256, 2048), BF16),
            pltpu.VMEM((4, HOPS, 256, HEAD), BF16),
            pltpu.VMEM((4, HOPS, 256, HEAD), BF16),
            pltpu.VMEM((2, NX, HEAD, 256), BF16),
            pltpu.VMEM((2, NY, HEAD, 256), F32),
            pltpu.VMEM((2, 2, 4, HEAD, 256), BF16),
            pltpu.VMEM((2, 2, 4, HEAD, 256), BF16),
            pltpu.VMEM((256, 256), BF16),
            pltpu.VMEM((16, 16, 256), BF16),
            pltpu.VMEM((2, 256, 256), BF16),
            pltpu.SemaphoreType.DMA((64,)),
            pltpu.SemaphoreType.DMA((64,)),
        ],
        compiler_params=pltpu.CompilerParams(
            collective_id=1, has_side_effects=True, vmem_limit_bytes=40 << 20
        ),
        name="reduce",
    )(dk, dv, xg)
    return (key_grad[None], wv_grad)


def solution(mesh):
    in_specs = (
        P("dp", "context", None),
        P("dp", "context", None),
        P("dp", "context", None),
        P("dp", "context", None),
        P("dp", "context", None),
        P("dp", None),
    )
    out_specs = (P("dp", "context", None), P(("dp", "context"), None))
    return jax.shard_map(
        on_device, mesh=mesh, in_specs=in_specs, out_specs=out_specs, check_vma=False
    )
```

```python
import math

import jax
import jax.numpy as jnp
from jax import lax
from jax.experimental import pallas as pl
from jax.experimental.pallas import tpu as pltpu
from jax.sharding import PartitionSpec as P

HEAD = 128
BLK = 128
NX, NY, NZ = 4, 8, 8
HOPS = 4
ROWS = 1152
MASKED = -1e30
SCALE = 1.0 / math.sqrt(HEAD)
MESH = pl.DeviceIdType.MESH
F32 = jnp.float32
BF16 = jnp.bfloat16


def place():
    d = lax.axis_index("dp")
    c = lax.axis_index("context")
    return lax.rem(d, NX), lax.div(d, NX), lax.div(c, 2), lax.rem(c, 2)


def device(x, y, z, h):
    return (y * NX + x, z * 2 + h)


def around(i, by, n):
    return lax.rem(i + (by + n), n)


class Copies:
    def __init__(self, send, recv):
        self.send, self.recv, self.used, self.all = send, recv, 0, []

    def claim(self):
        self.used += 1
        return self.used - 1

    def make(self, i, src, dst, target):
        return pltpu.make_async_remote_copy(
            src_ref=src,
            dst_ref=dst,
            send_sem=self.send.at[i],
            recv_sem=self.recv.at[i],
            device_id=target,
            device_id_type=MESH,
        )

    def remote(self, src, dst, target):
        copy = self.make(self.claim(), src, dst, target)
        copy.start()
        self.all.append(copy)
        return copy

    def remote_pieces(self, pieces, whole, target):
        i = self.claim()
        for src, dst in pieces:
            self.make(i, src, dst, target).start()
        copy = self.make(i, whole, whole, target)
        self.all.append(copy)
        return copy

    def local(self, src, dst):
        copy = pltpu.make_async_copy(src, dst, self.send.at[self.claim()])
        copy.start()
        return copy

    def wait_sends(self):
        for copy in self.all:
            copy.wait_send()


def greet(targets):
    barrier = pltpu.get_barrier_semaphore()
    for target in targets:
        pl.semaphore_signal(barrier, inc=1, device_id=target, device_id_type=MESH)
    pl.semaphore_wait(barrier, len(targets))


def lanes(start, size):
    return pl.ds(pl.multiple_of(start, 128), size)


def rows_at(start, size):
    return pl.ds(pl.multiple_of(start, 128), size)


def rows16(block):
    return pl.ds(pl.multiple_of(block * 16, 16), 16)


def fill_bias(docs, bias, z):
    ends = []
    total = docs[0, 0]
    for i in range(5):
        ends.append(total)
        if i < 4:
            total = total + docs[0, i + 1]

    def doc(b):
        return sum((b >= e).astype(jnp.int32) for e in ends)

    key = lax.broadcasted_iota(jnp.int32, (BLK, BLK), 0)
    query = lax.broadcasted_iota(jnp.int32, (BLK, BLK), 1)
    for j in range(2):
        qb = 2 * z + j
        for i in range(9):
            kb = 2 * z - 2 * (i // 2) + (1 if i == 8 else i % 2)
            if i < 2 and i == j:
                block = jnp.where(key <= query, 0.0, MASKED)
            elif i == 1 and j == 0:
                block = jnp.full((BLK, BLK), MASKED, F32)
            else:
                same = (kb >= 0) & (doc(kb) == doc(qb))
                block = jnp.full((BLK, BLK), jnp.where(same, 0.0, MASKED), F32)
            bias[pl.ds(i * BLK, BLK), pl.ds(j * BLK, BLK)] = block


def kernel(
    docs, q, g, k, v, xin, key_grad, wv_grad,
    qg, kv, xs, bias, prob, dv, dk, csend, crecv, dvt, part, ysend, yrecv, zsend, zrecv, kswap,
    send, recv,
):
    x, y, z, h = place()
    ctx = z * 2 + h
    sib = device(x, y, z, 1 - h)
    up = device(x, y, around(z, 1, NZ), h)
    down = device(x, y, around(z, -1, NZ), h)
    across = [device(around(x, dx, NX), y, z, h) for dx in range(1, NX)]
    ahead = device(x, around(y, 1, NY), z, h)
    behind = device(x, around(y, -1, NY), z, h)
    column = [(y * NX + x, around(ctx, o, 16)) for o in range(1, 16)]
    mine = rows_at(h * BLK, BLK)
    copies = Copies(send, recv)

    own_k, own_v = [
        [
            copies.local(src.at[:, lanes((2 * h + a) * HEAD, HEAD)], kv.at[a, j, mine])
            for a in range(2)
        ]
        for j, src in enumerate((k, v))
    ]
    own_q = [
        copies.local(src.at[:, lanes(h * 2048, 2048)], qg.at[j, mine])
        for j, src in enumerate((q, g))
    ]
    greet(column + across + [ahead, behind])

    def swap_kv(j, src):
        return [
            copies.remote(
                src.at[:, lanes((2 * (1 - h) + a) * HEAD, HEAD)], kv.at[a, j, mine], sib
            )
            for a in range(2)
        ]

    hops = {}
    swapped = {0: swap_kv(0, k)}

    def hop(j, a, step):
        if step == 1:
            swapped[j][a].wait_recv()
            (own_k, own_v)[j][a].wait()
        else:
            hops[j, a].wait_recv()
        lo, size = (768 + 128, 128) if step == 4 else ((step - 1) * 256, 256)
        hops[j, a] = copies.remote(
            kv.at[a, j, pl.ds(lo, size)], kv.at[a, j, pl.ds(step * 256, size)], up
        )

    for a in range(2):
        hop(0, a, 1)
    exchange = [
        copies.remote(src.at[:, lanes((1 - h) * 2048, 2048)], qg.at[j, mine], sib)
        for j, src in enumerate((q, g))
    ]
    swapped[1] = swap_kv(1, v)
    spread_x = {}
    for dx in (1, 3, 2):
        to = around(x, dx, NX)
        spread_x[dx] = copies.remote_pieces(
            [
                (
                    xin.at[:, lanes(c * 1024 + to * 256, 256)],
                    xs.at[dx, mine, pl.ds(c * 256, 256)],
                )
                for c in range(NY)
            ],
            xs.at[dx, mine],
            across[dx - 1],
        )
    own_x = [
        copies.local(
            xin.at[:, lanes(c * 1024 + x * 256, 256)], xs.at[0, mine, pl.ds(c * 256, 256)]
        )
        for c in range(NY)
    ]
    passed = {}

    def pass_x(dx):
        if dx == 0:
            for copy in own_x:
                copy.wait()
        else:
            spread_x[dx].wait_recv()
        passed[dx] = copies.remote(xs.at[dx, mine], xs.at[dx, mine], sib)

    fill_bias(docs, bias, z)
    dv[...] = jnp.zeros_like(dv)
    dk[...] = jnp.zeros_like(dk)
    for a in range(2):
        hop(0, a, 2)
    for a in range(2):
        hop(1, a, 1)
    for step in (3, 4):
        for a in range(2):
            hop(0, a, step)

    contract = (((1,), (1,)), ((), ()))

    def weigh(a, head):
        col = lanes((a * 8 + head) * HEAD, HEAD)
        s = lax.dot_general(kv[a, 0], qg[0, :, col], contract, preferred_element_type=F32)
        t = s * (SCALE * math.log2(math.e)) + bias[...]
        e = jnp.exp2(t - jnp.max(t, axis=0, keepdims=True))
        p = e * (1.0 / jnp.sum(e, axis=0, keepdims=True))
        prob[a * 8 + head] = p
        dv[a] += jnp.dot(p.astype(BF16), qg[1, :, col], preferred_element_type=F32)

    def push_back(a, head):
        col = lanes((a * 8 + head) * HEAD, HEAD)
        dp = lax.dot_general(kv[a, 1], qg[1, :, col], contract, preferred_element_type=F32)
        p = prob[a * 8 + head]
        delta = jnp.sum(p * dp, axis=0, keepdims=True)
        ds = (p * (dp - delta)).astype(BF16)
        dk[a] += jnp.dot(ds, qg[0, :, col], preferred_element_type=F32)

    def heads(one, a, lo, hi):
        @pl.loop(lo // 2, hi // 2)
        def _(i):
            one(a, 2 * i)
            one(a, 2 * i + 1)

    parts = (dv, dk)
    chain = {}

    def chain_step(w, a, step):
        i = 2 * w + a
        if step > 1:
            chain[i].wait_recv()
        if step == 1:
            csend[i, 0, pl.ds(0, 128)] = parts[w][a, pl.ds(1024, 128)].astype(BF16)
            src, dst = csend.at[i, 0, pl.ds(0, 128)], crecv.at[i, 0, pl.ds(0, 128)]
        else:
            here = parts[w][a, pl.ds((5 - step) * 256, 256)]
            if step == 2:
                csend[i, 1, pl.ds(0, 128)] = here[:128].astype(BF16)
                csend[i, 1, pl.ds(128, 128)] = (
                    here[128:] + crecv[i, 0, pl.ds(0, 128)].astype(F32)
                ).astype(BF16)
            else:
                csend[i, step - 1] = (here + crecv[i, step - 2].astype(F32)).astype(BF16)
            src, dst = csend.at[i, step - 1], crecv.at[i, step - 1]
        chain[i] = copies.remote(src, dst, down)

    def chain_end(w, a):
        i = 2 * w + a
        chain[i].wait_recv()
        return parts[w][a, pl.ds(0, 256)] + crecv[i, 3].astype(F32)

    spread = {}

    def spread_dv(a):
        dvt[a, 0] = chain_end(0, a).T.astype(BF16)
        for dx in (2, 1, 3):
            spread[a, dx] = copies.remote(dvt.at[a, 0], dvt.at[a, dx], across[dx - 1])

    def wait_x():
        for dx in range(NX):
            passed[dx].wait_recv()

    def product(a):
        for dx in range(1, NX):
            spread[a, dx].wait_recv()

        @pl.loop(0, NY)
        def _(c):
            cols = lanes(c * 256, 256)
            total = jnp.dot(dvt[a, 0], xs[0, :, cols], preferred_element_type=F32)
            for dx in range(1, NX):
                total += jnp.dot(dvt[a, dx], xs[dx, :, cols], preferred_element_type=F32)
            part[a, c] = total

    lengths = {(0, 0): 4, (0, 1): 3, (1, 0): 3, (1, 1): 4}
    ring = {}

    def ring_step(a, step):
        for way, target in ((0, ahead), (1, behind)):
            sign = 1 - 2 * way
            n = lengths[a, way]
            if step > n:
                continue
            here = part[a, around(y, sign * (n - step + 1), NY)]
            if step > 1:
                ring[a, way].wait_recv()
                here = here + yrecv[a, way, step - 2].astype(F32)
            ysend[a, way, step - 1] = here.astype(BF16)
            ring[a, way] = copies.remote(
                ysend.at[a, way, step - 1], yrecv.at[a, way, step - 1], target
            )

    def ring_end(a):
        for way in range(2):
            ring[a, way].wait_recv()
        total = (
            part[a, y]
            + yrecv[a, 0, lengths[a, 0] - 1].astype(F32)
            + yrecv[a, 1, lengths[a, 1] - 1].astype(F32)
        )
        zsend[:, a * HEAD : (a + 1) * HEAD] = total.T.astype(BF16)

    for copy in own_q:
        copy.wait()
    for copy in exchange:
        copy.wait_recv()
    for a in range(2):
        hops[0, a].wait_recv()
        heads(weigh, a, 0, 4)
        if a == 0:
            hop(1, 0, 2)
            hop(1, 1, 2)
        else:
            hop(1, 0, 4)
            hop(1, 1, 4)
            chain_step(0, 0, 2)
        heads(weigh, a, 4, 8)
        if a == 0:
            hop(1, 0, 3)
            hop(1, 1, 3)
            chain_step(0, 0, 1)
    chain_step(0, 1, 1)
    chain_step(0, 0, 3)

    for a in range(2):
        hops[1, a].wait_recv()
    heads(push_back, 0, 0, 2)
    chain_step(0, 0, 4)
    heads(push_back, 0, 2, 4)
    chain_step(0, 1, 2)
    heads(push_back, 0, 4, 6)
    spread_dv(0)
    heads(push_back, 0, 6, 8)
    chain_step(0, 1, 3)
    chain_step(1, 0, 1)
    heads(push_back, 1, 0, 4)
    chain_step(0, 1, 4)
    chain_step(1, 0, 2)
    pass_x(0)
    pass_x(1)
    pass_x(3)
    heads(push_back, 1, 4, 8)
    spread_dv(1)
    pass_x(2)
    chain_step(1, 1, 1)
    chain_step(1, 0, 3)
    wait_x()
    product(0)
    ring_step(0, 1)
    chain_step(1, 1, 2)
    product(1)
    ring_step(1, 1)
    chain_step(1, 0, 4)
    ring_step(0, 2)
    ring_step(1, 2)
    chain_step(1, 1, 3)
    ring_step(0, 3)
    ring_step(1, 3)
    chain_step(1, 1, 4)
    ring_step(0, 4)
    ring_step(1, 4)
    kswap[0, :, 0:HEAD] = (chain_end(1, 0) * SCALE).astype(BF16)
    ring_end(0)
    ring_end(1)
    direct = [
        copies.remote(zsend.at[rows16(around(ctx, o, 16))], zrecv.at[o], column[o - 1])
        for o in range(1, 16)
    ]
    kswap[0, :, HEAD : 2 * HEAD] = (chain_end(1, 1) * SCALE).astype(BF16)
    swap = copies.remote(
        kswap.at[0, rows_at((1 - h) * BLK, BLK)], kswap.at[1, pl.ds(0, BLK)], sib
    )
    key_grad[:, lanes(h * 256, 256)] = kswap[0, rows_at(h * BLK, BLK), :]
    sums = [zsend[rows16(ctx), :].astype(F32), None]
    for o in range(1, 16):
        direct[o - 1].wait_recv()
        got = zrecv[o].astype(F32)
        sums[o % 2] = got if sums[o % 2] is None else sums[o % 2] + got
    wv_grad[:, lanes(h * 256, 256)] = sums[0]
    wv_grad[:, lanes((1 - h) * 256, 256)] = sums[1]
    swap.wait_recv()
    key_grad[:, lanes((1 - h) * 256, 256)] = kswap[1, pl.ds(0, BLK), :]
    copies.wait_sends()


def on_device(queries, keys, values, out_grad, layer_input, doc_blocks):
    anywhere = pl.BlockSpec(memory_space=pl.ANY)
    in_vmem = pl.BlockSpec(memory_space=pltpu.VMEM)
    key_grad, wv_grad = pl.pallas_call(
        kernel,
        out_shape=(
            jax.ShapeDtypeStruct((BLK, 512), BF16),
            jax.ShapeDtypeStruct((16, 512), F32),
        ),
        in_specs=[pl.BlockSpec(memory_space=pltpu.SMEM)] + [anywhere] * 5,
        out_specs=(in_vmem, in_vmem),
        scratch_shapes=[
            pltpu.VMEM((2, 256, 2048), BF16),
            pltpu.VMEM((2, 2, ROWS, HEAD), BF16),
            pltpu.VMEM((NX, 256, 2048), BF16),
            pltpu.VMEM((ROWS, 256), F32),
            pltpu.VMEM((16, ROWS, 256), F32),
            pltpu.VMEM((2, ROWS, HEAD), F32),
            pltpu.VMEM((2, ROWS, HEAD), F32),
            pltpu.VMEM((4, HOPS, 256, HEAD), BF16),
            pltpu.VMEM((4, HOPS, 256, HEAD), BF16),
            pltpu.VMEM((2, NX, HEAD, 256), BF16),
            pltpu.VMEM((2, NY, HEAD, 256), F32),
            pltpu.VMEM((2, 2, 4, HEAD, 256), BF16),
            pltpu.VMEM((2, 2, 4, HEAD, 256), BF16),
            pltpu.VMEM((256, 256), BF16),
            pltpu.VMEM((16, 16, 256), BF16),
            pltpu.VMEM((2, 256, 256), BF16),
            pltpu.SemaphoreType.DMA((112,)),
            pltpu.SemaphoreType.DMA((112,)),
        ],
        compiler_params=pltpu.CompilerParams(
            collective_id=0, has_side_effects=True, vmem_limit_bytes=56 << 20
        ),
        name="grads",
    )(doc_blocks, queries[0], out_grad[0], keys[0], values[0], layer_input[0])
    return (key_grad[None], wv_grad)


def solution(mesh):
    in_specs = (
        P("dp", "context", None),
        P("dp", "context", None),
        P("dp", "context", None),
        P("dp", "context", None),
        P("dp", "context", None),
        P("dp", None),
    )
    out_specs = (P("dp", "context", None), P(("dp", "context"), None))
    return jax.shard_map(
        on_device, mesh=mesh, in_specs=in_specs, out_specs=out_specs, check_vma=False
    )
```

```python
import math

import jax
import jax.numpy as jnp
from jax import lax
from jax.experimental import pallas as pl
from jax.experimental.pallas import tpu as pltpu
from jax.sharding import PartitionSpec as P

HEAD = 128
BLK = 128
NX, NY, NZ = 4, 8, 8
HOPS = 4
ROWS = 1152
MASKED = -1e30
SCALE = 1.0 / math.sqrt(HEAD)
MESH = pl.DeviceIdType.MESH
F32 = jnp.float32
BF16 = jnp.bfloat16


def place():
    d = lax.axis_index("dp")
    c = lax.axis_index("context")
    return lax.rem(d, NX), lax.div(d, NX), lax.div(c, 2), lax.rem(c, 2)


def device(x, y, z, h):
    return (y * NX + x, z * 2 + h)


def around(i, by, n):
    return lax.rem(i + (by + n), n)


class Copies:
    def __init__(self, send, recv):
        self.send, self.recv, self.used, self.all = send, recv, 0, []

    def claim(self):
        self.used += 1
        return self.used - 1

    def make(self, i, src, dst, target):
        return pltpu.make_async_remote_copy(
            src_ref=src,
            dst_ref=dst,
            send_sem=self.send.at[i],
            recv_sem=self.recv.at[i],
            device_id=target,
            device_id_type=MESH,
        )

    def remote(self, src, dst, target):
        copy = self.make(self.claim(), src, dst, target)
        copy.start()
        self.all.append(copy)
        return copy

    def local(self, src, dst):
        copy = pltpu.make_async_copy(src, dst, self.send.at[self.claim()])
        copy.start()
        return copy

    def wait_sends(self):
        for copy in self.all:
            copy.wait_send()


def greet(targets):
    barrier = pltpu.get_barrier_semaphore()
    for target in targets:
        pl.semaphore_signal(barrier, inc=1, device_id=target, device_id_type=MESH)
    pl.semaphore_wait(barrier, len(targets))


def lanes(start, size):
    return pl.ds(pl.multiple_of(start, 128), size)


def rows_at(start, size):
    return pl.ds(pl.multiple_of(start, 128), size)


def rows16(block):
    return pl.ds(pl.multiple_of(block * 16, 16), 16)


def fill_bias(docs, bias, z):
    ends = []
    total = docs[0, 0]
    for i in range(5):
        ends.append(total)
        if i < 4:
            total = total + docs[0, i + 1]

    def doc(b):
        return sum((b >= e).astype(jnp.int32) for e in ends)

    key = lax.broadcasted_iota(jnp.int32, (BLK, BLK), 0)
    query = lax.broadcasted_iota(jnp.int32, (BLK, BLK), 1)
    for j in range(2):
        qb = 2 * z + j
        for i in range(9):
            kb = 2 * z - 2 * (i // 2) + (1 if i == 8 else i % 2)
            if i < 2 and i == j:
                block = jnp.where(key <= query, 0.0, MASKED)
            elif i == 1 and j == 0:
                block = jnp.full((BLK, BLK), MASKED, F32)
            else:
                same = (kb >= 0) & (doc(kb) == doc(qb))
                block = jnp.full((BLK, BLK), jnp.where(same, 0.0, MASKED), F32)
            bias[pl.ds(i * BLK, BLK), pl.ds(j * BLK, BLK)] = block


def kernel(
    docs, q, g, k, v, xin, key_grad, wv_grad,
    qg, kv, xs, relay, bias, prob, dv, dk, csend, crecv, dvt, part, ysend, yrecv, zsend, zrecv, kswap,
    send, recv,
):
    x, y, z, h = place()
    ctx = z * 2 + h
    sib = device(x, y, z, 1 - h)
    up = device(x, y, around(z, 1, NZ), h)
    down = device(x, y, around(z, -1, NZ), h)
    across = [device(around(x, dx, NX), y, z, h) for dx in range(1, NX)]
    ahead = device(x, around(y, 1, NY), z, h)
    behind = device(x, around(y, -1, NY), z, h)
    column = [(y * NX + x, around(ctx, o, 16)) for o in range(1, 16)]
    mine = rows_at(h * BLK, BLK)
    copies = Copies(send, recv)

    own_k, own_v = [
        [
            copies.local(src.at[:, lanes((2 * h + a) * HEAD, HEAD)], kv.at[a, j, mine])
            for a in range(2)
        ]
        for j, src in enumerate((k, v))
    ]
    own_q = [
        copies.local(src.at[:, lanes(h * 2048, 2048)], qg.at[j, mine])
        for j, src in enumerate((q, g))
    ]
    greet(column + across + [ahead, behind])

    def swap_kv(j, src):
        return [
            copies.remote(
                src.at[:, lanes((2 * (1 - h) + a) * HEAD, HEAD)], kv.at[a, j, mine], sib
            )
            for a in range(2)
        ]

    hops = {}
    swapped = {0: swap_kv(0, k)}

    def hop(j, a, step):
        if step == 1:
            swapped[j][a].wait_recv()
            (own_k, own_v)[j][a].wait()
        else:
            hops[j, a].wait_recv()
        lo, size = (768 + 128, 128) if step == 4 else ((step - 1) * 256, 256)
        hops[j, a] = copies.remote(
            kv.at[a, j, pl.ds(lo, size)], kv.at[a, j, pl.ds(step * 256, size)], up
        )

    for a in range(2):
        hop(0, a, 1)
    exchange = [
        copies.remote(src.at[:, lanes((1 - h) * 2048, 2048)], qg.at[j, mine], sib)
        for j, src in enumerate((q, g))
    ]
    swapped[1] = swap_kv(1, v)
    right, left = across[0], across[2]
    spread_x, relays, pieces = {}, {}, []

    def piece(i, dx, c, dst, target):
        to = around(x, dx, NX)
        src = xin.at[:, lanes(c * 1024 + to * 256, 256)]
        pieces.append(lambda: copies.make(i, src, dst, target).start())

    ways = ((0, right), (1, left))
    claimed = [copies.claim() for _ in range(4)]
    for c in range(4):
        for way, target in ways:
            dst = relay.at[way, :, pl.ds(c * 256, 256)]
            piece(claimed[way], 2, way * 4 + c, dst, target)
    for c in range(NY):
        for way, target in ways:
            dx = 1 + 2 * way
            piece(claimed[2 + way], dx, c, xs.at[dx, mine, pl.ds(c * 256, 256)], target)
    for way, target in ways:
        dx = 1 + 2 * way
        relays[way] = copies.make(claimed[way], relay.at[way], relay.at[way], target)
        spread_x[dx] = copies.make(claimed[2 + way], xs.at[dx, mine], xs.at[dx, mine], target)
        copies.all += [relays[way], spread_x[dx]]
    second = []

    def feed(n):
        for _ in range(n):
            pieces.pop(0)()

    def relay_on():
        for way, target in ways:
            relays[way].wait_recv()
            second.append(
                copies.remote(
                    relay.at[way], xs.at[2, mine, pl.ds(way * 1024, 1024)], target
                )
            )

    own_x = [
        copies.local(
            xin.at[:, lanes(c * 1024 + x * 256, 256)], xs.at[0, mine, pl.ds(c * 256, 256)]
        )
        for c in range(NY)
    ]
    passed = {}

    def pass_x(dx):
        if dx == 0:
            for copy in own_x:
                copy.wait()
        elif dx == 2:
            for copy in second:
                copy.wait_recv()
        else:
            spread_x[dx].wait_recv()
        passed[dx] = copies.remote(xs.at[dx, mine], xs.at[dx, mine], sib)

    feed(4)
    fill_bias(docs, bias, z)
    dv[...] = jnp.zeros_like(dv)
    dk[...] = jnp.zeros_like(dk)
    for a in range(2):
        hop(0, a, 2)
    feed(4)
    for a in range(2):
        hop(1, a, 1)
    for a in range(2):
        hop(0, a, 3)
    feed(4)
    for a in range(2):
        hop(0, a, 4)
    feed(4)

    contract = (((1,), (1,)), ((), ()))

    def weigh(a, head):
        col = lanes((a * 8 + head) * HEAD, HEAD)
        s = lax.dot_general(kv[a, 0], qg[0, :, col], contract, preferred_element_type=F32)
        t = s * (SCALE * math.log2(math.e)) + bias[...]
        e = jnp.exp2(t - jnp.max(t, axis=0, keepdims=True))
        p = e * (1.0 / jnp.sum(e, axis=0, keepdims=True))
        prob[a * 8 + head] = p
        dv[a] += jnp.dot(p.astype(BF16), qg[1, :, col], preferred_element_type=F32)

    def push_back(a, head):
        col = lanes((a * 8 + head) * HEAD, HEAD)
        dp = lax.dot_general(kv[a, 1], qg[1, :, col], contract, preferred_element_type=F32)
        p = prob[a * 8 + head]
        delta = jnp.sum(p * dp, axis=0, keepdims=True)
        ds = (p * (dp - delta)).astype(BF16)
        dk[a] += jnp.dot(ds, qg[0, :, col], preferred_element_type=F32)

    def heads(one, a, lo, hi):
        @pl.loop(lo // 2, hi // 2)
        def _(i):
            one(a, 2 * i)
            one(a, 2 * i + 1)

    parts = (dv, dk)
    chain = {}

    def chain_step(w, a, step):
        i = 2 * w + a
        if step > 1:
            chain[i].wait_recv()
        if step == 1:
            csend[i, 0, pl.ds(0, 128)] = parts[w][a, pl.ds(1024, 128)].astype(BF16)
            src, dst = csend.at[i, 0, pl.ds(0, 128)], crecv.at[i, 0, pl.ds(0, 128)]
        else:
            here = parts[w][a, pl.ds((5 - step) * 256, 256)]
            if step == 2:
                csend[i, 1, pl.ds(0, 128)] = here[:128].astype(BF16)
                csend[i, 1, pl.ds(128, 128)] = (
                    here[128:] + crecv[i, 0, pl.ds(0, 128)].astype(F32)
                ).astype(BF16)
            else:
                csend[i, step - 1] = (here + crecv[i, step - 2].astype(F32)).astype(BF16)
            src, dst = csend.at[i, step - 1], crecv.at[i, step - 1]
        chain[i] = copies.remote(src, dst, down)

    def chain_end(w, a):
        i = 2 * w + a
        chain[i].wait_recv()
        return parts[w][a, pl.ds(0, 256)] + crecv[i, 3].astype(F32)

    spread = {}

    def spread_dv(a):
        dvt[a, 0] = chain_end(0, a).T.astype(BF16)
        for dx in (2, 1, 3):
            spread[a, dx] = copies.remote(dvt.at[a, 0], dvt.at[a, dx], across[dx - 1])

    def wait_x():
        for dx in range(NX):
            passed[dx].wait_recv()

    def product(a):
        for dx in range(1, NX):
            spread[a, dx].wait_recv()

        @pl.loop(0, NY)
        def _(c):
            cols = lanes(c * 256, 256)
            total = jnp.dot(dvt[a, 0], xs[0, :, cols], preferred_element_type=F32)
            for dx in range(1, NX):
                total += jnp.dot(dvt[a, dx], xs[dx, :, cols], preferred_element_type=F32)
            part[a, c] = total

    lengths = {(0, 0): 4, (0, 1): 3, (1, 0): 3, (1, 1): 4}
    ring = {}

    def ring_step(a, step):
        for way, target in ((0, ahead), (1, behind)):
            sign = 1 - 2 * way
            n = lengths[a, way]
            if step > n:
                continue
            here = part[a, around(y, sign * (n - step + 1), NY)]
            if step > 1:
                ring[a, way].wait_recv()
                here = here + yrecv[a, way, step - 2].astype(F32)
            ysend[a, way, step - 1] = here.astype(BF16)
            ring[a, way] = copies.remote(
                ysend.at[a, way, step - 1], yrecv.at[a, way, step - 1], target
            )

    def ring_end(a):
        for way in range(2):
            ring[a, way].wait_recv()
        total = (
            part[a, y]
            + yrecv[a, 0, lengths[a, 0] - 1].astype(F32)
            + yrecv[a, 1, lengths[a, 1] - 1].astype(F32)
        )
        zsend[:, a * HEAD : (a + 1) * HEAD] = total.T.astype(BF16)

    for copy in own_q:
        copy.wait()
    for copy in exchange:
        copy.wait_recv()
    hops[0, 0].wait_recv()
    heads(weigh, 0, 0, 2)
    relay_on()
    feed(2)
    heads(weigh, 0, 2, 4)
    hop(1, 0, 2)
    hop(1, 1, 2)
    feed(2)
    heads(weigh, 0, 4, 6)
    feed(2)
    heads(weigh, 0, 6, 8)
    chain_step(0, 0, 1)
    hop(1, 0, 3)
    hop(1, 1, 3)
    feed(2)
    hops[0, 1].wait_recv()
    heads(weigh, 1, 0, 4)
    hop(1, 0, 4)
    hop(1, 1, 4)
    chain_step(0, 0, 2)
    heads(weigh, 1, 4, 8)
    chain_step(0, 1, 1)
    chain_step(0, 0, 3)

    for a in range(2):
        hops[1, a].wait_recv()
    heads(push_back, 0, 0, 2)
    chain_step(0, 0, 4)
    heads(push_back, 0, 2, 4)
    chain_step(0, 1, 2)
    heads(push_back, 0, 4, 6)
    spread_dv(0)
    heads(push_back, 0, 6, 8)
    chain_step(0, 1, 3)
    chain_step(1, 0, 1)
    heads(push_back, 1, 0, 4)
    chain_step(0, 1, 4)
    chain_step(1, 0, 2)
    pass_x(0)
    pass_x(1)
    pass_x(3)
    heads(push_back, 1, 4, 8)
    spread_dv(1)
    pass_x(2)
    chain_step(1, 1, 1)
    chain_step(1, 0, 3)
    wait_x()
    product(0)
    ring_step(0, 1)
    chain_step(1, 1, 2)
    product(1)
    ring_step(1, 1)
    chain_step(1, 0, 4)
    ring_step(0, 2)
    ring_step(1, 2)
    chain_step(1, 1, 3)
    ring_step(0, 3)
    ring_step(1, 3)
    chain_step(1, 1, 4)
    ring_step(0, 4)
    ring_step(1, 4)
    kswap[0, :, 0:HEAD] = (chain_end(1, 0) * SCALE).astype(BF16)
    ring_end(0)
    ring_end(1)
    direct = [
        copies.remote(zsend.at[rows16(around(ctx, o, 16))], zrecv.at[o], column[o - 1])
        for o in range(1, 16)
    ]
    kswap[0, :, HEAD : 2 * HEAD] = (chain_end(1, 1) * SCALE).astype(BF16)
    swap = copies.remote(
        kswap.at[0, rows_at((1 - h) * BLK, BLK)], kswap.at[1, pl.ds(0, BLK)], sib
    )
    key_grad[:, lanes(h * 256, 256)] = kswap[0, rows_at(h * BLK, BLK), :]
    sums = [zsend[rows16(ctx), :].astype(F32), None]
    for o in range(1, 16):
        direct[o - 1].wait_recv()
        got = zrecv[o].astype(F32)
        sums[o % 2] = got if sums[o % 2] is None else sums[o % 2] + got
    wv_grad[:, lanes(h * 256, 256)] = sums[0]
    wv_grad[:, lanes((1 - h) * 256, 256)] = sums[1]
    swap.wait_recv()
    key_grad[:, lanes((1 - h) * 256, 256)] = kswap[1, pl.ds(0, BLK), :]
    copies.wait_sends()


def on_device(queries, keys, values, out_grad, layer_input, doc_blocks):
    anywhere = pl.BlockSpec(memory_space=pl.ANY)
    in_vmem = pl.BlockSpec(memory_space=pltpu.VMEM)
    key_grad, wv_grad = pl.pallas_call(
        kernel,
        out_shape=(
            jax.ShapeDtypeStruct((BLK, 512), BF16),
            jax.ShapeDtypeStruct((16, 512), F32),
        ),
        in_specs=[pl.BlockSpec(memory_space=pltpu.SMEM)] + [anywhere] * 5,
        out_specs=(in_vmem, in_vmem),
        scratch_shapes=[
            pltpu.VMEM((2, 256, 2048), BF16),
            pltpu.VMEM((2, 2, ROWS, HEAD), BF16),
            pltpu.VMEM((NX, 256, 2048), BF16),
            pltpu.VMEM((2, BLK, 1024), BF16),
            pltpu.VMEM((ROWS, 256), F32),
            pltpu.VMEM((16, ROWS, 256), F32),
            pltpu.VMEM((2, ROWS, HEAD), F32),
            pltpu.VMEM((2, ROWS, HEAD), F32),
            pltpu.VMEM((4, HOPS, 256, HEAD), BF16),
            pltpu.VMEM((4, HOPS, 256, HEAD), BF16),
            pltpu.VMEM((2, NX, HEAD, 256), BF16),
            pltpu.VMEM((2, NY, HEAD, 256), F32),
            pltpu.VMEM((2, 2, 4, HEAD, 256), BF16),
            pltpu.VMEM((2, 2, 4, HEAD, 256), BF16),
            pltpu.VMEM((256, 256), BF16),
            pltpu.VMEM((16, 16, 256), BF16),
            pltpu.VMEM((2, 256, 256), BF16),
            pltpu.SemaphoreType.DMA((112,)),
            pltpu.SemaphoreType.DMA((112,)),
        ],
        compiler_params=pltpu.CompilerParams(
            collective_id=0, has_side_effects=True, vmem_limit_bytes=56 << 20
        ),
        name="grads",
    )(doc_blocks, queries[0], out_grad[0], keys[0], values[0], layer_input[0])
    return (key_grad[None], wv_grad)


def solution(mesh):
    in_specs = (
        P("dp", "context", None),
        P("dp", "context", None),
        P("dp", "context", None),
        P("dp", "context", None),
        P("dp", "context", None),
        P("dp", None),
    )
    out_specs = (P("dp", "context", None), P(("dp", "context"), None))
    return jax.shard_map(
        on_device, mesh=mesh, in_specs=in_specs, out_specs=out_specs, check_vma=False
    )
```

```python
import math

import jax
import jax.numpy as jnp
from jax import lax
from jax.experimental import pallas as pl
from jax.experimental.pallas import tpu as pltpu
from jax.sharding import PartitionSpec as P

HEAD = 128
BLK = 128
NX, NY, NZ = 4, 8, 8
HOPS = 4
ROWS = 1152
MASKED = -1e30
SCALE = 1.0 / math.sqrt(HEAD)
MESH = pl.DeviceIdType.MESH
F32 = jnp.float32
BF16 = jnp.bfloat16


def place():
    d = lax.axis_index("dp")
    c = lax.axis_index("context")
    return lax.rem(d, NX), lax.div(d, NX), lax.div(c, 2), lax.rem(c, 2)


def device(x, y, z, h):
    return (y * NX + x, z * 2 + h)


def around(i, by, n):
    return lax.rem(i + (by + n), n)


class Copies:
    def __init__(self, send, recv):
        self.send, self.recv, self.used, self.all = send, recv, 0, []

    def claim(self):
        self.used += 1
        return self.used - 1

    def make(self, i, src, dst, target):
        return pltpu.make_async_remote_copy(
            src_ref=src,
            dst_ref=dst,
            send_sem=self.send.at[i],
            recv_sem=self.recv.at[i],
            device_id=target,
            device_id_type=MESH,
        )

    def remote(self, src, dst, target):
        copy = self.make(self.claim(), src, dst, target)
        copy.start()
        self.all.append(copy)
        return copy

    def local(self, src, dst):
        copy = pltpu.make_async_copy(src, dst, self.send.at[self.claim()])
        copy.start()
        return copy

    def wait_sends(self):
        for copy in self.all:
            copy.wait_send()


def greet(targets):
    barrier = pltpu.get_barrier_semaphore()
    for target in targets:
        pl.semaphore_signal(barrier, inc=1, device_id=target, device_id_type=MESH)
    pl.semaphore_wait(barrier, len(targets))


def lanes(start, size):
    return pl.ds(pl.multiple_of(start, 128), size)


def rows_at(start, size):
    return pl.ds(pl.multiple_of(start, 128), size)


def rows16(block):
    return pl.ds(pl.multiple_of(block * 16, 16), 16)


def fill_bias(docs, bias, z):
    ends = []
    total = docs[0, 0]
    for i in range(5):
        ends.append(total)
        if i < 4:
            total = total + docs[0, i + 1]

    def doc(b):
        return sum((b >= e).astype(jnp.int32) for e in ends)

    key = lax.broadcasted_iota(jnp.int32, (BLK, BLK), 0)
    query = lax.broadcasted_iota(jnp.int32, (BLK, BLK), 1)
    for j in range(2):
        qb = 2 * z + j
        for i in range(9):
            kb = 2 * z - 2 * (i // 2) + (1 if i == 8 else i % 2)
            if i < 2 and i == j:
                block = jnp.where(key <= query, 0.0, MASKED)
            elif i == 1 and j == 0:
                block = jnp.full((BLK, BLK), MASKED, F32)
            else:
                same = (kb >= 0) & (doc(kb) == doc(qb))
                block = jnp.full((BLK, BLK), jnp.where(same, 0.0, MASKED), F32)
            bias[pl.ds(i * BLK, BLK), pl.ds(j * BLK, BLK)] = block


def kernel(
    docs, q, g, k, v, xin, key_grad, wv_grad,
    qg, qs, kv, xs, relay, bias, expo, low, top, inv, dv, dk, csend, crecv, dvt, part, ysend, yrecv, zsend, zrecv, kswap,
    send, recv,
):
    x, y, z, h = place()
    ctx = z * 2 + h
    sib = device(x, y, z, 1 - h)
    up = device(x, y, around(z, 1, NZ), h)
    down = device(x, y, around(z, -1, NZ), h)
    across = [device(around(x, dx, NX), y, z, h) for dx in range(1, NX)]
    ahead = device(x, around(y, 1, NY), z, h)
    behind = device(x, around(y, -1, NY), z, h)
    column = [(y * NX + x, around(ctx, o, 16)) for o in range(1, 16)]
    mine = rows_at(h * BLK, BLK)
    copies = Copies(send, recv)

    def x_rows(dx):
        return rows_at(dx * 256 + h * BLK, BLK)

    own_k, own_v = [
        [
            copies.local(src.at[:, lanes((2 * h + a) * HEAD, HEAD)], kv.at[a, j, mine])
            for a in range(2)
        ]
        for j, src in enumerate((k, v))
    ]
    own_q = [
        copies.local(src.at[:, lanes(h * 2048, 2048)], qg.at[j, mine])
        for j, src in enumerate((q, g))
    ]
    greet(column + across + [ahead, behind])

    def swap_kv(j, src):
        return [
            copies.remote(
                src.at[:, lanes((2 * (1 - h) + a) * HEAD, HEAD)], kv.at[a, j, mine], sib
            )
            for a in range(2)
        ]

    hops = {}
    swapped = {0: swap_kv(0, k)}

    def hop(j, a, step):
        if step == 1:
            swapped[j][a].wait_recv()
            (own_k, own_v)[j][a].wait()
        else:
            hops[j, a].wait_recv()
        lo, size = (768 + 128, 128) if step == 4 else ((step - 1) * 256, 256)
        hops[j, a] = copies.remote(
            kv.at[a, j, pl.ds(lo, size)], kv.at[a, j, pl.ds(step * 256, size)], up
        )

    for a in range(2):
        hop(0, a, 1)
    exchange = [
        copies.remote(src.at[:, lanes((1 - h) * 2048, 2048)], qg.at[j, mine], sib)
        for j, src in enumerate((q, g))
    ]
    swapped[1] = swap_kv(1, v)
    right, left = across[0], across[2]
    spread_x, relays, pieces = {}, {}, []

    def piece(i, dx, c, dst, target):
        to = around(x, dx, NX)
        src = xin.at[:, lanes(c * 1024 + to * 256, 256)]
        pieces.append(lambda: copies.make(i, src, dst, target).start())

    ways = ((0, right), (1, left))
    claimed = [copies.claim() for _ in range(4)]
    for c in range(4):
        for way, target in ways:
            dst = relay.at[way, :, pl.ds(c * 256, 256)]
            piece(claimed[way], 2, way * 4 + c, dst, target)
    for c in range(NY):
        for way, target in ways:
            dx = 1 + 2 * way
            piece(claimed[2 + way], dx, c, xs.at[x_rows(dx), pl.ds(c * 256, 256)], target)
    for way, target in ways:
        dx = 1 + 2 * way
        relays[way] = copies.make(claimed[way], relay.at[way], relay.at[way], target)
        spread_x[dx] = copies.make(claimed[2 + way], xs.at[x_rows(dx)], xs.at[x_rows(dx)], target)
        copies.all += [relays[way], spread_x[dx]]
    second = []

    def feed(n):
        for _ in range(n):
            pieces.pop(0)()

    def relay_on():
        for way, target in ways:
            relays[way].wait_recv()
            second.append(
                copies.remote(
                    relay.at[way], xs.at[x_rows(2), pl.ds(way * 1024, 1024)], target
                )
            )

    own_x = [
        copies.local(
            xin.at[:, lanes(c * 1024 + x * 256, 256)], xs.at[x_rows(0), pl.ds(c * 256, 256)]
        )
        for c in range(NY)
    ]
    passed = {}

    def pass_x(dx):
        if dx == 0:
            for copy in own_x:
                copy.wait()
        elif dx == 2:
            for copy in second:
                copy.wait_recv()
        else:
            spread_x[dx].wait_recv()
        passed[dx] = copies.remote(xs.at[x_rows(dx)], xs.at[x_rows(dx)], sib)

    contract = (((1,), (1,)), ((), ()))

    def slot_rows(slot):
        return pl.ds(slot * 256, 128 if slot == 4 else 256)

    def heads(one, *args):
        @pl.loop(0, 4)
        def _(i):
            one(*args, 2 * i)
            one(*args, 2 * i + 1)

    def score(a, slot, head):
        rows = slot_rows(slot)
        col = lanes((a * 8 + head) * HEAD, HEAD)
        s = lax.dot_general(kv[a, 0, rows], qg[0, :, col], contract, preferred_element_type=F32)
        t = s * (SCALE * math.log2(math.e)) + bias[rows, :]
        expo[a, rows, lanes(head * 256, 256)] = t
        highest = jnp.max(t.reshape(-1, 8, 256), axis=0)
        if slot > 0:
            highest = jnp.maximum(highest, top[a * 8 + head])
        top[a * 8 + head] = highest

    def weigh(a, head):
        cols = lanes(head * 256, 256)
        m = jnp.max(top[a * 8 + head], axis=0, keepdims=True)
        e = jnp.exp2(expo[a, :, cols] - m)
        expo[a, :, cols] = e
        r = 1.0 / jnp.sum(e, axis=0, keepdims=True)
        inv[a * 8 + head] = r
        low[a, :, cols] = (e * r).astype(BF16)

    def push_back(a, head):
        cols = lanes(head * 256, 256)
        col = lanes((a * 8 + head) * HEAD, HEAD)
        dp = lax.dot_general(kv[a, 1], qg[1, :, col], contract, preferred_element_type=F32)
        p = expo[a, :, cols] * inv[a * 8 + head]
        delta = jnp.sum(p * dp, axis=0, keepdims=True)
        low[a, :, cols] = (p * (dp - delta)).astype(BF16)

    def sum_heads(w, a, slot):
        rows = slot_rows(slot)
        parts[w][a, rows] = jnp.dot(low[a, rows], qs[1 - w, a], preferred_element_type=F32)

    parts = (dv, dk)
    chain = {}

    def chain_step(w, a, step):
        i = 2 * w + a
        if step > 1:
            chain[i].wait_recv()
        if step == 1:
            csend[i, 0, pl.ds(0, 128)] = parts[w][a, pl.ds(1024, 128)].astype(BF16)
            src, dst = csend.at[i, 0, pl.ds(0, 128)], crecv.at[i, 0, pl.ds(0, 128)]
        else:
            here = parts[w][a, pl.ds((5 - step) * 256, 256)]
            if step == 2:
                csend[i, 1, pl.ds(0, 128)] = here[:128].astype(BF16)
                csend[i, 1, pl.ds(128, 128)] = (
                    here[128:] + crecv[i, 0, pl.ds(0, 128)].astype(F32)
                ).astype(BF16)
            else:
                csend[i, step - 1] = (here + crecv[i, step - 2].astype(F32)).astype(BF16)
            src, dst = csend.at[i, step - 1], crecv.at[i, step - 1]
        chain[i] = copies.remote(src, dst, down)

    def chain_end(w, a):
        i = 2 * w + a
        chain[i].wait_recv()
        return parts[w][a, pl.ds(0, 256)] + crecv[i, 3].astype(F32)

    spread = {}

    def spread_dv(a):
        dvt[a, :, 0:256] = chain_end(0, a).T.astype(BF16)
        for dx in (2, 1, 3):
            spread[a, dx] = copies.remote(
                dvt.at[a, :, pl.ds(0, 256)], dvt.at[a, :, pl.ds(dx * 256, 256)], across[dx - 1]
            )

    def wait_x():
        for dx in range(NX):
            passed[dx].wait_recv()

    def product(a):
        for dx in range(1, NX):
            spread[a, dx].wait_recv()

        def chunk(c):
            part[a, c] = jnp.dot(
                dvt[a], xs[:, lanes(c * 256, 256)], preferred_element_type=F32
            )

        chunk(around(y, 4, NY))
        chunk(around(y, 5 - 2 * a, NY))
        ring_step(a, 1)

        @pl.loop(0, 6)
        def _(i):
            chunk(lax.rem(y + (6 - a) + i, NY))

    lengths = {(0, 0): 4, (0, 1): 3, (1, 0): 3, (1, 1): 4}
    ring = {}

    def ring_step(a, step):
        for way, target in ((0, ahead), (1, behind)):
            sign = 1 - 2 * way
            n = lengths[a, way]
            if step > n:
                continue
            here = part[a, around(y, sign * (n - step + 1), NY)]
            if step > 1:
                ring[a, way].wait_recv()
                here = here + yrecv[a, way, step - 2].astype(F32)
            ysend[a, way, step - 1] = here.astype(BF16)
            ring[a, way] = copies.remote(
                ysend.at[a, way, step - 1], yrecv.at[a, way, step - 1], target
            )

    def ring_end(a):
        for way in range(2):
            ring[a, way].wait_recv()
        total = (
            part[a, y]
            + yrecv[a, 0, lengths[a, 0] - 1].astype(F32)
            + yrecv[a, 1, lengths[a, 1] - 1].astype(F32)
        )
        zsend[:, a * HEAD : (a + 1) * HEAD] = total.T.astype(BF16)

    feed(4)
    fill_bias(docs, bias, z)
    for copy in own_q:
        copy.wait()
    for copy in exchange:
        copy.wait_recv()

    @pl.loop(0, 16)
    def _(i):
        a, head = lax.div(i, 8), lax.rem(i, 8)
        for j in range(2):
            qs[j, a, rows_at(head * 256, 256)] = qg[j, :, lanes(i * HEAD, HEAD)]

    for slot in range(5):
        for a in range(2):
            if 1 <= slot < 4:
                hop(0, a, slot + 1)
            elif slot == 4:
                hops[0, a].wait_recv()
        if slot >= 2:
            for a in range(2):
                hop(1, a, slot - 1)
        if slot == 3:
            relay_on()
        feed(4)
        for a in range(2):
            heads(score, a, slot)
    heads(weigh, 0)
    sum_heads(0, 0, 4)
    chain_step(0, 0, 1)
    for a in range(2):
        hop(1, a, 4)
    for slot in (3, 2, 1, 0):
        sum_heads(0, 0, slot)
    heads(weigh, 1)
    sum_heads(0, 1, 4)
    chain_step(0, 1, 1)
    for slot in (3, 2, 1, 0):
        sum_heads(0, 1, slot)
    chain_step(0, 0, 2)

    for a in range(2):
        hops[1, a].wait_recv()
    order = [(a, head) for a in range(2) for head in range(8)]

    def some(n):
        for _ in range(n):
            push_back(*order.pop(0))

    some(3)
    chain_step(0, 1, 2)
    some(2)
    chain_step(0, 0, 3)
    some(3)
    sum_heads(1, 0, 4)
    chain_step(1, 0, 1)
    chain_step(0, 1, 3)
    for slot in (3, 2, 1, 0):
        sum_heads(1, 0, slot)
    some(1)
    chain_step(0, 0, 4)
    for dx in (0, 1, 3):
        pass_x(dx)
    some(3)
    chain_step(0, 1, 4)
    chain_step(1, 0, 2)
    some(2)
    spread_dv(0)
    some(2)
    sum_heads(1, 1, 4)
    chain_step(1, 1, 1)
    pass_x(2)
    chain_step(1, 0, 3)
    for slot in (3, 2, 1, 0):
        sum_heads(1, 1, slot)
    spread_dv(1)
    wait_x()
    product(0)
    chain_step(1, 1, 2)
    chain_step(1, 0, 4)
    product(1)
    ring_step(0, 2)
    chain_step(1, 1, 3)
    ring_step(1, 2)
    ring_step(0, 3)
    ring_step(1, 3)
    chain_step(1, 1, 4)
    ring_step(0, 4)
    ring_step(1, 4)
    kswap[0, :, 0:HEAD] = (chain_end(1, 0) * SCALE).astype(BF16)
    ring_end(0)
    ring_end(1)
    direct = [
        copies.remote(zsend.at[rows16(around(ctx, o, 16))], zrecv.at[o], column[o - 1])
        for o in range(1, 16)
    ]
    kswap[0, :, HEAD : 2 * HEAD] = (chain_end(1, 1) * SCALE).astype(BF16)
    swap = copies.remote(
        kswap.at[0, rows_at((1 - h) * BLK, BLK)], kswap.at[1, pl.ds(0, BLK)], sib
    )
    key_grad[:, lanes(h * 256, 256)] = kswap[0, rows_at(h * BLK, BLK), :]
    sums = [zsend[rows16(ctx), :].astype(F32), None]
    for o in range(1, 16):
        direct[o - 1].wait_recv()
        got = zrecv[o].astype(F32)
        sums[o % 2] = got if sums[o % 2] is None else sums[o % 2] + got
    wv_grad[:, lanes(h * 256, 256)] = sums[0]
    wv_grad[:, lanes((1 - h) * 256, 256)] = sums[1]
    swap.wait_recv()
    key_grad[:, lanes((1 - h) * 256, 256)] = kswap[1, pl.ds(0, BLK), :]
    copies.wait_sends()


def on_device(queries, keys, values, out_grad, layer_input, doc_blocks):
    anywhere = pl.BlockSpec(memory_space=pl.ANY)
    in_vmem = pl.BlockSpec(memory_space=pltpu.VMEM)
    key_grad, wv_grad = pl.pallas_call(
        kernel,
        out_shape=(
            jax.ShapeDtypeStruct((BLK, 512), BF16),
            jax.ShapeDtypeStruct((16, 512), F32),
        ),
        in_specs=[pl.BlockSpec(memory_space=pltpu.SMEM)] + [anywhere] * 5,
        out_specs=(in_vmem, in_vmem),
        scratch_shapes=[
            pltpu.VMEM((2, 256, 2048), BF16),
            pltpu.VMEM((2, 2, 2048, HEAD), BF16),
            pltpu.VMEM((2, 2, ROWS, HEAD), BF16),
            pltpu.VMEM((NX * 256, 2048), BF16),
            pltpu.VMEM((2, BLK, 1024), BF16),
            pltpu.VMEM((ROWS, 256), F32),
            pltpu.VMEM((2, ROWS, 2048), F32),
            pltpu.VMEM((2, ROWS, 2048), BF16),
            pltpu.VMEM((16, 8, 256), F32),
            pltpu.VMEM((16, 1, 256), F32),
            pltpu.VMEM((2, ROWS, HEAD), F32),
            pltpu.VMEM((2, ROWS, HEAD), F32),
            pltpu.VMEM((4, HOPS, 256, HEAD), BF16),
            pltpu.VMEM((4, HOPS, 256, HEAD), BF16),
            pltpu.VMEM((2, HEAD, NX * 256), BF16),
            pltpu.VMEM((2, NY, HEAD, 256), F32),
            pltpu.VMEM((2, 2, 4, HEAD, 256), BF16),
            pltpu.VMEM((2, 2, 4, HEAD, 256), BF16),
            pltpu.VMEM((256, 256), BF16),
            pltpu.VMEM((16, 16, 256), BF16),
            pltpu.VMEM((2, 256, 256), BF16),
            pltpu.SemaphoreType.DMA((112,)),
            pltpu.SemaphoreType.DMA((112,)),
        ],
        compiler_params=pltpu.CompilerParams(
            collective_id=0, has_side_effects=True, vmem_limit_bytes=56 << 20
        ),
        name="grads",
    )(doc_blocks, queries[0], out_grad[0], keys[0], values[0], layer_input[0])
    return (key_grad[None], wv_grad)


def solution(mesh):
    in_specs = (
        P("dp", "context", None),
        P("dp", "context", None),
        P("dp", "context", None),
        P("dp", "context", None),
        P("dp", "context", None),
        P("dp", None),
    )
    out_specs = (P("dp", "context", None), P(("dp", "context"), None))
    return jax.shard_map(
        on_device, mesh=mesh, in_specs=in_specs, out_specs=out_specs, check_vma=False
    )
```

```python
import math

import jax
import jax.numpy as jnp
from jax import lax
from jax.experimental import pallas as pl
from jax.experimental.pallas import tpu as pltpu
from jax.sharding import PartitionSpec as P

HEAD = 128
BLK = 128
NX, NY, NZ = 4, 8, 8
HOPS = 4
ROWS = 1152
MASKED = -1e30
SCALE = 1.0 / math.sqrt(HEAD)
MESH = pl.DeviceIdType.MESH
F32 = jnp.float32
BF16 = jnp.bfloat16


def place():
    d = lax.axis_index("dp")
    c = lax.axis_index("context")
    return lax.rem(d, NX), lax.div(d, NX), lax.div(c, 2), lax.rem(c, 2)


def device(x, y, z, h):
    return (y * NX + x, z * 2 + h)


def around(i, by, n):
    return lax.rem(i + (by + n), n)


class Copies:
    def __init__(self, send, recv):
        self.send, self.recv, self.used, self.all = send, recv, 0, []

    def claim(self):
        self.used += 1
        return self.used - 1

    def make(self, i, src, dst, target):
        return pltpu.make_async_remote_copy(
            src_ref=src,
            dst_ref=dst,
            send_sem=self.send.at[i],
            recv_sem=self.recv.at[i],
            device_id=target,
            device_id_type=MESH,
        )

    def remote(self, src, dst, target):
        copy = self.make(self.claim(), src, dst, target)
        copy.start()
        self.all.append(copy)
        return copy

    def local(self, src, dst):
        copy = pltpu.make_async_copy(src, dst, self.send.at[self.claim()])
        copy.start()
        return copy

    def wait_sends(self):
        for copy in self.all:
            copy.wait_send()


def greet(targets):
    barrier = pltpu.get_barrier_semaphore()
    for target in targets:
        pl.semaphore_signal(barrier, inc=1, device_id=target, device_id_type=MESH)
    pl.semaphore_wait(barrier, len(targets))


def lanes(start, size):
    return pl.ds(pl.multiple_of(start, 128), size)


def rows_at(start, size):
    return pl.ds(pl.multiple_of(start, 128), size)


def rows16(block):
    return pl.ds(pl.multiple_of(block * 16, 16), 16)


def fill_bias(docs, bias, z):
    ends = []
    total = docs[0, 0]
    for i in range(5):
        ends.append(total)
        if i < 4:
            total = total + docs[0, i + 1]

    def doc(b):
        return sum((b >= e).astype(jnp.int32) for e in ends)

    key = lax.broadcasted_iota(jnp.int32, (BLK, BLK), 0)
    query = lax.broadcasted_iota(jnp.int32, (BLK, BLK), 1)
    for j in range(2):
        qb = 2 * z + j
        for i in range(9):
            kb = 2 * z - 2 * (i // 2) + (1 if i == 8 else i % 2)
            if i < 2 and i == j:
                block = jnp.where(key <= query, 0.0, MASKED)
            elif i == 1 and j == 0:
                block = jnp.full((BLK, BLK), MASKED, F32)
            else:
                same = (kb >= 0) & (doc(kb) == doc(qb))
                block = jnp.full((BLK, BLK), jnp.where(same, 0.0, MASKED), F32)
            bias[pl.ds(i * BLK, BLK), pl.ds(j * BLK, BLK)] = block


def kernel(
    docs, q, g, k, v, xin, key_grad, wv_grad,
    qg, qs, kv, xs, relay, bias, expo, low, top, inv, dv, dk, csend, crecv, dvt, part, ysend, yrecv, zsend, zrecv, kswap,
    send, recv,
):
    x, y, z, h = place()
    ctx = z * 2 + h
    sib = device(x, y, z, 1 - h)
    up = device(x, y, around(z, 1, NZ), h)
    down = device(x, y, around(z, -1, NZ), h)
    across = [device(around(x, dx, NX), y, z, h) for dx in range(1, NX)]
    ahead = device(x, around(y, 1, NY), z, h)
    behind = device(x, around(y, -1, NY), z, h)
    column = [(y * NX + x, around(ctx, o, 16)) for o in range(1, 16)]
    mine = rows_at(h * BLK, BLK)
    copies = Copies(send, recv)

    def x_rows(dx):
        return rows_at(dx * 256 + h * BLK, BLK)

    own_k, own_v = [
        [
            copies.local(src.at[:, lanes((2 * h + a) * HEAD, HEAD)], kv.at[a, j, mine])
            for a in range(2)
        ]
        for j, src in enumerate((k, v))
    ]
    own_q = [
        copies.local(src.at[:, lanes(h * 2048, 2048)], qg.at[j, mine])
        for j, src in enumerate((q, g))
    ]
    greet(column + across + [ahead, behind])

    def swap_kv(j, src):
        return [
            copies.remote(
                src.at[:, lanes((2 * (1 - h) + a) * HEAD, HEAD)], kv.at[a, j, mine], sib
            )
            for a in range(2)
        ]

    hops = {}
    swapped = {0: swap_kv(0, k)}

    def hop(j, a, step):
        if step == 1:
            swapped[j][a].wait_recv()
            (own_k, own_v)[j][a].wait()
        else:
            hops[j, a].wait_recv()
        lo, size = (768 + 128, 128) if step == 4 else ((step - 1) * 256, 256)
        hops[j, a] = copies.remote(
            kv.at[a, j, pl.ds(lo, size)], kv.at[a, j, pl.ds(step * 256, size)], up
        )

    for a in range(2):
        hop(0, a, 1)
    exchange = [
        copies.remote(src.at[:, lanes((1 - h) * 2048, 2048)], qg.at[j, mine], sib)
        for j, src in enumerate((q, g))
    ]
    swapped[1] = swap_kv(1, v)
    right, left = across[0], across[2]
    spread_x, relays, pieces = {}, {}, []

    def piece(i, dx, c, dst, target):
        to = around(x, dx, NX)
        src = xin.at[:, lanes(c * 1024 + to * 256, 256)]
        pieces.append(lambda: copies.make(i, src, dst, target).start())

    ways = ((0, right), (1, left))
    claimed = [copies.claim() for _ in range(4)]
    for c in range(4):
        for way, target in ways:
            dst = relay.at[way, :, pl.ds(c * 256, 256)]
            piece(claimed[way], 2, way * 4 + c, dst, target)
    for c in range(NY):
        for way, target in ways:
            dx = 1 + 2 * way
            piece(claimed[2 + way], dx, c, xs.at[x_rows(dx), pl.ds(c * 256, 256)], target)
    for way, target in ways:
        dx = 1 + 2 * way
        relays[way] = copies.make(claimed[way], relay.at[way], relay.at[way], target)
        spread_x[dx] = copies.make(claimed[2 + way], xs.at[x_rows(dx)], xs.at[x_rows(dx)], target)
        copies.all += [relays[way], spread_x[dx]]
    second = []

    def feed(n):
        for _ in range(n):
            pieces.pop(0)()

    def relay_on():
        for way, target in ways:
            relays[way].wait_recv()
            second.append(
                copies.remote(
                    relay.at[way], xs.at[x_rows(2), pl.ds(way * 1024, 1024)], target
                )
            )

    own_x = [
        copies.local(
            xin.at[:, lanes(c * 1024 + x * 256, 256)], xs.at[x_rows(0), pl.ds(c * 256, 256)]
        )
        for c in range(NY)
    ]
    passed = {}

    i = copies.claim()
    for c in range(NY):
        copies.make(
            i,
            xin.at[:, lanes(c * 1024 + x * 256, 256)],
            xs.at[x_rows(0), pl.ds(c * 256, 256)],
            sib,
        ).start()
    passed[0] = copies.make(i, xs.at[x_rows(0)], xs.at[x_rows(0)], sib)
    copies.all.append(passed[0])

    def pass_x(dx):
        if dx == 2:
            for copy in second:
                copy.wait_recv()
        else:
            spread_x[dx].wait_recv()
        passed[dx] = copies.remote(xs.at[x_rows(dx)], xs.at[x_rows(dx)], sib)

    contract = (((1,), (1,)), ((), ()))

    def slot_rows(slot):
        return pl.ds(slot * 256, 128 if slot == 4 else 256)

    def heads(one, *args):
        @pl.loop(0, 4)
        def _(i):
            one(*args, 2 * i)
            one(*args, 2 * i + 1)

    def score(a, slot, head):
        rows = slot_rows(slot)
        col = lanes((a * 8 + head) * HEAD, HEAD)
        s = lax.dot_general(kv[a, 0, rows], qg[0, :, col], contract, preferred_element_type=F32)
        t = s * (SCALE * math.log2(math.e)) + bias[rows, :]
        expo[a, rows, lanes(head * 256, 256)] = t
        highest = jnp.max(t.reshape(-1, 8, 256), axis=0)
        if slot > 0:
            highest = jnp.maximum(highest, top[a * 8 + head])
        top[a * 8 + head] = highest

    def weigh(a, head):
        cols = lanes(head * 256, 256)
        m = jnp.max(top[a * 8 + head], axis=0, keepdims=True)
        e = jnp.exp2(expo[a, :, cols] - m)
        expo[a, :, cols] = e
        r = 1.0 / jnp.sum(e, axis=0, keepdims=True)
        inv[a * 8 + head] = r
        low[a, :, cols] = (e * r).astype(BF16)

    def push_back(a, head):
        cols = lanes(head * 256, 256)
        col = lanes((a * 8 + head) * HEAD, HEAD)
        dp = lax.dot_general(kv[a, 1], qg[1, :, col], contract, preferred_element_type=F32)
        p = expo[a, :, cols] * inv[a * 8 + head]
        delta = jnp.sum(p * dp, axis=0, keepdims=True)
        low[a, :, cols] = (p * (dp - delta)).astype(BF16)

    def sum_heads(w, a, slot):
        rows = slot_rows(slot)
        parts[w][a, rows] = jnp.dot(low[a, rows], qs[1 - w, a], preferred_element_type=F32)

    parts = (dv, dk)
    chain = {}

    def chain_step(w, a, step):
        i = 2 * w + a
        if step > 1:
            chain[i].wait_recv()
        if step == 1:
            csend[i, 0, pl.ds(0, 128)] = parts[w][a, pl.ds(1024, 128)].astype(BF16)
            src, dst = csend.at[i, 0, pl.ds(0, 128)], crecv.at[i, 0, pl.ds(0, 128)]
        else:
            here = parts[w][a, pl.ds((5 - step) * 256, 256)]
            if step == 2:
                csend[i, 1, pl.ds(0, 128)] = here[:128].astype(BF16)
                csend[i, 1, pl.ds(128, 128)] = (
                    here[128:] + crecv[i, 0, pl.ds(0, 128)].astype(F32)
                ).astype(BF16)
            else:
                csend[i, step - 1] = (here + crecv[i, step - 2].astype(F32)).astype(BF16)
            src, dst = csend.at[i, step - 1], crecv.at[i, step - 1]
        chain[i] = copies.remote(src, dst, down)

    def chain_end(w, a):
        i = 2 * w + a
        chain[i].wait_recv()
        return parts[w][a, pl.ds(0, 256)] + crecv[i, 3].astype(F32)

    spread = {}

    def spread_dv(a):
        dvt[a, :, 0:256] = chain_end(0, a).T.astype(BF16)
        for dx in (2, 1, 3):
            spread[a, dx] = copies.remote(
                dvt.at[a, :, pl.ds(0, 256)], dvt.at[a, :, pl.ds(dx * 256, 256)], across[dx - 1]
            )

    def wait_x():
        for copy in own_x:
            copy.wait()
        for dx in range(NX):
            passed[dx].wait_recv()

    def product(a):
        for dx in range(1, NX):
            spread[a, dx].wait_recv()

        def chunk(c):
            part[a, c] = jnp.dot(
                dvt[a], xs[:, lanes(c * 256, 256)], preferred_element_type=F32
            )

        chunk(around(y, 4, NY))
        chunk(around(y, 5 - 2 * a, NY))
        ring_step(a, 1)

        @pl.loop(0, 6)
        def _(i):
            chunk(lax.rem(y + (6 - a) + i, NY))

    lengths = {(0, 0): 4, (0, 1): 3, (1, 0): 3, (1, 1): 4}
    ring = {}

    def ring_step(a, step):
        for way, target in ((0, ahead), (1, behind)):
            sign = 1 - 2 * way
            n = lengths[a, way]
            if step > n:
                continue
            here = part[a, around(y, sign * (n - step + 1), NY)]
            if step > 1:
                ring[a, way].wait_recv()
                here = here + yrecv[a, way, step - 2].astype(F32)
            ysend[a, way, step - 1] = here.astype(BF16)
            ring[a, way] = copies.remote(
                ysend.at[a, way, step - 1], yrecv.at[a, way, step - 1], target
            )

    def ring_end(a):
        for way in range(2):
            ring[a, way].wait_recv()
        total = (
            part[a, y]
            + yrecv[a, 0, lengths[a, 0] - 1].astype(F32)
            + yrecv[a, 1, lengths[a, 1] - 1].astype(F32)
        )
        zsend[:, a * HEAD : (a + 1) * HEAD] = total.T.astype(BF16)

    feed(4)
    fill_bias(docs, bias, z)
    for copy in own_q:
        copy.wait()
    for copy in exchange:
        copy.wait_recv()

    @pl.loop(0, 16)
    def _(i):
        a, head = lax.div(i, 8), lax.rem(i, 8)
        for j in range(2):
            qs[j, a, rows_at(head * 256, 256)] = qg[j, :, lanes(i * HEAD, HEAD)]

    for slot in range(5):
        for a in range(2):
            if 1 <= slot < 4:
                hop(0, a, slot + 1)
            elif slot == 4:
                hops[0, a].wait_recv()
        if slot >= 2:
            for a in range(2):
                hop(1, a, slot - 1)
        if slot == 3:
            relay_on()
        feed(4)
        for a in range(2):
            heads(score, a, slot)
    heads(weigh, 0)
    sum_heads(0, 0, 4)
    chain_step(0, 0, 1)
    for a in range(2):
        hop(1, a, 4)
    for slot in (3, 2, 1, 0):
        sum_heads(0, 0, slot)
    heads(weigh, 1)
    sum_heads(0, 1, 4)
    chain_step(0, 1, 1)
    for slot in (3, 2, 1, 0):
        sum_heads(0, 1, slot)
    chain_step(0, 0, 2)
    pass_x(1)
    pass_x(3)

    for a in range(2):
        hops[1, a].wait_recv()
    order = [(a, head) for a in range(2) for head in range(8)]

    def some(n):
        for _ in range(n):
            push_back(*order.pop(0))

    some(3)
    chain_step(0, 1, 2)
    some(2)
    chain_step(0, 0, 3)
    some(3)
    sum_heads(1, 0, 4)
    chain_step(1, 0, 1)
    chain_step(0, 1, 3)
    pass_x(2)
    for slot in (3, 2, 1, 0):
        sum_heads(1, 0, slot)
    some(1)
    chain_step(0, 0, 4)
    some(3)
    chain_step(0, 1, 4)
    chain_step(1, 0, 2)
    some(2)
    spread_dv(0)
    some(2)
    sum_heads(1, 1, 4)
    chain_step(1, 1, 1)
    chain_step(1, 0, 3)
    for slot in (3, 2, 1, 0):
        sum_heads(1, 1, slot)
    spread_dv(1)
    wait_x()
    product(0)
    chain_step(1, 1, 2)
    chain_step(1, 0, 4)
    product(1)
    ring_step(0, 2)
    chain_step(1, 1, 3)
    ring_step(1, 2)
    ring_step(0, 3)
    ring_step(1, 3)
    chain_step(1, 1, 4)
    ring_step(0, 4)
    ring_step(1, 4)
    kswap[0, :, 0:HEAD] = (chain_end(1, 0) * SCALE).astype(BF16)
    ring_end(0)
    ring_end(1)
    direct = [
        copies.remote(zsend.at[rows16(around(ctx, o, 16))], zrecv.at[o], column[o - 1])
        for o in range(1, 16)
    ]
    kswap[0, :, HEAD : 2 * HEAD] = (chain_end(1, 1) * SCALE).astype(BF16)
    swap = copies.remote(
        kswap.at[0, rows_at((1 - h) * BLK, BLK)], kswap.at[1, pl.ds(0, BLK)], sib
    )
    key_grad[:, lanes(h * 256, 256)] = kswap[0, rows_at(h * BLK, BLK), :]
    sums = [zsend[rows16(ctx), :].astype(F32), None]
    for o in range(1, 16):
        direct[o - 1].wait_recv()
        got = zrecv[o].astype(F32)
        sums[o % 2] = got if sums[o % 2] is None else sums[o % 2] + got
    wv_grad[:, lanes(h * 256, 256)] = sums[0]
    wv_grad[:, lanes((1 - h) * 256, 256)] = sums[1]
    swap.wait_recv()
    key_grad[:, lanes((1 - h) * 256, 256)] = kswap[1, pl.ds(0, BLK), :]
    copies.wait_sends()


def on_device(queries, keys, values, out_grad, layer_input, doc_blocks):
    anywhere = pl.BlockSpec(memory_space=pl.ANY)
    in_vmem = pl.BlockSpec(memory_space=pltpu.VMEM)
    key_grad, wv_grad = pl.pallas_call(
        kernel,
        out_shape=(
            jax.ShapeDtypeStruct((BLK, 512), BF16),
            jax.ShapeDtypeStruct((16, 512), F32),
        ),
        in_specs=[pl.BlockSpec(memory_space=pltpu.SMEM)] + [anywhere] * 5,
        out_specs=(in_vmem, in_vmem),
        scratch_shapes=[
            pltpu.VMEM((2, 256, 2048), BF16),
            pltpu.VMEM((2, 2, 2048, HEAD), BF16),
            pltpu.VMEM((2, 2, ROWS, HEAD), BF16),
            pltpu.VMEM((NX * 256, 2048), BF16),
            pltpu.VMEM((2, BLK, 1024), BF16),
            pltpu.VMEM((ROWS, 256), F32),
            pltpu.VMEM((2, ROWS, 2048), F32),
            pltpu.VMEM((2, ROWS, 2048), BF16),
            pltpu.VMEM((16, 8, 256), F32),
            pltpu.VMEM((16, 1, 256), F32),
            pltpu.VMEM((2, ROWS, HEAD), F32),
            pltpu.VMEM((2, ROWS, HEAD), F32),
            pltpu.VMEM((4, HOPS, 256, HEAD), BF16),
            pltpu.VMEM((4, HOPS, 256, HEAD), BF16),
            pltpu.VMEM((2, HEAD, NX * 256), BF16),
            pltpu.VMEM((2, NY, HEAD, 256), F32),
            pltpu.VMEM((2, 2, 4, HEAD, 256), BF16),
            pltpu.VMEM((2, 2, 4, HEAD, 256), BF16),
            pltpu.VMEM((256, 256), BF16),
            pltpu.VMEM((16, 16, 256), BF16),
            pltpu.VMEM((2, 256, 256), BF16),
            pltpu.SemaphoreType.DMA((112,)),
            pltpu.SemaphoreType.DMA((112,)),
        ],
        compiler_params=pltpu.CompilerParams(
            collective_id=0, has_side_effects=True, vmem_limit_bytes=53 << 20
        ),
        name="grads",
    )(doc_blocks, queries[0], out_grad[0], keys[0], values[0], layer_input[0])
    return (key_grad[None], wv_grad)


def solution(mesh):
    in_specs = (
        P("dp", "context", None),
        P("dp", "context", None),
        P("dp", "context", None),
        P("dp", "context", None),
        P("dp", "context", None),
        P("dp", None),
    )
    out_specs = (P("dp", "context", None), P(("dp", "context"), None))
    return jax.shard_map(
        on_device, mesh=mesh, in_specs=in_specs, out_specs=out_specs, check_vma=False
    )
```

```python
import math

import jax
import jax.numpy as jnp
from jax import lax
from jax.experimental import pallas as pl
from jax.experimental.pallas import tpu as pltpu
from jax.sharding import PartitionSpec as P

HEAD = 128
BLK = 128
NX, NY, NZ = 4, 8, 8
HOPS = 4
ROWS = 1152
MASKED = -1e30
SCALE = 1.0 / math.sqrt(HEAD)
MESH = pl.DeviceIdType.MESH
F32 = jnp.float32
BF16 = jnp.bfloat16


def place():
    d = lax.axis_index("dp")
    c = lax.axis_index("context")
    return lax.rem(d, NX), lax.div(d, NX), lax.div(c, 2), lax.rem(c, 2)


def device(x, y, z, h):
    return (y * NX + x, z * 2 + h)


def around(i, by, n):
    return lax.rem(i + (by + n), n)


class Copies:
    def __init__(self, send, recv):
        self.send, self.recv, self.used, self.all = send, recv, 0, []

    def claim(self):
        self.used += 1
        return self.used - 1

    def make(self, i, src, dst, target):
        return pltpu.make_async_remote_copy(
            src_ref=src,
            dst_ref=dst,
            send_sem=self.send.at[i],
            recv_sem=self.recv.at[i],
            device_id=target,
            device_id_type=MESH,
        )

    def remote(self, src, dst, target):
        copy = self.make(self.claim(), src, dst, target)
        copy.start()
        self.all.append(copy)
        return copy

    def local(self, src, dst):
        copy = pltpu.make_async_copy(src, dst, self.send.at[self.claim()])
        copy.start()
        return copy

    def wait_sends(self):
        for copy in self.all:
            copy.wait_send()


def greet(targets):
    barrier = pltpu.get_barrier_semaphore()
    for target in targets:
        pl.semaphore_signal(barrier, inc=1, device_id=target, device_id_type=MESH)
    pl.semaphore_wait(barrier, len(targets))


def lanes(start, size):
    return pl.ds(pl.multiple_of(start, 128), size)


def rows_at(start, size):
    return pl.ds(pl.multiple_of(start, 128), size)


def rows16(block):
    return pl.ds(pl.multiple_of(block * 16, 16), 16)


def fill_bias(docs, bias, z):
    ends = []
    total = docs[0, 0]
    for i in range(5):
        ends.append(total)
        if i < 4:
            total = total + docs[0, i + 1]

    def doc(b):
        return sum((b >= e).astype(jnp.int32) for e in ends)

    key = lax.broadcasted_iota(jnp.int32, (BLK, BLK), 0)
    query = lax.broadcasted_iota(jnp.int32, (BLK, BLK), 1)
    for j in range(2):
        qb = 2 * z + j
        for i in range(9):
            kb = 2 * z - 2 * (i // 2) + (1 if i == 8 else i % 2)
            if i < 2 and i == j:
                block = jnp.where(key <= query, 0.0, MASKED)
            elif i == 1 and j == 0:
                block = jnp.full((BLK, BLK), MASKED, F32)
            else:
                same = (kb >= 0) & (doc(kb) == doc(qb))
                block = jnp.full((BLK, BLK), jnp.where(same, 0.0, MASKED), F32)
            bias[pl.ds(i * BLK, BLK), pl.ds(j * BLK, BLK)] = block


def kernel(
    docs, q, g, k, v, xin, key_grad, wv_grad,
    qg, qs, kv, xs, relay, bias, expo, low, top, inv, dv, dk, csend, crecv, dvt, part, ysend, yrecv, zsend, zrecv, kswap,
    send, recv,
):
    x, y, z, h = place()
    ctx = z * 2 + h
    sib = device(x, y, z, 1 - h)
    up = device(x, y, around(z, 1, NZ), h)
    down = device(x, y, around(z, -1, NZ), h)
    across = [device(around(x, dx, NX), y, z, h) for dx in range(1, NX)]
    ahead = device(x, around(y, 1, NY), z, h)
    behind = device(x, around(y, -1, NY), z, h)
    column = [(y * NX + x, around(ctx, o, 16)) for o in range(1, 16)]
    mine = rows_at(h * BLK, BLK)
    copies = Copies(send, recv)

    def x_rows(dx):
        return rows_at(dx * 256 + h * BLK, BLK)

    own_k, own_v = [
        [
            copies.local(src.at[:, lanes((2 * h + a) * HEAD, HEAD)], kv.at[a, j, mine])
            for a in range(2)
        ]
        for j, src in enumerate((k, v))
    ]
    own_q = [
        copies.local(src.at[:, lanes(h * 2048, 2048)], qg.at[j, mine])
        for j, src in enumerate((q, g))
    ]
    greet(column + across + [ahead, behind])

    up_other = device(x, y, around(z, 1, NZ), 1 - h)
    hops, swapped = {}, {}

    def first_hop(j, src):
        for a in range(2):
            own = src.at[:, lanes((2 * h + a) * HEAD, HEAD)]
            other = src.at[:, lanes((2 * (1 - h) + a) * HEAD, HEAD)]
            dst = kv.at[a, j, rows_at(256 + h * BLK, BLK)]
            hops[j, a] = [copies.remote(own, dst, up), copies.remote(other, dst, up_other)]

    def swap_kv(j, src):
        for a in range(2):
            other = src.at[:, lanes((2 * (1 - h) + a) * HEAD, HEAD)]
            swapped[j, a] = copies.remote(other, kv.at[a, j, mine], sib)

    def arrived(j, a):
        for copy in hops[j, a]:
            copy.wait_recv()

    def hop(j, a, step):
        arrived(j, a)
        lo, size = (768 + 128, 128) if step == 4 else ((step - 1) * 256, 256)
        hops[j, a] = [
            copies.remote(kv.at[a, j, pl.ds(lo, size)], kv.at[a, j, pl.ds(step * 256, size)], up)
        ]

    first_hop(0, k)
    swap_kv(0, k)
    exchange = [
        copies.remote(src.at[:, lanes((1 - h) * 2048, 2048)], qg.at[j, mine], sib)
        for j, src in enumerate((q, g))
    ]
    swap_kv(1, v)
    right, left = across[0], across[2]
    spread_x, relays, pieces = {}, {}, []

    def piece(i, dx, c, dst, target):
        to = around(x, dx, NX)
        src = xin.at[:, lanes(c * 1024 + to * 256, 256)]
        pieces.append(lambda: copies.make(i, src, dst, target).start())

    ways = ((0, right), (1, left))
    claimed = [copies.claim() for _ in range(4)]
    for c in range(4):
        for way, target in ways:
            dst = relay.at[way, :, pl.ds(c * 256, 256)]
            piece(claimed[way], 2, way * 4 + c, dst, target)
    for c in range(NY):
        for way, target in ways:
            dx = 1 + 2 * way
            piece(claimed[2 + way], dx, c, xs.at[x_rows(dx), pl.ds(c * 256, 256)], target)
    for way, target in ways:
        dx = 1 + 2 * way
        relays[way] = copies.make(claimed[way], relay.at[way], relay.at[way], target)
        spread_x[dx] = copies.make(claimed[2 + way], xs.at[x_rows(dx)], xs.at[x_rows(dx)], target)
        copies.all += [relays[way], spread_x[dx]]
    second = []

    def feed(n):
        for _ in range(n):
            pieces.pop(0)()

    def relay_on():
        for way, target in ways:
            relays[way].wait_recv()
            second.append(
                copies.remote(
                    relay.at[way], xs.at[x_rows(2), pl.ds(way * 1024, 1024)], target
                )
            )

    own_x = [
        copies.local(
            xin.at[:, lanes(c * 1024 + x * 256, 256)], xs.at[x_rows(0), pl.ds(c * 256, 256)]
        )
        for c in range(NY)
    ]
    passed = {}

    i = copies.claim()
    for c in range(NY):
        copies.make(
            i,
            xin.at[:, lanes(c * 1024 + x * 256, 256)],
            xs.at[x_rows(0), pl.ds(c * 256, 256)],
            sib,
        ).start()
    passed[0] = copies.make(i, xs.at[x_rows(0)], xs.at[x_rows(0)], sib)
    copies.all.append(passed[0])

    def pass_x(dx):
        if dx == 2:
            for copy in second:
                copy.wait_recv()
        else:
            spread_x[dx].wait_recv()
        passed[dx] = copies.remote(xs.at[x_rows(dx)], xs.at[x_rows(dx)], sib)

    contract = (((1,), (1,)), ((), ()))

    def slot_rows(slot):
        return pl.ds(slot * 256, 128 if slot == 4 else 256)

    def heads(one, *args):
        @pl.loop(0, 4)
        def _(i):
            one(*args, 2 * i)
            one(*args, 2 * i + 1)

    def score(a, slot, head):
        rows = slot_rows(slot)
        col = lanes((a * 8 + head) * HEAD, HEAD)
        s = lax.dot_general(kv[a, 0, rows], qg[0, :, col], contract, preferred_element_type=F32)
        t = s * (SCALE * math.log2(math.e)) + bias[rows, :]
        expo[a, rows, lanes(head * 256, 256)] = t
        highest = jnp.max(t.reshape(-1, 8, 256), axis=0)
        if slot > 0:
            highest = jnp.maximum(highest, top[a * 8 + head])
        top[a * 8 + head] = highest

    def weigh(a, head):
        cols = lanes(head * 256, 256)
        m = jnp.max(top[a * 8 + head], axis=0, keepdims=True)
        e = jnp.exp2(expo[a, :, cols] - m)
        expo[a, :, cols] = e
        r = 1.0 / jnp.sum(e, axis=0, keepdims=True)
        inv[a * 8 + head] = r
        low[a, :, cols] = (e * r).astype(BF16)

    def push_back(a, head):
        cols = lanes(head * 256, 256)
        col = lanes((a * 8 + head) * HEAD, HEAD)
        dp = lax.dot_general(kv[a, 1], qg[1, :, col], contract, preferred_element_type=F32)
        p = expo[a, :, cols] * inv[a * 8 + head]
        delta = jnp.sum(p * dp, axis=0, keepdims=True)
        low[a, :, cols] = (p * (dp - delta)).astype(BF16)

    def sum_heads(w, a, slot):
        rows = slot_rows(slot)
        parts[w][a, rows] = jnp.dot(low[a, rows], qs[1 - w, a], preferred_element_type=F32)

    parts = (dv, dk)
    chain = {}

    def chain_step(w, a, step):
        i = 2 * w + a
        if step > 1:
            chain[i].wait_recv()
        if step == 1:
            csend[i, 0, pl.ds(0, 128)] = parts[w][a, pl.ds(1024, 128)].astype(BF16)
            src, dst = csend.at[i, 0, pl.ds(0, 128)], crecv.at[i, 0, pl.ds(0, 128)]
        else:
            here = parts[w][a, pl.ds((5 - step) * 256, 256)]
            if step == 2:
                csend[i, 1, pl.ds(0, 128)] = here[:128].astype(BF16)
                csend[i, 1, pl.ds(128, 128)] = (
                    here[128:] + crecv[i, 0, pl.ds(0, 128)].astype(F32)
                ).astype(BF16)
            else:
                csend[i, step - 1] = (here + crecv[i, step - 2].astype(F32)).astype(BF16)
            src, dst = csend.at[i, step - 1], crecv.at[i, step - 1]
        chain[i] = copies.remote(src, dst, down)

    def chain_end(w, a):
        i = 2 * w + a
        chain[i].wait_recv()
        return parts[w][a, pl.ds(0, 256)] + crecv[i, 3].astype(F32)

    spread = {}

    def spread_dv(a):
        dvt[a, :, 0:256] = chain_end(0, a).T.astype(BF16)
        for dx in (2, 1, 3):
            spread[a, dx] = copies.remote(
                dvt.at[a, :, pl.ds(0, 256)], dvt.at[a, :, pl.ds(dx * 256, 256)], across[dx - 1]
            )

    def wait_x():
        for copy in own_x:
            copy.wait()
        for dx in range(NX):
            passed[dx].wait_recv()

    def product(a):
        for dx in range(1, NX):
            spread[a, dx].wait_recv()

        def chunk(c):
            part[a, c] = jnp.dot(
                dvt[a], xs[:, lanes(c * 256, 256)], preferred_element_type=F32
            )

        chunk(around(y, 4, NY))
        chunk(around(y, 5 - 2 * a, NY))
        ring_step(a, 1)

        @pl.loop(0, 6)
        def _(i):
            chunk(lax.rem(y + (6 - a) + i, NY))

    lengths = {(0, 0): 4, (0, 1): 3, (1, 0): 3, (1, 1): 4}
    ring, direct = {}, {}

    def ring_step(a, step):
        for way, target in ((0, ahead), (1, behind)):
            sign = 1 - 2 * way
            n = lengths[a, way]
            if step > n:
                continue
            here = part[a, around(y, sign * (n - step + 1), NY)]
            if step > 1:
                ring[a, way].wait_recv()
                here = here + yrecv[a, way, step - 2].astype(F32)
            ysend[a, way, step - 1] = here.astype(BF16)
            ring[a, way] = copies.remote(
                ysend.at[a, way, step - 1], yrecv.at[a, way, step - 1], target
            )

    def ring_end(a):
        for way in range(2):
            ring[a, way].wait_recv()
        total = (
            part[a, y]
            + yrecv[a, 0, lengths[a, 0] - 1].astype(F32)
            + yrecv[a, 1, lengths[a, 1] - 1].astype(F32)
        )
        zsend[a] = total.T.astype(BF16)
        direct[a] = [
            copies.remote(zsend.at[a, rows16(around(ctx, o, 16))], zrecv.at[a, o], column[o - 1])
            for o in range(1, 16)
        ]

    feed(4)
    fill_bias(docs, bias, z)
    for copy in own_q:
        copy.wait()
    exchange[0].wait_recv()
    for a in range(2):
        swapped[0, a].wait_recv()
        own_k[a].wait()
        heads(score, a, 0)
    feed(4)
    for slot in range(1, 4):
        for a in range(2):
            hop(0, a, slot + 1)
            heads(score, a, slot)
        if slot == 2:
            first_hop(1, v)
        feed(4)
    relay_on()
    for a in range(2):
        hop(1, a, 2)
    feed(4)
    exchange[1].wait_recv()

    @pl.loop(0, 16)
    def _(i):
        a, head = lax.div(i, 8), lax.rem(i, 8)
        for j in range(2):
            qs[j, a, rows_at(head * 256, 256)] = qg[j, :, lanes(i * HEAD, HEAD)]

    for a in range(2):
        arrived(0, a)
        heads(score, a, 4)
    heads(weigh, 0)
    sum_heads(0, 0, 4)
    chain_step(0, 0, 1)
    for a in range(2):
        hop(1, a, 3)
    for slot in (3, 2, 1, 0):
        sum_heads(0, 0, slot)
    heads(weigh, 1)
    sum_heads(0, 1, 4)
    chain_step(0, 1, 1)
    for a in range(2):
        hop(1, a, 4)
    for slot in (3, 2, 1, 0):
        sum_heads(0, 1, slot)
    chain_step(0, 0, 2)
    pass_x(1)
    pass_x(3)
    chain_step(0, 1, 2)
    chain_step(0, 0, 3)

    for a in range(2):
        arrived(1, a)
        swapped[1, a].wait_recv()
        own_v[a].wait()
    order = [(a, head) for a in range(2) for head in range(8)]

    def some(n):
        for _ in range(n):
            push_back(*order.pop(0))

    some(3)
    chain_step(0, 0, 4)
    chain_step(0, 1, 3)
    some(4)
    spread_dv(0)
    chain_step(0, 1, 4)
    some(1)
    sum_heads(1, 0, 4)
    chain_step(1, 0, 1)
    for slot in (3, 2, 1, 0):
        sum_heads(1, 0, slot)
    pass_x(2)
    some(2)
    spread_dv(1)
    chain_step(1, 0, 2)
    some(2)
    wait_x()
    product(0)
    some(1)
    chain_step(1, 0, 3)
    some(2)
    ring_step(0, 2)
    product(1)
    some(1)
    sum_heads(1, 1, 4)
    chain_step(1, 1, 1)
    chain_step(1, 0, 4)
    ring_step(0, 3)
    ring_step(1, 2)
    for slot in (3, 2, 1, 0):
        sum_heads(1, 1, slot)
    chain_step(1, 1, 2)
    ring_step(0, 4)
    ring_step(1, 3)
    chain_step(1, 1, 3)
    ring_end(0)
    ring_step(1, 4)
    chain_step(1, 1, 4)
    kswap[0, :, 0:HEAD] = (chain_end(1, 0) * SCALE).astype(BF16)
    ring_end(1)
    kswap[0, :, HEAD : 2 * HEAD] = (chain_end(1, 1) * SCALE).astype(BF16)
    swap = copies.remote(
        kswap.at[0, rows_at((1 - h) * BLK, BLK)], kswap.at[1, pl.ds(0, BLK)], sib
    )
    key_grad[:, lanes(h * 256, 256)] = kswap[0, rows_at(h * BLK, BLK), :]
    for a in range(2):
        sums = [zsend[a, rows16(ctx), :].astype(F32), None]
        for o in range(1, 16):
            direct[a][o - 1].wait_recv()
            got = zrecv[a, o].astype(F32)
            sums[o % 2] = got if sums[o % 2] is None else sums[o % 2] + got
        wv_grad[:, lanes(h * 256 + a * HEAD, HEAD)] = sums[0]
        wv_grad[:, lanes((1 - h) * 256 + a * HEAD, HEAD)] = sums[1]
    swap.wait_recv()
    key_grad[:, lanes((1 - h) * 256, 256)] = kswap[1, pl.ds(0, BLK), :]
    copies.wait_sends()


def on_device(queries, keys, values, out_grad, layer_input, doc_blocks):
    anywhere = pl.BlockSpec(memory_space=pl.ANY)
    in_vmem = pl.BlockSpec(memory_space=pltpu.VMEM)
    key_grad, wv_grad = pl.pallas_call(
        kernel,
        out_shape=(
            jax.ShapeDtypeStruct((BLK, 512), BF16),
            jax.ShapeDtypeStruct((16, 512), F32),
        ),
        in_specs=[pl.BlockSpec(memory_space=pltpu.SMEM)] + [anywhere] * 5,
        out_specs=(in_vmem, in_vmem),
        scratch_shapes=[
            pltpu.VMEM((2, 256, 2048), BF16),
            pltpu.VMEM((2, 2, 2048, HEAD), BF16),
            pltpu.VMEM((2, 2, ROWS, HEAD), BF16),
            pltpu.VMEM((NX * 256, 2048), BF16),
            pltpu.VMEM((2, BLK, 1024), BF16),
            pltpu.VMEM((ROWS, 256), F32),
            pltpu.VMEM((2, ROWS, 2048), F32),
            pltpu.VMEM((2, ROWS, 2048), BF16),
            pltpu.VMEM((16, 8, 256), F32),
            pltpu.VMEM((16, 1, 256), F32),
            pltpu.VMEM((2, ROWS, HEAD), F32),
            pltpu.VMEM((2, ROWS, HEAD), F32),
            pltpu.VMEM((4, HOPS, 256, HEAD), BF16),
            pltpu.VMEM((4, HOPS, 256, HEAD), BF16),
            pltpu.VMEM((2, HEAD, NX * 256), BF16),
            pltpu.VMEM((2, NY, HEAD, 256), F32),
            pltpu.VMEM((2, 2, 4, HEAD, 256), BF16),
            pltpu.VMEM((2, 2, 4, HEAD, 256), BF16),
            pltpu.VMEM((2, 256, HEAD), BF16),
            pltpu.VMEM((2, 16, 16, HEAD), BF16),
            pltpu.VMEM((2, 256, 256), BF16),
            pltpu.SemaphoreType.DMA((144,)),
            pltpu.SemaphoreType.DMA((144,)),
        ],
        compiler_params=pltpu.CompilerParams(
            collective_id=0, has_side_effects=True, vmem_limit_bytes=56307712
        ),
        name="grads",
    )(doc_blocks, queries[0], out_grad[0], keys[0], values[0], layer_input[0])
    return (key_grad[None], wv_grad)


def solution(mesh):
    in_specs = (
        P("dp", "context", None),
        P("dp", "context", None),
        P("dp", "context", None),
        P("dp", "context", None),
        P("dp", "context", None),
        P("dp", None),
    )
    out_specs = (P("dp", "context", None), P(("dp", "context"), None))
    return jax.shard_map(
        on_device, mesh=mesh, in_specs=in_specs, out_specs=out_specs, check_vma=False
    )
```

```python
import math

import jax
import jax.numpy as jnp
from jax import lax
from jax.experimental import pallas as pl
from jax.experimental.pallas import tpu as pltpu
from jax.sharding import PartitionSpec as P

HEAD = 128
BLK = 128
NX, NY, NZ = 4, 8, 8
HOPS = 4
ROWS = 1152
MASKED = -1e30
SCALE = 1.0 / math.sqrt(HEAD)
MESH = pl.DeviceIdType.MESH
F32 = jnp.float32
BF16 = jnp.bfloat16


def place():
    d = lax.axis_index("dp")
    c = lax.axis_index("context")
    return lax.rem(d, NX), lax.div(d, NX), lax.div(c, 2), lax.rem(c, 2)


def device(x, y, z, h):
    return (y * NX + x, z * 2 + h)


def around(i, by, n):
    return lax.rem(i + (by + n), n)


class Copies:
    def __init__(self, send, recv):
        self.send, self.recv, self.used, self.all = send, recv, 0, []

    def claim(self):
        self.used += 1
        return self.used - 1

    def make(self, i, src, dst, target):
        return pltpu.make_async_remote_copy(
            src_ref=src,
            dst_ref=dst,
            send_sem=self.send.at[i],
            recv_sem=self.recv.at[i],
            device_id=target,
            device_id_type=MESH,
        )

    def remote(self, src, dst, target):
        copy = self.make(self.claim(), src, dst, target)
        copy.start()
        self.all.append(copy)
        return copy

    def local(self, src, dst):
        copy = pltpu.make_async_copy(src, dst, self.send.at[self.claim()])
        copy.start()
        return copy

    def wait_sends(self):
        for copy in self.all:
            copy.wait_send()


def greet(targets):
    barrier = pltpu.get_barrier_semaphore()
    for target in targets:
        pl.semaphore_signal(barrier, inc=1, device_id=target, device_id_type=MESH)
    pl.semaphore_wait(barrier, len(targets))


def lanes(start, size):
    return pl.ds(pl.multiple_of(start, 128), size)


def rows_at(start, size):
    return pl.ds(pl.multiple_of(start, 128), size)


def rows16(block):
    return pl.ds(pl.multiple_of(block * 16, 16), 16)


def fill_bias(docs, bias, z):
    ends = []
    total = docs[0, 0]
    for i in range(5):
        ends.append(total)
        if i < 4:
            total = total + docs[0, i + 1]

    def doc(b):
        return sum((b >= e).astype(jnp.int32) for e in ends)

    key = lax.broadcasted_iota(jnp.int32, (BLK, BLK), 0)
    query = lax.broadcasted_iota(jnp.int32, (BLK, BLK), 1)
    for j in range(2):
        qb = 2 * z + j
        for i in range(9):
            kb = 2 * z - 2 * (i // 2) + (1 if i == 8 else i % 2)
            if i < 2 and i == j:
                block = jnp.where(key <= query, 0.0, MASKED)
            elif i == 1 and j == 0:
                block = jnp.full((BLK, BLK), MASKED, F32)
            else:
                same = (kb >= 0) & (doc(kb) == doc(qb))
                block = jnp.full((BLK, BLK), jnp.where(same, 0.0, MASKED), F32)
            bias[pl.ds(i * BLK, BLK), pl.ds(j * BLK, BLK)] = block


def kernel(
    docs, q, g, k, v, xin, key_grad, wv_grad,
    qg, qs, kv, xs, relay, bias, expo, low, top, inv, dv, dk, csend, crecv, dvt, part, ysend, yrecv, zsend, zrecv, kswap,
    send, recv,
):
    x, y, z, h = place()
    ctx = z * 2 + h
    sib = device(x, y, z, 1 - h)
    up = device(x, y, around(z, 1, NZ), h)
    down = device(x, y, around(z, -1, NZ), h)
    across = [device(around(x, dx, NX), y, z, h) for dx in range(1, NX)]
    ahead = device(x, around(y, 1, NY), z, h)
    behind = device(x, around(y, -1, NY), z, h)
    column = [(y * NX + x, around(ctx, o, 16)) for o in range(1, 16)]
    mine = rows_at(h * BLK, BLK)
    copies = Copies(send, recv)

    def x_rows(dx):
        return rows_at(dx * 256 + h * BLK, BLK)

    own_k, own_v = [
        [
            copies.local(src.at[:, lanes((2 * h + a) * HEAD, HEAD)], kv.at[a, j, mine])
            for a in range(2)
        ]
        for j, src in enumerate((k, v))
    ]
    own_q = [
        copies.local(src.at[:, lanes(h * 2048, 2048)], qg.at[j, mine])
        for j, src in enumerate((q, g))
    ]
    greet(column + across + [ahead, behind])

    up_other = device(x, y, around(z, 1, NZ), 1 - h)
    hops, swapped = {}, {}

    def first_hop(j, src):
        for a in range(2):
            own = src.at[:, lanes((2 * h + a) * HEAD, HEAD)]
            other = src.at[:, lanes((2 * (1 - h) + a) * HEAD, HEAD)]
            dst = kv.at[a, j, rows_at(256 + h * BLK, BLK)]
            hops[j, a] = [copies.remote(own, dst, up), copies.remote(other, dst, up_other)]

    def swap_kv(j, src):
        for a in range(2):
            other = src.at[:, lanes((2 * (1 - h) + a) * HEAD, HEAD)]
            swapped[j, a] = copies.remote(other, kv.at[a, j, mine], sib)

    def arrived(j, a):
        for copy in hops[j, a]:
            copy.wait_recv()

    def hop(j, a, step):
        arrived(j, a)
        lo, size = (768 + 128, 128) if step == 4 else ((step - 1) * 256, 256)
        hops[j, a] = [
            copies.remote(kv.at[a, j, pl.ds(lo, size)], kv.at[a, j, pl.ds(step * 256, size)], up)
        ]

    first_hop(0, k)
    swap_kv(0, k)
    exchange = [
        copies.remote(src.at[:, lanes((1 - h) * 2048, 2048)], qg.at[j, mine], sib)
        for j, src in enumerate((q, g))
    ]
    swap_kv(1, v)
    spread_x, relays, pieces = [], [], []

    def piece(i, dx, c, dst, target):
        to = around(x, dx, NX)
        src = xin.at[:, lanes(c * 1024 + to * 256, 256)]
        pieces.append(lambda: copies.make(i, src, dst, target).start())

    ways = []
    for way in (h, 1 - h):
        dx = 1 + 2 * way
        ways.append((way, dx, device(around(x, dx, NX), y, z, h)))
    claimed = [copies.claim() for _ in range(4)]
    for c in range(4):
        for i, (way, dx, target) in enumerate(ways):
            piece(claimed[i], 2, way * 4 + c, relay.at[way, :, pl.ds(c * 256, 256)], target)
    for c in range(NY):
        for i, (way, dx, target) in enumerate(ways):
            piece(claimed[2 + i], dx, c, xs.at[x_rows(dx), pl.ds(c * 256, 256)], target)
    for i, (way, dx, target) in enumerate(ways):
        relays.append(copies.make(claimed[i], relay.at[way], relay.at[way], target))
        spread_x.append(copies.make(claimed[2 + i], xs.at[x_rows(dx)], xs.at[x_rows(dx)], target))
    copies.all += relays + spread_x
    second = []

    def feed(n):
        for _ in range(n):
            pieces.pop(0)()

    def relay_on():
        for i, (way, dx, target) in enumerate(ways):
            relays[i].wait_recv()
            cols = lanes(way * 1024, 1024)
            second.append(copies.remote(relay.at[way], xs.at[x_rows(2), cols], target))

    own_x = [
        copies.local(
            xin.at[:, lanes(c * 1024 + x * 256, 256)], xs.at[x_rows(0), pl.ds(c * 256, 256)]
        )
        for c in range(NY)
    ]
    passed = {}

    def pass_x():
        for copy in own_x:
            copy.wait()
        sources = [0, 2]
        for i, (way, dx, target) in enumerate(ways):
            spread_x[i].wait_recv()
            sources.append(dx)
        for copy in second:
            copy.wait_recv()
        for n, dx in enumerate(sources):
            passed[n] = copies.remote(xs.at[x_rows(dx)], xs.at[x_rows(dx)], sib)

    contract = (((1,), (1,)), ((), ()))

    def slot_rows(slot):
        return pl.ds(slot * 256, 128 if slot == 4 else 256)

    def heads(one, *args):
        @pl.loop(0, 4)
        def _(i):
            one(*args, 2 * i)
            one(*args, 2 * i + 1)

    def score(a, slot, head):
        rows = slot_rows(slot)
        col = lanes((a * 8 + head) * HEAD, HEAD)
        s = lax.dot_general(kv[a, 0, rows], qg[0, :, col], contract, preferred_element_type=F32)
        t = s * (SCALE * math.log2(math.e)) + bias[rows, :]
        expo[a, rows, lanes(head * 256, 256)] = t
        highest = jnp.max(t.reshape(-1, 8, 256), axis=0)
        if slot > 0:
            highest = jnp.maximum(highest, top[a * 8 + head])
        top[a * 8 + head] = highest

    def weigh(a, head):
        cols = lanes(head * 256, 256)
        m = jnp.max(top[a * 8 + head], axis=0, keepdims=True)
        e = jnp.exp2(expo[a, :, cols] - m)
        expo[a, :, cols] = e
        r = 1.0 / jnp.sum(e, axis=0, keepdims=True)
        inv[a * 8 + head] = r
        low[a, :, cols] = (e * r).astype(BF16)

    def push_back(a, head):
        cols = lanes(head * 256, 256)
        col = lanes((a * 8 + head) * HEAD, HEAD)
        dp = lax.dot_general(kv[a, 1], qg[1, :, col], contract, preferred_element_type=F32)
        p = expo[a, :, cols] * inv[a * 8 + head]
        delta = jnp.sum(p * dp, axis=0, keepdims=True)
        low[a, :, cols] = (p * (dp - delta)).astype(BF16)

    def sum_heads(w, a, slot):
        rows = slot_rows(slot)
        parts[w][a, rows] = jnp.dot(low[a, rows], qs[1 - w, a], preferred_element_type=F32)

    parts = (dv, dk)
    chain = {}

    def chain_step(w, a, step):
        i = 2 * w + a
        if step > 1:
            chain[i].wait_recv()
        if step == 1:
            csend[i, 0, pl.ds(0, 128)] = parts[w][a, pl.ds(1024, 128)].astype(BF16)
            src, dst = csend.at[i, 0, pl.ds(0, 128)], crecv.at[i, 0, pl.ds(0, 128)]
        else:
            here = parts[w][a, pl.ds((5 - step) * 256, 256)]
            if step == 2:
                csend[i, 1, pl.ds(0, 128)] = here[:128].astype(BF16)
                csend[i, 1, pl.ds(128, 128)] = (
                    here[128:] + crecv[i, 0, pl.ds(0, 128)].astype(F32)
                ).astype(BF16)
            else:
                csend[i, step - 1] = (here + crecv[i, step - 2].astype(F32)).astype(BF16)
            src, dst = csend.at[i, step - 1], crecv.at[i, step - 1]
        chain[i] = copies.remote(src, dst, down)

    def chain_end(w, a):
        i = 2 * w + a
        chain[i].wait_recv()
        return parts[w][a, pl.ds(0, 256)] + crecv[i, 3].astype(F32)

    spread = {}

    def spread_dv(a):
        dvt[a, :, 0:256] = chain_end(0, a).T.astype(BF16)
        for dx in (2, 1, 3):
            spread[a, dx] = copies.remote(
                dvt.at[a, :, pl.ds(0, 256)], dvt.at[a, :, pl.ds(dx * 256, 256)], across[dx - 1]
            )

    def wait_x():
        for n in range(NX):
            passed[n].wait_recv()

    def product(a):
        for dx in range(1, NX):
            spread[a, dx].wait_recv()

        def chunk(c):
            part[a, c] = jnp.dot(
                dvt[a], xs[:, lanes(c * 256, 256)], preferred_element_type=F32
            )

        near = 3 + 2 * (1 - h)
        chunk(around(y, 4, NY))
        chunk(around(y, near, NY))
        ring_step(a, 1)

        @pl.loop(0, 6)
        def _(i):
            chunk(lax.rem(y + near + 1 + h + i, NY))

    lengths = {(0, 0): 4, (0, 1): 3, (1, 0): 4, (1, 1): 3}
    ring, direct = {}, {}
    sides = []
    for way in (h, 1 - h):
        sign = 1 - 2 * way
        sides.append((sign, device(x, around(y, sign, NY), z, h)))

    def ring_step(a, step):
        for s, (sign, target) in enumerate(sides):
            n = lengths[a, s]
            if step > n:
                continue
            here = part[a, around(y, sign * (n - step + 1), NY)]
            if step > 1:
                ring[a, s].wait_recv()
                here = here + yrecv[a, s, step - 2].astype(F32)
            ysend[a, s, step - 1] = here.astype(BF16)
            ring[a, s] = copies.remote(
                ysend.at[a, s, step - 1], yrecv.at[a, s, step - 1], target
            )

    def ring_end(a):
        for s in range(2):
            ring[a, s].wait_recv()
        total = (
            part[a, y]
            + yrecv[a, 0, lengths[a, 0] - 1].astype(F32)
            + yrecv[a, 1, lengths[a, 1] - 1].astype(F32)
        )
        zsend[a] = total.T.astype(BF16)
        direct[a] = [
            copies.remote(zsend.at[a, rows16(around(ctx, o, 16))], zrecv.at[a, o], column[o - 1])
            for o in range(1, 16)
        ]

    feed(6)
    fill_bias(docs, bias, z)
    for copy in own_q:
        copy.wait()
    exchange[0].wait_recv()
    for a in range(2):
        swapped[0, a].wait_recv()
        own_k[a].wait()
        heads(score, a, 0)
    feed(6)
    for slot in range(1, 4):
        for a in range(2):
            hop(0, a, slot + 1)
            heads(score, a, slot)
        if slot == 2:
            first_hop(1, v)
        feed(4)
    relay_on()
    for a in range(2):
        hop(1, a, 2)
    exchange[1].wait_recv()

    @pl.loop(0, 16)
    def _(i):
        a, head = lax.div(i, 8), lax.rem(i, 8)
        for j in range(2):
            qs[j, a, rows_at(head * 256, 256)] = qg[j, :, lanes(i * HEAD, HEAD)]

    for a in range(2):
        arrived(0, a)
        heads(score, a, 4)
    heads(weigh, 0)
    sum_heads(0, 0, 4)
    chain_step(0, 0, 1)
    for a in range(2):
        hop(1, a, 3)
    for slot in (3, 2, 1, 0):
        sum_heads(0, 0, slot)
    heads(weigh, 1)
    sum_heads(0, 1, 4)
    chain_step(0, 1, 1)
    for a in range(2):
        hop(1, a, 4)
    for slot in (3, 2, 1, 0):
        sum_heads(0, 1, slot)
    chain_step(0, 0, 2)
    chain_step(0, 1, 2)
    chain_step(0, 0, 3)

    for a in range(2):
        arrived(1, a)
        swapped[1, a].wait_recv()
        own_v[a].wait()
    order = [(a, head) for a in range(2) for head in range(8)]

    def some(n):
        for _ in range(n):
            push_back(*order.pop(0))

    some(3)
    chain_step(0, 0, 4)
    chain_step(0, 1, 3)
    some(4)
    spread_dv(0)
    chain_step(0, 1, 4)
    some(1)
    sum_heads(1, 0, 4)
    chain_step(1, 0, 1)
    for slot in (3, 2, 1, 0):
        sum_heads(1, 0, slot)
    some(2)
    spread_dv(1)
    chain_step(1, 0, 2)
    some(2)
    pass_x()
    some(1)
    chain_step(1, 0, 3)
    some(1)
    wait_x()
    product(0)
    some(1)
    ring_step(0, 2)
    product(1)
    some(1)
    sum_heads(1, 1, 4)
    chain_step(1, 1, 1)
    chain_step(1, 0, 4)
    ring_step(0, 3)
    ring_step(1, 2)
    for slot in (3, 2, 1, 0):
        sum_heads(1, 1, slot)
    chain_step(1, 1, 2)
    ring_step(0, 4)
    ring_step(1, 3)
    chain_step(1, 1, 3)
    ring_end(0)
    ring_step(1, 4)
    chain_step(1, 1, 4)
    kswap[0, :, 0:HEAD] = (chain_end(1, 0) * SCALE).astype(BF16)
    ring_end(1)
    kswap[0, :, HEAD : 2 * HEAD] = (chain_end(1, 1) * SCALE).astype(BF16)
    swap = copies.remote(
        kswap.at[0, rows_at((1 - h) * BLK, BLK)], kswap.at[1, pl.ds(0, BLK)], sib
    )
    key_grad[:, lanes(h * 256, 256)] = kswap[0, rows_at(h * BLK, BLK), :]
    for a in range(2):
        sums = [zsend[a, rows16(ctx), :].astype(F32), None]
        for o in range(1, 16):
            direct[a][o - 1].wait_recv()
            got = zrecv[a, o].astype(F32)
            sums[o % 2] = got if sums[o % 2] is None else sums[o % 2] + got
        wv_grad[:, lanes(h * 256 + a * HEAD, HEAD)] = sums[0]
        wv_grad[:, lanes((1 - h) * 256 + a * HEAD, HEAD)] = sums[1]
    swap.wait_recv()
    key_grad[:, lanes((1 - h) * 256, 256)] = kswap[1, pl.ds(0, BLK), :]
    copies.wait_sends()


def on_device(queries, keys, values, out_grad, layer_input, doc_blocks):
    anywhere = pl.BlockSpec(memory_space=pl.ANY)
    in_vmem = pl.BlockSpec(memory_space=pltpu.VMEM)
    key_grad, wv_grad = pl.pallas_call(
        kernel,
        out_shape=(
            jax.ShapeDtypeStruct((BLK, 512), BF16),
            jax.ShapeDtypeStruct((16, 512), F32),
        ),
        in_specs=[pl.BlockSpec(memory_space=pltpu.SMEM)] + [anywhere] * 5,
        out_specs=(in_vmem, in_vmem),
        scratch_shapes=[
            pltpu.VMEM((2, 256, 2048), BF16),
            pltpu.VMEM((2, 2, 2048, HEAD), BF16),
            pltpu.VMEM((2, 2, ROWS, HEAD), BF16),
            pltpu.VMEM((NX * 256, 2048), BF16),
            pltpu.VMEM((2, BLK, 1024), BF16),
            pltpu.VMEM((ROWS, 256), F32),
            pltpu.VMEM((2, ROWS, 2048), F32),
            pltpu.VMEM((2, ROWS, 2048), BF16),
            pltpu.VMEM((16, 8, 256), F32),
            pltpu.VMEM((16, 1, 256), F32),
            pltpu.VMEM((2, ROWS, HEAD), F32),
            pltpu.VMEM((2, ROWS, HEAD), F32),
            pltpu.VMEM((4, HOPS, 256, HEAD), BF16),
            pltpu.VMEM((4, HOPS, 256, HEAD), BF16),
            pltpu.VMEM((2, HEAD, NX * 256), BF16),
            pltpu.VMEM((2, NY, HEAD, 256), F32),
            pltpu.VMEM((2, 2, 4, HEAD, 256), BF16),
            pltpu.VMEM((2, 2, 4, HEAD, 256), BF16),
            pltpu.VMEM((2, 256, HEAD), BF16),
            pltpu.VMEM((2, 16, 16, HEAD), BF16),
            pltpu.VMEM((2, 256, 256), BF16),
            pltpu.SemaphoreType.DMA((144,)),
            pltpu.SemaphoreType.DMA((144,)),
        ],
        compiler_params=pltpu.CompilerParams(
            collective_id=0, has_side_effects=True, vmem_limit_bytes=56307712
        ),
        name="grads",
    )(doc_blocks, queries[0], out_grad[0], keys[0], values[0], layer_input[0])
    return (key_grad[None], wv_grad)


def solution(mesh):
    in_specs = (
        P("dp", "context", None),
        P("dp", "context", None),
        P("dp", "context", None),
        P("dp", "context", None),
        P("dp", "context", None),
        P("dp", None),
    )
    out_specs = (P("dp", "context", None), P(("dp", "context"), None))
    return jax.shard_map(
        on_device, mesh=mesh, in_specs=in_specs, out_specs=out_specs, check_vma=False
    )
```

```python
import math

import jax
import jax.numpy as jnp
from jax import lax
from jax.experimental import pallas as pl
from jax.experimental.pallas import tpu as pltpu
from jax.sharding import PartitionSpec as P

HEAD = 128
BLK = 128
NX, NY, NZ = 4, 8, 8
HOPS = 4
ROWS = 1152
MASKED = -1e30
SCALE = 1.0 / math.sqrt(HEAD)
MESH = pl.DeviceIdType.MESH
F32 = jnp.float32
BF16 = jnp.bfloat16


def place():
    d = lax.axis_index("dp")
    c = lax.axis_index("context")
    return lax.rem(d, NX), lax.div(d, NX), lax.div(c, 2), lax.rem(c, 2)


def device(x, y, z, h):
    return (y * NX + x, z * 2 + h)


def around(i, by, n):
    return lax.rem(i + (by + n), n)


class Copies:
    def __init__(self, send, recv):
        self.send, self.recv, self.used, self.all = send, recv, 0, []

    def claim(self):
        self.used += 1
        return self.used - 1

    def make(self, i, src, dst, target):
        return pltpu.make_async_remote_copy(
            src_ref=src,
            dst_ref=dst,
            send_sem=self.send.at[i],
            recv_sem=self.recv.at[i],
            device_id=target,
            device_id_type=MESH,
        )

    def remote(self, src, dst, target):
        copy = self.make(self.claim(), src, dst, target)
        copy.start()
        self.all.append(copy)
        return copy

    def local(self, src, dst):
        copy = pltpu.make_async_copy(src, dst, self.send.at[self.claim()])
        copy.start()
        return copy

    def wait_sends(self, leave=0):
        while len(self.all) > leave:
            self.all.pop(0).wait_send()


def greet(targets):
    barrier = pltpu.get_barrier_semaphore()
    for target in targets:
        pl.semaphore_signal(barrier, inc=1, device_id=target, device_id_type=MESH)
    pl.semaphore_wait(barrier, len(targets))


def lanes(start, size):
    return pl.ds(pl.multiple_of(start, 128), size)


def rows_at(start, size):
    return pl.ds(pl.multiple_of(start, 128), size)


def rows16(block):
    return pl.ds(pl.multiple_of(block * 16, 16), 16)


def fill_bias(docs, bias, z):
    ends = []
    total = docs[0, 0]
    for i in range(5):
        ends.append(total)
        if i < 4:
            total = total + docs[0, i + 1]

    def doc(b):
        return sum((b >= e).astype(jnp.int32) for e in ends)

    key = lax.broadcasted_iota(jnp.int32, (BLK, BLK), 0)
    query = lax.broadcasted_iota(jnp.int32, (BLK, BLK), 1)
    for j in range(2):
        qb = 2 * z + j
        for i in range(9):
            kb = 2 * z - 2 * (i // 2) + (1 if i == 8 else i % 2)
            if i < 2 and i == j:
                block = jnp.where(key <= query, 0.0, MASKED)
            elif i == 1 and j == 0:
                block = jnp.full((BLK, BLK), MASKED, F32)
            else:
                same = (kb >= 0) & (doc(kb) == doc(qb))
                block = jnp.full((BLK, BLK), jnp.where(same, 0.0, MASKED), F32)
            bias[pl.ds(i * BLK, BLK), pl.ds(j * BLK, BLK)] = block


def kernel(
    docs, q, g, k, v, xin, key_grad, wv_grad,
    qg, qs, kv, xs, relay, bias, expo, low, top, inv, dv, dk, csend, crecv, dvt, part, ysend, yrecv, zsend, zrecv, kswap,
    send, recv,
):
    x, y, z, h = place()
    ctx = z * 2 + h
    sib = device(x, y, z, 1 - h)
    up = device(x, y, around(z, 1, NZ), h)
    down = device(x, y, around(z, -1, NZ), h)
    across = [device(around(x, dx, NX), y, z, h) for dx in range(1, NX)]
    ahead = device(x, around(y, 1, NY), z, h)
    behind = device(x, around(y, -1, NY), z, h)
    column = [(y * NX + x, around(ctx, o, 16)) for o in range(1, 16)]
    mine = rows_at(h * BLK, BLK)
    copies = Copies(send, recv)

    def x_rows(dx):
        return rows_at(dx * 256 + h * BLK, BLK)

    own_k, own_v = [
        [
            copies.local(src.at[:, lanes((2 * h + a) * HEAD, HEAD)], kv.at[a, j, mine])
            for a in range(2)
        ]
        for j, src in enumerate((k, v))
    ]
    own_q = [
        copies.local(src.at[:, lanes(h * 2048, 2048)], qg.at[j, mine])
        for j, src in enumerate((q, g))
    ]
    greet(column + across + [ahead, behind])

    up_other = device(x, y, around(z, 1, NZ), 1 - h)
    hops, swapped = {}, {}

    def first_hop(j, src):
        for a in range(2):
            own = src.at[:, lanes((2 * h + a) * HEAD, HEAD)]
            other = src.at[:, lanes((2 * (1 - h) + a) * HEAD, HEAD)]
            dst = kv.at[a, j, rows_at(256 + h * BLK, BLK)]
            hops[j, a] = [copies.remote(own, dst, up), copies.remote(other, dst, up_other)]

    def swap_kv(j, src):
        for a in range(2):
            other = src.at[:, lanes((2 * (1 - h) + a) * HEAD, HEAD)]
            swapped[j, a] = copies.remote(other, kv.at[a, j, mine], sib)

    def arrived(j, a):
        for copy in hops[j, a]:
            copy.wait_recv()

    def hop(j, a, step):
        arrived(j, a)
        lo, size = (768 + 128, 128) if step == 4 else ((step - 1) * 256, 256)
        hops[j, a] = [
            copies.remote(kv.at[a, j, pl.ds(lo, size)], kv.at[a, j, pl.ds(step * 256, size)], up)
        ]

    first_hop(0, k)
    swap_kv(0, k)
    exchange = [
        copies.remote(src.at[:, lanes((1 - h) * 2048, 2048)], qg.at[j, mine], sib)
        for j, src in enumerate((q, g))
    ]

    spread_x, relays, pieces = [], [], []

    def piece(i, dx, c, dst, target):
        to = around(x, dx, NX)
        src = xin.at[:, lanes(c * 1024 + to * 256, 256)]
        pieces.append(lambda: copies.make(i, src, dst, target).start())

    ways = []
    for way in (h, 1 - h):
        dx = 1 + 2 * way
        ways.append((way, dx, device(around(x, dx, NX), y, z, h)))
    claimed = [copies.claim() for _ in range(4)]
    for c in range(4):
        for i, (way, dx, target) in enumerate(ways):
            piece(claimed[i], 2, way * 4 + c, relay.at[way, :, pl.ds(c * 256, 256)], target)
    for c in range(NY):
        for i, (way, dx, target) in enumerate(ways):
            piece(claimed[2 + i], dx, c, xs.at[x_rows(dx), pl.ds(c * 256, 256)], target)
    for i, (way, dx, target) in enumerate(ways):
        relays.append(copies.make(claimed[i], relay.at[way], relay.at[way], target))
        spread_x.append(copies.make(claimed[2 + i], xs.at[x_rows(dx)], xs.at[x_rows(dx)], target))
    copies.all += relays + spread_x
    second = []

    def feed(n):
        for _ in range(n):
            pieces.pop(0)()

    def relay_on():
        for i, (way, dx, target) in enumerate(ways):
            relays[i].wait_recv()
            cols = lanes(way * 1024, 1024)
            second.append(copies.remote(relay.at[way], xs.at[x_rows(2), cols], target))

    own_x = []

    def take_own_x():
        for c in range(NY):
            own_x.append(
                copies.local(
                    xin.at[:, lanes(c * 1024 + x * 256, 256)],
                    xs.at[x_rows(0), pl.ds(c * 256, 256)],
                )
            )

    passed = {}

    def pass_on(dx):
        passed[len(passed)] = copies.remote(xs.at[x_rows(dx)], xs.at[x_rows(dx)], sib)

    def pass_own():
        for copy in own_x:
            copy.wait()
        pass_on(0)

    def pass_near():
        for i, (way, dx, target) in enumerate(ways):
            spread_x[i].wait_recv()
            pass_on(dx)

    def pass_far():
        for copy in second:
            copy.wait_recv()
        pass_on(2)

    contract = (((1,), (1,)), ((), ()))

    def slot_rows(slot):
        return pl.ds(slot * 256, 128 if slot == 4 else 256)

    def heads(one, *args):
        @pl.loop(0, 4)
        def _(i):
            one(*args, 2 * i)
            one(*args, 2 * i + 1)

    def score(a, slot, head):
        rows = slot_rows(slot)
        col = lanes((a * 8 + head) * HEAD, HEAD)
        s = lax.dot_general(kv[a, 0, rows], qg[0, :, col], contract, preferred_element_type=F32)
        t = s * (SCALE * math.log2(math.e)) + bias[rows, :]
        expo[a, rows, lanes(head * 256, 256)] = t
        highest = jnp.max(t.reshape(-1, 8, 256), axis=0)
        if slot > 0:
            highest = jnp.maximum(highest, top[a * 8 + head])
        top[a * 8 + head] = highest

    def weigh(a, head):
        cols = lanes(head * 256, 256)
        m = jnp.max(top[a * 8 + head], axis=0, keepdims=True)
        e = jnp.exp2(expo[a, :, cols] - m)
        expo[a, :, cols] = e
        r = 1.0 / jnp.sum(e, axis=0, keepdims=True)
        inv[a * 8 + head] = r
        low[a, :, cols] = (e * r).astype(BF16)

    def push_back(a, head):
        cols = lanes(head * 256, 256)
        col = lanes((a * 8 + head) * HEAD, HEAD)
        dp = lax.dot_general(kv[a, 1], qg[1, :, col], contract, preferred_element_type=F32)
        p = expo[a, :, cols] * inv[a * 8 + head]
        delta = jnp.sum(p * dp, axis=0, keepdims=True)
        low[a, :, cols] = (p * (dp - delta)).astype(BF16)

    def sum_heads(w, a, slot):
        rows = slot_rows(slot)
        parts[w][a, rows] = jnp.dot(low[a, rows], qs[1 - w, a], preferred_element_type=F32)

    parts = (dv, dk)
    chain = {}

    def chain_step(w, a, step):
        i = 2 * w + a
        if step > 1:
            chain[i].wait_recv()
        if step == 1:
            csend[i, 0, pl.ds(0, 128)] = parts[w][a, pl.ds(1024, 128)].astype(BF16)
            src, dst = csend.at[i, 0, pl.ds(0, 128)], crecv.at[i, 0, pl.ds(0, 128)]
        else:
            here = parts[w][a, pl.ds((5 - step) * 256, 256)]
            if step == 2:
                csend[i, 1, pl.ds(0, 128)] = here[:128].astype(BF16)
                csend[i, 1, pl.ds(128, 128)] = (
                    here[128:] + crecv[i, 0, pl.ds(0, 128)].astype(F32)
                ).astype(BF16)
            else:
                csend[i, step - 1] = (here + crecv[i, step - 2].astype(F32)).astype(BF16)
            src, dst = csend.at[i, step - 1], crecv.at[i, step - 1]
        chain[i] = copies.remote(src, dst, down)

    def chain_end(w, a):
        i = 2 * w + a
        chain[i].wait_recv()
        return parts[w][a, pl.ds(0, 256)] + crecv[i, 3].astype(F32)

    spread = {}

    def spread_dv(a):
        dvt[a, :, 0:256] = chain_end(0, a).T.astype(BF16)
        for dx in (2, 1, 3):
            spread[a, dx] = copies.remote(
                dvt.at[a, :, pl.ds(0, 256)], dvt.at[a, :, pl.ds(dx * 256, 256)], across[dx - 1]
            )

    def wait_x():
        for n in range(NX):
            passed[n].wait_recv()

    def product(a):
        for dx in range(1, NX):
            spread[a, dx].wait_recv()

        def chunk(c):
            part[a, c] = jnp.dot(
                dvt[a], xs[:, lanes(c * 256, 256)], preferred_element_type=F32
            )

        near = 3 + 2 * (1 - h)
        chunk(around(y, 4, NY))
        chunk(around(y, near, NY))
        ring_step(a, 1)

        @pl.loop(0, 6)
        def _(i):
            chunk(lax.rem(y + near + 1 + h + i, NY))

    lengths = {(0, 0): 4, (0, 1): 3, (1, 0): 4, (1, 1): 3}
    ring, direct = {}, {}
    sides = []
    for way in (h, 1 - h):
        sign = 1 - 2 * way
        sides.append((sign, device(x, around(y, sign, NY), z, h)))

    def ring_step(a, step):
        for s, (sign, target) in enumerate(sides):
            n = lengths[a, s]
            if step > n:
                continue
            here = part[a, around(y, sign * (n - step + 1), NY)]
            if step > 1:
                ring[a, s].wait_recv()
                here = here + yrecv[a, s, step - 2].astype(F32)
            ysend[a, s, step - 1] = here.astype(BF16)
            ring[a, s] = copies.remote(
                ysend.at[a, s, step - 1], yrecv.at[a, s, step - 1], target
            )

    def ring_end(a):
        for s in range(2):
            ring[a, s].wait_recv()
        total = (
            part[a, y]
            + yrecv[a, 0, lengths[a, 0] - 1].astype(F32)
            + yrecv[a, 1, lengths[a, 1] - 1].astype(F32)
        )
        zsend[a] = total.T.astype(BF16)
        direct[a] = [
            copies.remote(zsend.at[a, rows16(around(ctx, o, 16))], zrecv.at[a, o], column[o - 1])
            for o in range(1, 16)
        ]

    fill_bias(docs, bias, z)
    feed(6)
    for copy in own_q:
        copy.wait()
    exchange[0].wait_recv()
    for slot in range(4):
        for a in range(2):
            if slot < 3:
                hop(0, a, slot + 2)
            if slot == 0:
                swapped[0, a].wait_recv()
                own_k[a].wait()
            heads(score, a, slot)
        if slot == 0:
            swap_kv(1, v)
        if slot == 1:
            first_hop(1, v)
        if slot < 3:
            feed(6)
    take_own_x()
    for a in range(2):
        hop(1, a, 2)
    relay_on()
    exchange[1].wait_recv()

    @pl.loop(0, 16)
    def _(i):
        a, head = lax.div(i, 8), lax.rem(i, 8)
        for j in range(2):
            qs[j, a, rows_at(head * 256, 256)] = qg[j, :, lanes(i * HEAD, HEAD)]

    for a in range(2):
        arrived(0, a)
        heads(score, a, 4)
    heads(weigh, 0)
    sum_heads(0, 0, 4)
    chain_step(0, 0, 1)
    for a in range(2):
        hop(1, a, 3)
    for slot in (3, 2, 1, 0):
        sum_heads(0, 0, slot)
    heads(weigh, 1)
    sum_heads(0, 1, 4)
    chain_step(0, 1, 1)
    for a in range(2):
        hop(1, a, 4)
    for slot in (3, 2, 1, 0):
        sum_heads(0, 1, slot)
    chain_step(0, 0, 2)
    pass_own()
    pass_near()
    chain_step(0, 1, 2)
    chain_step(0, 0, 3)

    for a in range(2):
        arrived(1, a)
        swapped[1, a].wait_recv()
        own_v[a].wait()
    done = [0]

    def some(n):
        first = done[0]
        done[0] += n
        if n == 1:
            push_back(first // 8, first % 8)
        else:

            @pl.loop(first % 8, first % 8 + n)
            def _(head):
                push_back(first // 8, head)

    some(3)
    chain_step(0, 0, 4)
    chain_step(0, 1, 3)
    some(4)
    spread_dv(0)
    chain_step(0, 1, 4)
    some(1)
    sum_heads(1, 0, 4)
    chain_step(1, 0, 1)
    for slot in (3, 2, 1, 0):
        sum_heads(1, 0, slot)
    pass_far()
    some(2)
    spread_dv(1)
    chain_step(1, 0, 2)
    some(2)
    copies.wait_sends(8)
    wait_x()
    product(0)
    chain_step(1, 0, 3)
    some(2)
    ring_step(0, 2)
    product(1)
    some(2)
    ring_step(0, 3)
    ring_step(1, 2)
    sum_heads(1, 1, 4)
    chain_step(1, 1, 1)
    chain_step(1, 0, 4)
    for slot in (3, 2, 1, 0):
        sum_heads(1, 1, slot)
    ring_step(0, 4)
    ring_step(1, 3)
    chain_step(1, 1, 2)
    copies.wait_sends(8)
    ring_step(1, 4)
    ring_end(0)
    chain_step(1, 1, 3)
    ring_end(1)
    chain_step(1, 1, 4)
    copies.wait_sends(32)
    kswap[0, :, 0:HEAD] = (chain_end(1, 0) * SCALE).astype(BF16)
    kswap[0, :, HEAD : 2 * HEAD] = (chain_end(1, 1) * SCALE).astype(BF16)
    swap = copies.remote(
        kswap.at[0, rows_at((1 - h) * BLK, BLK)], kswap.at[1, pl.ds(0, BLK)], sib
    )
    key_grad[:, lanes(h * 256, 256)] = kswap[0, rows_at(h * BLK, BLK), :]
    for a in range(2):
        sums = [zsend[a, rows16(ctx), :].astype(F32), None]
        for o in range(1, 16):
            direct[a][o - 1].wait_recv()
            got = zrecv[a, o].astype(F32)
            sums[o % 2] = got if sums[o % 2] is None else sums[o % 2] + got
        wv_grad[:, lanes(h * 256 + a * HEAD, HEAD)] = sums[0]
        wv_grad[:, lanes((1 - h) * 256 + a * HEAD, HEAD)] = sums[1]
    swap.wait_recv()
    key_grad[:, lanes((1 - h) * 256, 256)] = kswap[1, pl.ds(0, BLK), :]
    copies.wait_sends()


def on_device(queries, keys, values, out_grad, layer_input, doc_blocks):
    anywhere = pl.BlockSpec(memory_space=pl.ANY)
    in_vmem = pl.BlockSpec(memory_space=pltpu.VMEM)
    key_grad, wv_grad = pl.pallas_call(
        kernel,
        out_shape=(
            jax.ShapeDtypeStruct((BLK, 512), BF16),
            jax.ShapeDtypeStruct((16, 512), F32),
        ),
        in_specs=[pl.BlockSpec(memory_space=pltpu.SMEM)] + [anywhere] * 5,
        out_specs=(in_vmem, in_vmem),
        scratch_shapes=[
            pltpu.VMEM((2, 256, 2048), BF16),
            pltpu.VMEM((2, 2, 2048, HEAD), BF16),
            pltpu.VMEM((2, 2, ROWS, HEAD), BF16),
            pltpu.VMEM((NX * 256, 2048), BF16),
            pltpu.VMEM((2, BLK, 1024), BF16),
            pltpu.VMEM((ROWS, 256), F32),
            pltpu.VMEM((2, ROWS, 2048), F32),
            pltpu.VMEM((2, ROWS, 2048), BF16),
            pltpu.VMEM((16, 8, 256), F32),
            pltpu.VMEM((16, 1, 256), F32),
            pltpu.VMEM((2, ROWS, HEAD), F32),
            pltpu.VMEM((2, ROWS, HEAD), F32),
            pltpu.VMEM((4, HOPS, 256, HEAD), BF16),
            pltpu.VMEM((4, HOPS, 256, HEAD), BF16),
            pltpu.VMEM((2, HEAD, NX * 256), BF16),
            pltpu.VMEM((2, NY, HEAD, 256), F32),
            pltpu.VMEM((2, 2, 4, HEAD, 256), BF16),
            pltpu.VMEM((2, 2, 4, HEAD, 256), BF16),
            pltpu.VMEM((2, 256, HEAD), BF16),
            pltpu.VMEM((2, 16, 16, HEAD), BF16),
            pltpu.VMEM((2, 256, 256), BF16),
            pltpu.SemaphoreType.DMA((144,)),
            pltpu.SemaphoreType.DMA((144,)),
        ],
        compiler_params=pltpu.CompilerParams(
            collective_id=0, has_side_effects=True, vmem_limit_bytes=56307712
        ),
        name="grads",
    )(doc_blocks, queries[0], out_grad[0], keys[0], values[0], layer_input[0])
    return (key_grad[None], wv_grad)


def solution(mesh):
    in_specs = (
        P("dp", "context", None),
        P("dp", "context", None),
        P("dp", "context", None),
        P("dp", "context", None),
        P("dp", "context", None),
        P("dp", None),
    )
    out_specs = (P("dp", "context", None), P(("dp", "context"), None))
    return jax.shard_map(
        on_device, mesh=mesh, in_specs=in_specs, out_specs=out_specs, check_vma=False
    )
```

```python
import math

import jax
import jax.numpy as jnp
from jax import lax
from jax.experimental import pallas as pl
from jax.experimental.pallas import tpu as pltpu
from jax.sharding import PartitionSpec as P

HEAD = 128
BLK = 128
NX, NY, NZ = 4, 8, 8
HOPS = 4
ROWS = 1152
MASKED = -1e30
SCALE = 1.0 / math.sqrt(HEAD)
MESH = pl.DeviceIdType.MESH
F32 = jnp.float32
BF16 = jnp.bfloat16


def place():
    d = lax.axis_index("dp")
    c = lax.axis_index("context")
    return lax.rem(d, NX), lax.div(d, NX), lax.div(c, 2), lax.rem(c, 2)


def device(x, y, z, h):
    return (y * NX + x, z * 2 + h)


def around(i, by, n):
    return lax.rem(i + (by + n), n)


class Copies:
    def __init__(self, send, recv):
        self.send, self.recv, self.used, self.all = send, recv, 0, []

    def claim(self):
        self.used += 1
        return self.used - 1

    def make(self, i, src, dst, target):
        return pltpu.make_async_remote_copy(
            src_ref=src,
            dst_ref=dst,
            send_sem=self.send.at[i],
            recv_sem=self.recv.at[i],
            device_id=target,
            device_id_type=MESH,
        )

    def remote(self, src, dst, target):
        copy = self.make(self.claim(), src, dst, target)
        copy.start()
        self.all.append(copy)
        return copy

    def local(self, src, dst):
        copy = pltpu.make_async_copy(src, dst, self.send.at[self.claim()])
        copy.start()
        return copy

    def wait_sends(self, leave=0):
        while len(self.all) > leave:
            self.all.pop(0).wait_send()


def greet(targets):
    barrier = pltpu.get_barrier_semaphore()
    for target in targets:
        pl.semaphore_signal(barrier, inc=1, device_id=target, device_id_type=MESH)
    pl.semaphore_wait(barrier, len(targets))


def lanes(start, size):
    return pl.ds(pl.multiple_of(start, 128), size)


def rows_at(start, size):
    return pl.ds(pl.multiple_of(start, 128), size)


def rows16(block):
    return pl.ds(pl.multiple_of(block * 16, 16), 16)


def fill_bias(docs, bias, z):
    ends = []
    total = docs[0, 0]
    for i in range(5):
        ends.append(total)
        if i < 4:
            total = total + docs[0, i + 1]

    def doc(b):
        return sum((b >= e).astype(jnp.int32) for e in ends)

    key = lax.broadcasted_iota(jnp.int32, (BLK, BLK), 0)
    query = lax.broadcasted_iota(jnp.int32, (BLK, BLK), 1)
    for j in range(2):
        qb = 2 * z + j
        for i in range(9):
            kb = 2 * z - 2 * (i // 2) + (1 if i == 8 else i % 2)
            if i < 2 and i == j:
                block = jnp.where(key <= query, 0.0, MASKED)
            elif i == 1 and j == 0:
                block = jnp.full((BLK, BLK), MASKED, F32)
            else:
                same = (kb >= 0) & (doc(kb) == doc(qb))
                block = jnp.full((BLK, BLK), jnp.where(same, 0.0, MASKED), F32)
            bias[pl.ds(i * BLK, BLK), pl.ds(j * BLK, BLK)] = block


def kernel(
    docs, q, g, k, v, xin, key_grad, wv_grad,
    qg, qs, kv, xs, stage, relay, bias, expo, low, top, inv, dv, dk, csend, crecv, dvt, part, ysend, yrecv, zsend, zrecv, kswap,
    send, recv,
):
    x, y, z, h = place()
    ctx = z * 2 + h
    sib = device(x, y, z, 1 - h)
    up = device(x, y, around(z, 1, NZ), h)
    down = device(x, y, around(z, -1, NZ), h)
    across = [device(around(x, dx, NX), y, z, h) for dx in range(1, NX)]
    ahead = device(x, around(y, 1, NY), z, h)
    behind = device(x, around(y, -1, NY), z, h)
    column = [(y * NX + x, around(ctx, o, 16)) for o in range(1, 16)]
    mine = rows_at(h * BLK, BLK)
    copies = Copies(send, recv)

    def x_rows(dx):
        return rows_at(dx * 256 + h * BLK, BLK)

    own_k, own_v = [
        [
            copies.local(src.at[:, lanes((2 * h + a) * HEAD, HEAD)], kv.at[a, j, mine])
            for a in range(2)
        ]
        for j, src in enumerate((k, v))
    ]
    own_q = [
        copies.local(src.at[:, lanes(h * 2048, 2048)], qg.at[j, mine])
        for j, src in enumerate((q, g))
    ]
    stage_sem = send.at[copies.claim()]
    for dx in (2, 1, 3, 0):
        to = around(x, dx, NX)
        for c in range(NY):
            src = xin.at[:, lanes(c * 1024 + to * 256, 256)]
            dst = xs.at[c, x_rows(0)] if dx == 0 else stage.at[dx, c]
            pltpu.make_async_copy(src, dst, stage_sem).start()

    def staged():
        pltpu.make_async_copy(stage, stage, stage_sem).wait()

    greet(column + across + [ahead, behind])

    up_other = device(x, y, around(z, 1, NZ), 1 - h)
    hops, swapped = {}, {}

    def first_hop(j, src):
        for a in range(2):
            own = src.at[:, lanes((2 * h + a) * HEAD, HEAD)]
            other = src.at[:, lanes((2 * (1 - h) + a) * HEAD, HEAD)]
            dst = kv.at[a, j, rows_at(256 + h * BLK, BLK)]
            hops[j, a] = [copies.remote(own, dst, up), copies.remote(other, dst, up_other)]

    def swap_kv(j, src):
        for a in range(2):
            other = src.at[:, lanes((2 * (1 - h) + a) * HEAD, HEAD)]
            swapped[j, a] = copies.remote(other, kv.at[a, j, mine], sib)

    def arrived(j, a):
        for copy in hops[j, a]:
            copy.wait_recv()

    def hop(j, a, step):
        arrived(j, a)
        lo, size = (768 + 128, 128) if step == 4 else ((step - 1) * 256, 256)
        hops[j, a] = [
            copies.remote(kv.at[a, j, pl.ds(lo, size)], kv.at[a, j, pl.ds(step * 256, size)], up)
        ]

    first_hop(0, k)
    swap_kv(0, k)
    exchange = [
        copies.remote(src.at[:, lanes((1 - h) * 2048, 2048)], qg.at[j, mine], sib)
        for j, src in enumerate((q, g))
    ]

    own_x, spread_x, relays, second, pieces = [], [], [], [], []
    ways = []
    for way in (h, 1 - h):
        dx = 1 + 2 * way
        ways.append((way, dx, device(around(x, dx, NX), y, z, h)))

    def x_part(dx, lo=0, size=NY):
        return xs.at[pl.ds(lo, size), x_rows(dx)]

    for way, dx, target in ways:
        far = pl.ds(way * 4, 4)
        pieces.append((stage.at[2, far], relay.at[way], target, relays))
    for lo in (0, 4):
        for way, dx, target in ways:
            pieces.append((stage.at[dx, pl.ds(lo, 4)], x_part(dx, lo, 4), target, spread_x))

    def feed(n):
        for _ in range(n):
            src, dst, target, group = pieces.pop(0)
            group.append(copies.remote(src, dst, target))

    def relay_on():
        for i, (way, dx, target) in enumerate(ways):
            relays[i].wait_recv()
            second.append(copies.remote(relay.at[way], x_part(2, way * 4, 4), target))

    passed = {}

    def pass_on(dx):
        passed[len(passed)] = copies.remote(x_part(dx), x_part(dx), sib)

    def pass_own():
        pass_on(0)

    def pass_near():
        for copy in spread_x:
            copy.wait_recv()
        for way, dx, target in ways:
            pass_on(dx)

    def pass_far():
        for copy in second:
            copy.wait_recv()
        pass_on(2)

    contract = (((1,), (1,)), ((), ()))

    def slot_rows(slot):
        return pl.ds(slot * 256, 128 if slot == 4 else 256)

    def heads(one, *args):
        @pl.loop(0, 4)
        def _(i):
            one(*args, 2 * i)
            one(*args, 2 * i + 1)

    def score(a, slot, head):
        rows = slot_rows(slot)
        col = lanes((a * 8 + head) * HEAD, HEAD)
        s = lax.dot_general(kv[a, 0, rows], qg[0, :, col], contract, preferred_element_type=F32)
        t = s * (SCALE * math.log2(math.e)) + bias[rows, :]
        expo[a, rows, lanes(head * 256, 256)] = t
        highest = jnp.max(t.reshape(-1, 8, 256), axis=0)
        if slot > 0:
            highest = jnp.maximum(highest, top[a * 8 + head])
        top[a * 8 + head] = highest

    def weigh(a, head):
        cols = lanes(head * 256, 256)
        m = jnp.max(top[a * 8 + head], axis=0, keepdims=True)
        e = jnp.exp2(expo[a, :, cols] - m)
        expo[a, :, cols] = e
        r = 1.0 / jnp.sum(e, axis=0, keepdims=True)
        inv[a * 8 + head] = r
        low[a, :, cols] = (e * r).astype(BF16)

    def push_back(a, head):
        cols = lanes(head * 256, 256)
        col = lanes((a * 8 + head) * HEAD, HEAD)
        dp = lax.dot_general(kv[a, 1], qg[1, :, col], contract, preferred_element_type=F32)
        p = expo[a, :, cols] * inv[a * 8 + head]
        delta = jnp.sum(p * dp, axis=0, keepdims=True)
        low[a, :, cols] = (p * (dp - delta)).astype(BF16)

    def sum_heads(w, a, slot):
        rows = slot_rows(slot)
        parts[w][a, rows] = jnp.dot(low[a, rows], qs[1 - w, a], preferred_element_type=F32)

    parts = (dv, dk)
    chain = {}

    def chain_step(w, a, step):
        i = 2 * w + a
        if step > 1:
            chain[i].wait_recv()
        if step == 1:
            csend[i, 0, pl.ds(0, 128)] = parts[w][a, pl.ds(1024, 128)].astype(BF16)
            src, dst = csend.at[i, 0, pl.ds(0, 128)], crecv.at[i, 0, pl.ds(0, 128)]
        else:
            here = parts[w][a, pl.ds((5 - step) * 256, 256)]
            if step == 2:
                csend[i, 1, pl.ds(0, 128)] = here[:128].astype(BF16)
                csend[i, 1, pl.ds(128, 128)] = (
                    here[128:] + crecv[i, 0, pl.ds(0, 128)].astype(F32)
                ).astype(BF16)
            else:
                csend[i, step - 1] = (here + crecv[i, step - 2].astype(F32)).astype(BF16)
            src, dst = csend.at[i, step - 1], crecv.at[i, step - 1]
        chain[i] = copies.remote(src, dst, down)

    def chain_end(w, a):
        i = 2 * w + a
        chain[i].wait_recv()
        return parts[w][a, pl.ds(0, 256)] + crecv[i, 3].astype(F32)

    spread = {}

    def spread_dv(a):
        dvt[a, :, 0:256] = chain_end(0, a).T.astype(BF16)
        for dx in (2, 1, 3):
            spread[a, dx] = copies.remote(
                dvt.at[a, :, pl.ds(0, 256)], dvt.at[a, :, pl.ds(dx * 256, 256)], across[dx - 1]
            )

    def wait_x():
        for n in range(NX):
            passed[n].wait_recv()

    def product(a):
        for dx in range(1, NX):
            spread[a, dx].wait_recv()

        def chunk(c):
            part[a, c] = jnp.dot(dvt[a], xs[c], preferred_element_type=F32)

        near = 3 + 2 * (1 - h)
        chunk(around(y, 4, NY))
        chunk(around(y, near, NY))
        ring_step(a, 1)

        @pl.loop(0, 6)
        def _(i):
            chunk(lax.rem(y + near + 1 + h + i, NY))

    lengths = {(0, 0): 4, (0, 1): 3, (1, 0): 4, (1, 1): 3}
    ring, direct = {}, {}
    sides = []
    for way in (h, 1 - h):
        sign = 1 - 2 * way
        sides.append((sign, device(x, around(y, sign, NY), z, h)))

    def ring_step(a, step):
        for s, (sign, target) in enumerate(sides):
            n = lengths[a, s]
            if step > n:
                continue
            here = part[a, around(y, sign * (n - step + 1), NY)]
            if step > 1:
                ring[a, s].wait_recv()
                here = here + yrecv[a, s, step - 2].astype(F32)
            ysend[a, s, step - 1] = here.astype(BF16)
            ring[a, s] = copies.remote(
                ysend.at[a, s, step - 1], yrecv.at[a, s, step - 1], target
            )

    def ring_end(a):
        for s in range(2):
            ring[a, s].wait_recv()
        total = (
            part[a, y]
            + yrecv[a, 0, lengths[a, 0] - 1].astype(F32)
            + yrecv[a, 1, lengths[a, 1] - 1].astype(F32)
        )
        zsend[a] = total.T.astype(BF16)
        direct[a] = [
            copies.remote(zsend.at[a, rows16(around(ctx, o, 16))], zrecv.at[a, o], column[o - 1])
            for o in range(1, 16)
        ]

    fill_bias(docs, bias, z)
    staged()
    feed(2)
    for copy in own_q:
        copy.wait()
    exchange[0].wait_recv()
    for slot in range(4):
        for a in range(2):
            if slot < 3:
                hop(0, a, slot + 2)
            if slot == 0:
                swapped[0, a].wait_recv()
                own_k[a].wait()
            heads(score, a, slot)
        if slot == 0:
            swap_kv(1, v)
            feed(2)
        if slot == 1:
            first_hop(1, v)
        if slot == 2:
            feed(2)
    for a in range(2):
        hop(1, a, 2)
    relay_on()
    exchange[1].wait_recv()

    @pl.loop(0, 16)
    def _(i):
        a, head = lax.div(i, 8), lax.rem(i, 8)
        for j in range(2):
            qs[j, a, rows_at(head * 256, 256)] = qg[j, :, lanes(i * HEAD, HEAD)]

    arrived(0, 0)
    heads(score, 0, 4)
    heads(weigh, 0)
    sum_heads(0, 0, 4)
    chain_step(0, 0, 1)
    arrived(0, 1)
    heads(score, 1, 4)
    for a in range(2):
        hop(1, a, 3)
    heads(weigh, 1)
    sum_heads(0, 1, 4)
    chain_step(0, 1, 1)
    for a in range(2):
        hop(1, a, 4)
    sum_heads(0, 0, 3)
    chain_step(0, 0, 2)
    sum_heads(0, 1, 3)
    pass_own()
    for slot in (2, 1, 0):
        sum_heads(0, 0, slot)
    chain_step(0, 1, 2)
    for slot in (2, 1, 0):
        sum_heads(0, 1, slot)
    chain_step(0, 0, 3)

    for a in range(2):
        arrived(1, a)
        swapped[1, a].wait_recv()
        own_v[a].wait()
    order = [(a, head) for a in range(2) for head in range(8)]

    def some(n):
        for _ in range(n):
            push_back(*order.pop(0))

    some(2)
    chain_step(0, 1, 3)
    some(1)
    chain_step(0, 0, 4)
    some(3)
    chain_step(0, 1, 4)
    some(1)
    spread_dv(0)
    pass_near()
    some(1)
    sum_heads(1, 0, 4)
    chain_step(1, 0, 1)
    for slot in (3, 2, 1, 0):
        sum_heads(1, 0, slot)
    spread_dv(1)
    some(2)
    pass_far()
    chain_step(1, 0, 2)
    some(2)
    copies.wait_sends(8)
    wait_x()
    product(0)
    chain_step(1, 0, 3)
    some(2)
    ring_step(0, 2)
    product(1)
    some(2)
    ring_step(0, 3)
    ring_step(1, 2)
    sum_heads(1, 1, 4)
    chain_step(1, 1, 1)
    chain_step(1, 0, 4)
    for slot in (3, 2, 1, 0):
        sum_heads(1, 1, slot)
    ring_step(0, 4)
    ring_step(1, 3)
    chain_step(1, 1, 2)
    copies.wait_sends(8)
    ring_step(1, 4)
    ring_end(0)
    chain_step(1, 1, 3)
    ring_end(1)
    chain_step(1, 1, 4)
    copies.wait_sends(32)
    kswap[0, :, 0:HEAD] = (chain_end(1, 0) * SCALE).astype(BF16)
    kswap[0, :, HEAD : 2 * HEAD] = (chain_end(1, 1) * SCALE).astype(BF16)
    swap = copies.remote(
        kswap.at[0, rows_at((1 - h) * BLK, BLK)], kswap.at[1, pl.ds(0, BLK)], sib
    )
    key_grad[:, lanes(h * 256, 256)] = kswap[0, rows_at(h * BLK, BLK), :]
    for a in range(2):
        sums = [zsend[a, rows16(ctx), :].astype(F32), None]
        for o in range(1, 16):
            direct[a][o - 1].wait_recv()
            got = zrecv[a, o].astype(F32)
            sums[o % 2] = got if sums[o % 2] is None else sums[o % 2] + got
        wv_grad[:, lanes(h * 256 + a * HEAD, HEAD)] = sums[0]
        wv_grad[:, lanes((1 - h) * 256 + a * HEAD, HEAD)] = sums[1]
    swap.wait_recv()
    key_grad[:, lanes((1 - h) * 256, 256)] = kswap[1, pl.ds(0, BLK), :]
    copies.wait_sends()


def on_device(queries, keys, values, out_grad, layer_input, doc_blocks):
    anywhere = pl.BlockSpec(memory_space=pl.ANY)
    in_vmem = pl.BlockSpec(memory_space=pltpu.VMEM)
    key_grad, wv_grad = pl.pallas_call(
        kernel,
        out_shape=(
            jax.ShapeDtypeStruct((BLK, 512), BF16),
            jax.ShapeDtypeStruct((16, 512), F32),
        ),
        in_specs=[pl.BlockSpec(memory_space=pltpu.SMEM)] + [anywhere] * 5,
        out_specs=(in_vmem, in_vmem),
        scratch_shapes=[
            pltpu.VMEM((2, 256, 2048), BF16),
            pltpu.VMEM((2, 2, 2048, HEAD), BF16),
            pltpu.VMEM((2, 2, ROWS, HEAD), BF16),
            pltpu.VMEM((NY, NX * 256, 256), BF16),
            pltpu.VMEM((NX, NY, BLK, 256), BF16),
            pltpu.VMEM((2, 4, BLK, 256), BF16),
            pltpu.VMEM((ROWS, 256), F32),
            pltpu.VMEM((2, ROWS, 2048), F32),
            pltpu.VMEM((2, ROWS, 2048), BF16),
            pltpu.VMEM((16, 8, 256), F32),
            pltpu.VMEM((16, 1, 256), F32),
            pltpu.VMEM((2, ROWS, HEAD), F32),
            pltpu.VMEM((2, ROWS, HEAD), F32),
            pltpu.VMEM((4, HOPS, 256, HEAD), BF16),
            pltpu.VMEM((4, HOPS, 256, HEAD), BF16),
            pltpu.VMEM((2, HEAD, NX * 256), BF16),
            pltpu.VMEM((2, NY, HEAD, 256), F32),
            pltpu.VMEM((2, 2, 4, HEAD, 256), BF16),
            pltpu.VMEM((2, 2, 4, HEAD, 256), BF16),
            pltpu.VMEM((2, 256, HEAD), BF16),
            pltpu.VMEM((2, 16, 16, HEAD), BF16),
            pltpu.VMEM((2, 256, 256), BF16),
            pltpu.SemaphoreType.DMA((144,)),
            pltpu.SemaphoreType.DMA((144,)),
        ],
        compiler_params=pltpu.CompilerParams(
            collective_id=0, has_side_effects=True, vmem_limit_bytes=56 << 20
        ),
        name="grads",
    )(doc_blocks, queries[0], out_grad[0], keys[0], values[0], layer_input[0])
    return (key_grad[None], wv_grad)


def solution(mesh):
    in_specs = (
        P("dp", "context", None),
        P("dp", "context", None),
        P("dp", "context", None),
        P("dp", "context", None),
        P("dp", "context", None),
        P("dp", None),
    )
    out_specs = (P("dp", "context", None), P(("dp", "context"), None))
    return jax.shard_map(
        on_device, mesh=mesh, in_specs=in_specs, out_specs=out_specs, check_vma=False
    )
```

```python
import math

import jax
import jax.numpy as jnp
from jax import lax
from jax.experimental import pallas as pl
from jax.experimental.pallas import tpu as pltpu
from jax.sharding import PartitionSpec as P

HEAD = 128
BLK = 128
NX, NY, NZ = 4, 8, 8
HOPS = 4
ROWS = 1152
MASKED = -1e30
SCALE = 1.0 / math.sqrt(HEAD)
MESH = pl.DeviceIdType.MESH
F32 = jnp.float32
BF16 = jnp.bfloat16


def place():
    d = lax.axis_index("dp")
    c = lax.axis_index("context")
    return lax.rem(d, NX), lax.div(d, NX), lax.div(c, 2), lax.rem(c, 2)


def device(x, y, z, h):
    return (y * NX + x, z * 2 + h)


def around(i, by, n):
    return lax.rem(i + (by + n), n)


class Copies:
    def __init__(self, send, recv):
        self.send, self.recv, self.used, self.all = send, recv, 0, []

    def claim(self):
        self.used += 1
        return self.used - 1

    def make(self, i, src, dst, target):
        return pltpu.make_async_remote_copy(
            src_ref=src,
            dst_ref=dst,
            send_sem=self.send.at[i],
            recv_sem=self.recv.at[i],
            device_id=target,
            device_id_type=MESH,
        )

    def remote(self, src, dst, target):
        copy = self.make(self.claim(), src, dst, target)
        copy.start()
        self.all.append(copy)
        return copy

    def local(self, src, dst):
        copy = pltpu.make_async_copy(src, dst, self.send.at[self.claim()])
        copy.start()
        return copy

    def wait_sends(self, leave=0):
        while len(self.all) > leave:
            self.all.pop(0).wait_send()


def greet(targets):
    barrier = pltpu.get_barrier_semaphore()
    for target in targets:
        pl.semaphore_signal(barrier, inc=1, device_id=target, device_id_type=MESH)
    pl.semaphore_wait(barrier, len(targets))


def lanes(start, size):
    return pl.ds(pl.multiple_of(start, 128), size)


def rows_at(start, size):
    return pl.ds(pl.multiple_of(start, 128), size)


def rows16(block):
    return pl.ds(pl.multiple_of(block * 16, 16), 16)


def fill_bias(docs, bias, z):
    ends = []
    total = docs[0, 0]
    for i in range(5):
        ends.append(total)
        if i < 4:
            total = total + docs[0, i + 1]

    def doc(b):
        return sum((b >= e).astype(jnp.int32) for e in ends)

    key = lax.broadcasted_iota(jnp.int32, (BLK, BLK), 0)
    query = lax.broadcasted_iota(jnp.int32, (BLK, BLK), 1)
    for j in range(2):
        qb = 2 * z + j
        for i in range(9):
            kb = 2 * z - 2 * (i // 2) + (1 if i == 8 else i % 2)
            if i < 2 and i == j:
                block = jnp.where(key <= query, 0.0, MASKED)
            elif i == 1 and j == 0:
                block = jnp.full((BLK, BLK), MASKED, F32)
            else:
                same = (kb >= 0) & (doc(kb) == doc(qb))
                block = jnp.full((BLK, BLK), jnp.where(same, 0.0, MASKED), F32)
            bias[pl.ds(i * BLK, BLK), pl.ds(j * BLK, BLK)] = block


def kernel(
    docs, q, g, k, v, xin, key_grad, wv_grad,
    qg, qs, kv, xs, stage, relay, bias, expo, low, top, inv, dv, dk, csend, crecv, dvt, ysend, yrecv, zsend, zrecv, kswap,
    send, recv,
):
    x, y, z, h = place()
    ctx = z * 2 + h
    sib = device(x, y, z, 1 - h)
    up = device(x, y, around(z, 1, NZ), h)
    down = device(x, y, around(z, -1, NZ), h)
    across = [device(around(x, dx, NX), y, z, h) for dx in range(1, NX)]
    ahead = device(x, around(y, 1, NY), z, h)
    behind = device(x, around(y, -1, NY), z, h)
    column = [(y * NX + x, around(ctx, o, 16)) for o in range(1, 16)]
    mine = rows_at(h * BLK, BLK)
    copies = Copies(send, recv)

    def x_rows(dx):
        return rows_at(dx * 256 + h * BLK, BLK)

    own_k, own_v = [
        [
            copies.local(src.at[:, lanes((2 * h + a) * HEAD, HEAD)], kv.at[a, j, mine])
            for a in range(2)
        ]
        for j, src in enumerate((k, v))
    ]
    own_q = [
        copies.local(src.at[:, lanes(h * 2048, 2048)], qg.at[j, mine])
        for j, src in enumerate((q, g))
    ]
    stage_sem, own_x_sem = send.at[copies.claim()], send.at[copies.claim()]
    for dx in (2, 1, 3, 0):
        to = around(x, dx, NX)
        for c in range(NY):
            src = xin.at[:, lanes(c * 1024 + to * 256, 256)]
            if dx == 0:
                pltpu.make_async_copy(src, xs.at[c, x_rows(0)], own_x_sem).start()
            else:
                pltpu.make_async_copy(src, stage.at[dx - 1, c], stage_sem).start()

    def staged():
        pltpu.make_async_copy(stage, stage, stage_sem).wait()
        own = xs.at[:, x_rows(0)]
        pltpu.make_async_copy(own, own, own_x_sem).wait()

    greet(column + across + [ahead, behind])

    up_other = device(x, y, around(z, 1, NZ), 1 - h)
    hops, swapped = {}, {}

    def first_hop(j, src):
        for a in range(2):
            own = src.at[:, lanes((2 * h + a) * HEAD, HEAD)]
            other = src.at[:, lanes((2 * (1 - h) + a) * HEAD, HEAD)]
            dst = kv.at[a, j, rows_at(256 + h * BLK, BLK)]
            hops[j, a] = [copies.remote(own, dst, up), copies.remote(other, dst, up_other)]

    def swap_kv(j, src):
        for a in range(2):
            other = src.at[:, lanes((2 * (1 - h) + a) * HEAD, HEAD)]
            swapped[j, a] = copies.remote(other, kv.at[a, j, mine], sib)

    def arrived(j, a):
        for copy in hops[j, a]:
            copy.wait_recv()

    def hop(j, a, step):
        arrived(j, a)
        lo, size = (768 + 128, 128) if step == 4 else ((step - 1) * 256, 256)
        hops[j, a] = [
            copies.remote(kv.at[a, j, pl.ds(lo, size)], kv.at[a, j, pl.ds(step * 256, size)], up)
        ]

    first_hop(0, k)
    swap_kv(0, k)
    exchange = [
        copies.remote(src.at[:, lanes((1 - h) * 2048, 2048)], qg.at[j, mine], sib)
        for j, src in enumerate((q, g))
    ]

    own_x, spread_x, relays, second, pieces = [], [], [], [], []
    ways = []
    for way in (h, 1 - h):
        dx = 1 + 2 * way
        ways.append((way, dx, device(around(x, dx, NX), y, z, h)))

    def x_part(dx, lo=0, size=NY):
        return xs.at[pl.ds(lo, size), x_rows(dx)]

    for way, dx, target in ways:
        far = pl.ds(way * 4, 4)
        pieces.append((stage.at[1, far], relay.at[way], target, relays))
    for lo in (0, 4):
        for way, dx, target in ways:
            pieces.append((stage.at[dx - 1, pl.ds(lo, 4)], x_part(dx, lo, 4), target, spread_x))

    def feed(n):
        for _ in range(n):
            src, dst, target, group = pieces.pop(0)
            group.append(copies.remote(src, dst, target))

    def relay_on():
        for i, (way, dx, target) in enumerate(ways):
            relays[i].wait_recv()
            second.append(copies.remote(relay.at[way], x_part(2, way * 4, 4), target))

    passed = {}

    def pass_on(dx):
        passed[len(passed)] = copies.remote(x_part(dx), x_part(dx), sib)

    def pass_own():
        pass_on(0)

    def pass_near():
        for copy in spread_x:
            copy.wait_recv()
        for way, dx, target in ways:
            pass_on(dx)

    def pass_far():
        for copy in second:
            copy.wait_recv()
        pass_on(2)

    contract = (((1,), (1,)), ((), ()))

    def slot_rows(slot):
        return pl.ds(slot * 256, 128 if slot == 4 else 256)

    def heads(one, *args):
        @pl.loop(0, 2)
        def _(i):
            for j in range(4):
                one(*args, 4 * i + j)

    def score(a, slot, head):
        rows = slot_rows(slot)
        col = lanes((a * 8 + head) * HEAD, HEAD)
        s = lax.dot_general(kv[a, 0, rows], qg[0, :, col], contract, preferred_element_type=F32)
        t = s * (SCALE * math.log2(math.e)) + bias[rows, :]
        expo[a, rows, lanes(head * 256, 256)] = t
        highest = jnp.max(t.reshape(-1, 8, 256), axis=0)
        if slot > 0:
            highest = jnp.maximum(highest, top[a * 8 + head])
        top[a * 8 + head] = highest

    def weigh(a, head):
        cols = lanes(head * 256, 256)
        m = jnp.max(top[a * 8 + head], axis=0, keepdims=True)
        e = jnp.exp2(expo[a, :, cols] - m)
        expo[a, :, cols] = e
        r = 1.0 / jnp.sum(e, axis=0, keepdims=True)
        inv[a * 8 + head] = r
        low[a, :, cols] = (e * r).astype(BF16)

    def push_back(a, head):
        cols = lanes(head * 256, 256)
        col = lanes((a * 8 + head) * HEAD, HEAD)
        dp = lax.dot_general(kv[a, 1], qg[1, :, col], contract, preferred_element_type=F32)
        p = expo[a, :, cols] * inv[a * 8 + head]
        delta = jnp.sum(p * dp, axis=0, keepdims=True)
        low[a, :, cols] = (p * (dp - delta)).astype(BF16)

    def sum_heads(w, a, slot):
        rows = slot_rows(slot)
        parts[w][a, rows] = jnp.dot(low[a, rows], qs[1 - w, a], preferred_element_type=F32)

    parts = (dv, dk)
    chain = {}

    def chain_step(w, a, step):
        i = 2 * w + a
        if step > 1:
            chain[i].wait_recv()
        if step == 1:
            csend[i, 0, pl.ds(0, 128)] = parts[w][a, pl.ds(1024, 128)].astype(BF16)
            src, dst = csend.at[i, 0, pl.ds(0, 128)], crecv.at[i, 0, pl.ds(0, 128)]
        else:
            here = parts[w][a, pl.ds((5 - step) * 256, 256)]
            if step == 2:
                csend[i, 1, pl.ds(0, 128)] = here[:128].astype(BF16)
                csend[i, 1, pl.ds(128, 128)] = (
                    here[128:] + crecv[i, 0, pl.ds(0, 128)].astype(F32)
                ).astype(BF16)
            else:
                csend[i, step - 1] = (here + crecv[i, step - 2].astype(F32)).astype(BF16)
            src, dst = csend.at[i, step - 1], crecv.at[i, step - 1]
        chain[i] = copies.remote(src, dst, down)

    def chain_end(w, a):
        i = 2 * w + a
        chain[i].wait_recv()
        return parts[w][a, pl.ds(0, 256)] + crecv[i, 3].astype(F32)

    spread = {}

    def spread_dv(a):
        dvt[a, :, 0:256] = chain_end(0, a).T.astype(BF16)
        for dx in (2, 1, 3):
            spread[a, dx] = copies.remote(
                dvt.at[a, :, pl.ds(0, 256)], dvt.at[a, :, pl.ds(dx * 256, 256)], across[dx - 1]
            )

    def wait_x():
        for n in range(NX):
            passed[n].wait_recv()

    part = expo.at[0]

    def partial(a, c):
        return part[rows_at(c * HEAD, HEAD), a * 256 : (a + 1) * 256]

    def product(a):
        for dx in range(1, NX):
            spread[a, dx].wait_recv()

        def chunk(c):
            part[rows_at(c * HEAD, HEAD), a * 256 : (a + 1) * 256] = jnp.dot(
                dvt[a], xs[c], preferred_element_type=F32
            )

        near = 3 + 2 * (1 - h)
        chunk(around(y, 4, NY))
        chunk(around(y, near, NY))
        ring_step(a, 1)

        @pl.loop(0, 6)
        def _(i):
            chunk(lax.rem(y + near + 1 + h + i, NY))

    lengths = {(0, 0): 4, (0, 1): 3, (1, 0): 4, (1, 1): 3}
    ring, direct = {}, {}
    sides = []
    for way in (h, 1 - h):
        sign = 1 - 2 * way
        sides.append((sign, device(x, around(y, sign, NY), z, h)))

    def ring_step(a, step):
        for s, (sign, target) in enumerate(sides):
            n = lengths[a, s]
            if step > n:
                continue
            here = partial(a, around(y, sign * (n - step + 1), NY))
            if step > 1:
                ring[a, s].wait_recv()
                here = here + yrecv[a, s, step - 2].astype(F32)
            ysend[a, s, step - 1] = here.astype(BF16)
            ring[a, s] = copies.remote(
                ysend.at[a, s, step - 1], yrecv.at[a, s, step - 1], target
            )

    def ring_end(a):
        for s in range(2):
            ring[a, s].wait_recv()
        total = (
            partial(a, y)
            + yrecv[a, 0, lengths[a, 0] - 1].astype(F32)
            + yrecv[a, 1, lengths[a, 1] - 1].astype(F32)
        )
        zsend[a] = total.T.astype(BF16)
        direct[a] = [
            copies.remote(zsend.at[a, rows16(around(ctx, o, 16))], zrecv.at[a, o], column[o - 1])
            for o in range(1, 16)
        ]

    fill_bias(docs, bias, z)
    staged()
    feed(2)
    for copy in own_q:
        copy.wait()
    exchange[0].wait_recv()
    for slot in range(4):
        for a in range(2):
            if slot < 3:
                hop(0, a, slot + 2)
            if slot == 0:
                swapped[0, a].wait_recv()
                own_k[a].wait()
            heads(score, a, slot)
        if slot == 0:
            swap_kv(1, v)
            feed(2)
        if slot == 1:
            first_hop(1, v)
        if slot == 2:
            feed(2)
    for a in range(2):
        hop(1, a, 2)
    relay_on()
    exchange[1].wait_recv()

    @pl.loop(0, 16)
    def _(i):
        a, head = lax.div(i, 8), lax.rem(i, 8)
        for j in range(2):
            qs[j, a, rows_at(head * 256, 256)] = qg[j, :, lanes(i * HEAD, HEAD)]

    arrived(0, 0)
    heads(score, 0, 4)
    heads(weigh, 0)
    sum_heads(0, 0, 4)
    chain_step(0, 0, 1)
    arrived(0, 1)
    heads(score, 1, 4)
    for a in range(2):
        hop(1, a, 3)
    for head in range(8):
        weigh(1, head)
        if head == 1:
            sum_heads(0, 0, 3)
        elif head == 4:
            chain_step(0, 0, 2)
            sum_heads(0, 0, 2)
        elif head == 6:
            sum_heads(0, 0, 1)
    sum_heads(0, 1, 4)
    chain_step(0, 1, 1)
    for a in range(2):
        hop(1, a, 4)
    sum_heads(0, 1, 3)
    sum_heads(0, 0, 0)
    sum_heads(0, 1, 2)
    pass_own()
    chain_step(0, 0, 3)
    chain_step(0, 1, 2)

    for a in range(2):
        arrived(1, a)
        swapped[1, a].wait_recv()
        own_v[a].wait()
    order = [(a, head) for a in range(2) for head in range(8)]

    def some(n):
        for _ in range(n):
            push_back(*order.pop(0))

    sum_heads(0, 1, 1)
    sum_heads(0, 1, 0)
    some(2)
    chain_step(0, 1, 3)
    some(1)
    chain_step(0, 0, 4)
    some(3)
    chain_step(0, 1, 4)
    some(1)
    spread_dv(0)
    pass_near()
    some(1)
    sum_heads(1, 0, 4)
    chain_step(1, 0, 1)
    sum_heads(1, 0, 3)
    some(1)
    spread_dv(1)
    sum_heads(1, 0, 2)
    sum_heads(1, 0, 1)
    sum_heads(1, 0, 0)
    some(1)
    pass_far()
    chain_step(1, 0, 2)
    some(2)
    copies.wait_sends(8)
    wait_x()
    product(0)
    chain_step(1, 0, 3)
    some(2)
    ring_step(0, 2)
    product(1)
    some(2)
    ring_step(0, 3)
    ring_step(1, 2)
    sum_heads(1, 1, 4)
    chain_step(1, 1, 1)
    chain_step(1, 0, 4)
    for slot in (3, 2, 1, 0):
        sum_heads(1, 1, slot)
    ring_step(0, 4)
    ring_step(1, 3)
    chain_step(1, 1, 2)
    copies.wait_sends(8)
    ring_step(1, 4)
    ring_end(0)
    chain_step(1, 1, 3)
    ring_end(1)
    chain_step(1, 1, 4)
    copies.wait_sends(32)
    kswap[0, :, 0:HEAD] = (chain_end(1, 0) * SCALE).astype(BF16)
    kswap[0, :, HEAD : 2 * HEAD] = (chain_end(1, 1) * SCALE).astype(BF16)
    swap = copies.remote(
        kswap.at[0, rows_at((1 - h) * BLK, BLK)], kswap.at[1, pl.ds(0, BLK)], sib
    )
    key_grad[:, lanes(h * 256, 256)] = kswap[0, rows_at(h * BLK, BLK), :]
    for a in range(2):
        sums = [zsend[a, rows16(ctx), :].astype(F32), None]
        for o in range(1, 16):
            direct[a][o - 1].wait_recv()
            got = zrecv[a, o].astype(F32)
            sums[o % 2] = got if sums[o % 2] is None else sums[o % 2] + got
        wv_grad[:, lanes(h * 256 + a * HEAD, HEAD)] = sums[0]
        wv_grad[:, lanes((1 - h) * 256 + a * HEAD, HEAD)] = sums[1]
    swap.wait_recv()
    key_grad[:, lanes((1 - h) * 256, 256)] = kswap[1, pl.ds(0, BLK), :]
    copies.wait_sends()


def on_device(queries, keys, values, out_grad, layer_input, doc_blocks):
    anywhere = pl.BlockSpec(memory_space=pl.ANY)
    in_vmem = pl.BlockSpec(memory_space=pltpu.VMEM)
    key_grad, wv_grad = pl.pallas_call(
        kernel,
        out_shape=(
            jax.ShapeDtypeStruct((BLK, 512), BF16),
            jax.ShapeDtypeStruct((16, 512), F32),
        ),
        in_specs=[pl.BlockSpec(memory_space=pltpu.SMEM)] + [anywhere] * 5,
        out_specs=(in_vmem, in_vmem),
        scratch_shapes=[
            pltpu.VMEM((2, 256, 2048), BF16),
            pltpu.VMEM((2, 2, 2048, HEAD), BF16),
            pltpu.VMEM((2, 2, ROWS, HEAD), BF16),
            pltpu.VMEM((NY, NX * 256, 256), BF16),
            pltpu.VMEM((NX - 1, NY, BLK, 256), BF16),
            pltpu.VMEM((2, 4, BLK, 256), BF16),
            pltpu.VMEM((ROWS, 256), F32),
            pltpu.VMEM((2, ROWS, 2048), F32),
            pltpu.VMEM((2, ROWS, 2048), BF16),
            pltpu.VMEM((16, 8, 256), F32),
            pltpu.VMEM((16, 1, 256), F32),
            pltpu.VMEM((2, ROWS, HEAD), F32),
            pltpu.VMEM((2, ROWS, HEAD), F32),
            pltpu.VMEM((4, HOPS, 256, HEAD), BF16),
            pltpu.VMEM((4, HOPS, 256, HEAD), BF16),
            pltpu.VMEM((2, HEAD, NX * 256), BF16),
            pltpu.VMEM((2, 2, 4, HEAD, 256), BF16),
            pltpu.VMEM((2, 2, 4, HEAD, 256), BF16),
            pltpu.VMEM((2, 256, HEAD), BF16),
            pltpu.VMEM((2, 16, 16, HEAD), BF16),
            pltpu.VMEM((2, 256, 256), BF16),
            pltpu.SemaphoreType.DMA((144,)),
            pltpu.SemaphoreType.DMA((144,)),
        ],
        compiler_params=pltpu.CompilerParams(
            collective_id=0, has_side_effects=True, vmem_limit_bytes=56307712
        ),
        name="grads",
    )(doc_blocks, queries[0], out_grad[0], keys[0], values[0], layer_input[0])
    return (key_grad[None], wv_grad)


def solution(mesh):
    in_specs = (
        P("dp", "context", None),
        P("dp", "context", None),
        P("dp", "context", None),
        P("dp", "context", None),
        P("dp", "context", None),
        P("dp", None),
    )
    out_specs = (P("dp", "context", None), P(("dp", "context"), None))
    return jax.shard_map(
        on_device, mesh=mesh, in_specs=in_specs, out_specs=out_specs, check_vma=False
    )
```

```python
import math

import jax
import jax.numpy as jnp
from jax import lax
from jax.experimental import pallas as pl
from jax.experimental.pallas import tpu as pltpu
from jax.sharding import PartitionSpec as P

HEAD = 128
BLK = 128
NX, NY, NZ = 4, 8, 8
HOPS = 4
ROWS = 1152
MASKED = -1e30
SCALE = 1.0 / math.sqrt(HEAD)
MESH = pl.DeviceIdType.MESH
F32 = jnp.float32
BF16 = jnp.bfloat16


def place():
    d = lax.axis_index("dp")
    c = lax.axis_index("context")
    return lax.rem(d, NX), lax.div(d, NX), lax.div(c, 2), lax.rem(c, 2)


def device(x, y, z, h):
    return (y * NX + x, z * 2 + h)


def around(i, by, n):
    return lax.rem(i + (by + n), n)


class Copies:
    def __init__(self, send, recv):
        self.send, self.recv, self.used, self.all = send, recv, 0, []

    def claim(self):
        self.used += 1
        return self.used - 1

    def make(self, i, src, dst, target):
        return pltpu.make_async_remote_copy(
            src_ref=src,
            dst_ref=dst,
            send_sem=self.send.at[i],
            recv_sem=self.recv.at[i],
            device_id=target,
            device_id_type=MESH,
        )

    def remote(self, src, dst, target):
        copy = self.make(self.claim(), src, dst, target)
        copy.start()
        self.all.append(copy)
        return copy

    def local(self, src, dst):
        copy = pltpu.make_async_copy(src, dst, self.send.at[self.claim()])
        copy.start()
        return copy

    def wait_sends(self, leave=0):
        while len(self.all) > leave:
            self.all.pop(0).wait_send()


def greet(targets):
    barrier = pltpu.get_barrier_semaphore()
    for target in targets:
        pl.semaphore_signal(barrier, inc=1, device_id=target, device_id_type=MESH)
    pl.semaphore_wait(barrier, len(targets))


def lanes(start, size):
    return pl.ds(pl.multiple_of(start, 128), size)


def rows_at(start, size):
    return pl.ds(pl.multiple_of(start, 128), size)


def rows16(block):
    return pl.ds(pl.multiple_of(block * 16, 16), 16)


def fill_bias(docs, bias, z):
    ends = []
    total = docs[0, 0]
    for i in range(5):
        ends.append(total)
        if i < 4:
            total = total + docs[0, i + 1]

    def doc(b):
        return sum((b >= e).astype(jnp.int32) for e in ends)

    key = lax.broadcasted_iota(jnp.int32, (BLK, BLK), 0)
    query = lax.broadcasted_iota(jnp.int32, (BLK, BLK), 1)
    for j in range(2):
        qb = 2 * z + j
        for i in range(9):
            kb = 2 * z - 2 * (i // 2) + (1 if i == 8 else i % 2)
            if i < 2 and i == j:
                block = jnp.where(key <= query, 0.0, MASKED)
            elif i == 1 and j == 0:
                block = jnp.full((BLK, BLK), MASKED, F32)
            else:
                same = (kb >= 0) & (doc(kb) == doc(qb))
                block = jnp.full((BLK, BLK), jnp.where(same, 0.0, MASKED), F32)
            bias[pl.ds(i * BLK, BLK), pl.ds(j * BLK, BLK)] = block


def kernel(
    docs, q, g, k, v, xin, key_grad, wv_grad,
    qg, qs, kv, xs, stage, relay, bias, expo, low, top, inv, dv, dk, csend, crecv, dvt, ysend, yrecv, zsend, zrecv, kswap,
    send, recv,
):
    x, y, z, h = place()
    ctx = z * 2 + h
    sib = device(x, y, z, 1 - h)
    up = device(x, y, around(z, 1, NZ), h)
    down = device(x, y, around(z, -1, NZ), h)
    across = [device(around(x, dx, NX), y, z, h) for dx in range(1, NX)]
    ahead = device(x, around(y, 1, NY), z, h)
    behind = device(x, around(y, -1, NY), z, h)
    column = [(y * NX + x, around(ctx, o, 16)) for o in range(1, 16)]
    mine = rows_at(h * BLK, BLK)
    copies = Copies(send, recv)

    def x_rows(dx):
        return rows_at(dx * 256 + h * BLK, BLK)

    own_k, own_v = [
        [
            copies.local(src.at[:, lanes((2 * h + a) * HEAD, HEAD)], kv.at[a, j, mine])
            for a in range(2)
        ]
        for j, src in enumerate((k, v))
    ]
    own_q = [
        copies.local(src.at[:, lanes(h * 2048, 2048)], qg.at[j, mine])
        for j, src in enumerate((q, g))
    ]
    stage_sem, own_x_sem = send.at[copies.claim()], send.at[copies.claim()]
    for dx in (2, 1, 3, 0):
        to = around(x, dx, NX)
        for c in range(NY):
            src = xin.at[:, lanes(c * 1024 + to * 256, 256)]
            if dx == 0:
                pltpu.make_async_copy(src, xs.at[c, x_rows(0)], own_x_sem).start()
            else:
                pltpu.make_async_copy(src, stage.at[dx - 1, c], stage_sem).start()

    def staged():
        pltpu.make_async_copy(stage, stage, stage_sem).wait()
        own = xs.at[:, x_rows(0)]
        pltpu.make_async_copy(own, own, own_x_sem).wait()

    greet(column + across + [ahead, behind])

    up_other = device(x, y, around(z, 1, NZ), 1 - h)
    hops, swapped = {}, {}

    def first_hop(j, src):
        for a in range(2):
            own = src.at[:, lanes((2 * h + a) * HEAD, HEAD)]
            other = src.at[:, lanes((2 * (1 - h) + a) * HEAD, HEAD)]
            dst = kv.at[a, j, rows_at(256 + h * BLK, BLK)]
            hops[j, a] = [copies.remote(own, dst, up), copies.remote(other, dst, up_other)]

    def swap_kv(j, src):
        for a in range(2):
            other = src.at[:, lanes((2 * (1 - h) + a) * HEAD, HEAD)]
            swapped[j, a] = copies.remote(other, kv.at[a, j, mine], sib)

    def arrived(j, a):
        for copy in hops[j, a]:
            copy.wait_recv()

    def hop(j, a, step):
        arrived(j, a)
        lo, size = (768 + 128, 128) if step == 4 else ((step - 1) * 256, 256)
        hops[j, a] = [
            copies.remote(kv.at[a, j, pl.ds(lo, size)], kv.at[a, j, pl.ds(step * 256, size)], up)
        ]

    first_hop(0, k)
    swap_kv(0, k)
    exchange = [
        copies.remote(src.at[:, lanes((1 - h) * 2048, 2048)], qg.at[j, mine], sib)
        for j, src in enumerate((q, g))
    ]

    own_x, spread_x, relays, second, pieces = [], [], [], [], []
    ways = []
    for way in (h, 1 - h):
        dx = 1 + 2 * way
        ways.append((way, dx, device(around(x, dx, NX), y, z, h)))

    def x_part(dx, lo=0, size=NY):
        return xs.at[pl.ds(lo, size), x_rows(dx)]

    for way, dx, target in ways:
        far = pl.ds(way * 4, 4)
        pieces.append((stage.at[1, far], relay.at[way], target, relays))
    for lo in (0, 4):
        for way, dx, target in ways:
            pieces.append((stage.at[dx - 1, pl.ds(lo, 4)], x_part(dx, lo, 4), target, spread_x))

    def feed(n):
        for _ in range(n):
            src, dst, target, group = pieces.pop(0)
            group.append(copies.remote(src, dst, target))

    def relay_on():
        for i, (way, dx, target) in enumerate(ways):
            relays[i].wait_recv()
            second.append(copies.remote(relay.at[way], x_part(2, way * 4, 4), target))

    passed = {}

    def pass_on(dx):
        passed[len(passed)] = copies.remote(x_part(dx), x_part(dx), sib)

    def pass_own():
        pass_on(0)

    def pass_near():
        for copy in spread_x:
            copy.wait_recv()
        for way, dx, target in ways:
            pass_on(dx)

    def pass_far():
        for copy in second:
            copy.wait_recv()
        pass_on(2)

    contract = (((1,), (1,)), ((), ()))

    def slot_rows(slot):
        return pl.ds(slot * 256, 128 if slot == 4 else 256)

    def heads(one, *args):
        @pl.loop(0, 2)
        def _(i):
            for j in range(4):
                one(*args, 4 * i + j)

    def score(a, slot, head):
        rows = slot_rows(slot)
        col = lanes((a * 8 + head) * HEAD, HEAD)
        s = lax.dot_general(kv[a, 0, rows], qg[0, :, col], contract, preferred_element_type=F32)
        t = s * (SCALE * math.log2(math.e)) + bias[rows, :]
        expo[a, rows, lanes(head * 256, 256)] = t
        highest = jnp.max(t.reshape(-1, 8, 256), axis=0)
        if slot > 0:
            highest = jnp.maximum(highest, top[a * 8 + head])
        top[a * 8 + head] = highest

    def weigh(a, head):
        cols = lanes(head * 256, 256)
        m = jnp.max(top[a * 8 + head], axis=0, keepdims=True)
        e = jnp.exp2(expo[a, :, cols] - m)
        expo[a, :, cols] = e
        r = 1.0 / jnp.sum(e, axis=0, keepdims=True)
        inv[a * 8 + head] = r
        low[a, :, cols] = (e * r).astype(BF16)

    def push_back(a, head):
        cols = lanes(head * 256, 256)
        col = lanes((a * 8 + head) * HEAD, HEAD)
        dp = lax.dot_general(kv[a, 1], qg[1, :, col], contract, preferred_element_type=F32)
        p = expo[a, :, cols] * inv[a * 8 + head]
        delta = jnp.sum(p * dp, axis=0, keepdims=True)
        low[a, :, cols] = (p * (dp - delta)).astype(BF16)

    def sum_heads(w, a, slot):
        rows = slot_rows(slot)
        parts[w][a, rows] = jnp.dot(low[a, rows], qs[1 - w, a], preferred_element_type=F32)

    parts = (dv, dk)
    chain = {}

    def chain_step(w, a, step):
        i = 2 * w + a
        if step > 1:
            chain[i].wait_recv()
        if step == 1:
            csend[i, 0, pl.ds(0, 128)] = parts[w][a, pl.ds(1024, 128)].astype(BF16)
            src, dst = csend.at[i, 0, pl.ds(0, 128)], crecv.at[i, 0, pl.ds(0, 128)]
        else:
            here = parts[w][a, pl.ds((5 - step) * 256, 256)]
            if step == 2:
                csend[i, 1, pl.ds(0, 128)] = here[:128].astype(BF16)
                csend[i, 1, pl.ds(128, 128)] = (
                    here[128:] + crecv[i, 0, pl.ds(0, 128)].astype(F32)
                ).astype(BF16)
            else:
                csend[i, step - 1] = (here + crecv[i, step - 2].astype(F32)).astype(BF16)
            src, dst = csend.at[i, step - 1], crecv.at[i, step - 1]
        chain[i] = copies.remote(src, dst, down)

    def chain_end(w, a):
        i = 2 * w + a
        chain[i].wait_recv()
        return parts[w][a, pl.ds(0, 256)] + crecv[i, 3].astype(F32)

    spread = {}

    def spread_dv(a):
        dvt[a, :, 0:256] = chain_end(0, a).T.astype(BF16)
        for dx in (2, 1, 3):
            spread[a, dx] = copies.remote(
                dvt.at[a, :, pl.ds(0, 256)], dvt.at[a, :, pl.ds(dx * 256, 256)], across[dx - 1]
            )

    def wait_x():
        for n in range(NX):
            passed[n].wait_recv()

    part = expo.at[0]

    def partial(a, c):
        return part[rows_at(c * HEAD, HEAD), a * 256 : (a + 1) * 256]

    def product(a):
        for dx in range(1, NX):
            spread[a, dx].wait_recv()

        def chunk(c):
            part[rows_at(c * HEAD, HEAD), a * 256 : (a + 1) * 256] = jnp.dot(
                dvt[a], xs[c], preferred_element_type=F32
            )

        near = 3 + 2 * (1 - h)
        chunk(around(y, 4, NY))
        chunk(around(y, near, NY))
        ring_step(a, 1)

        @pl.loop(0, 6)
        def _(i):
            chunk(lax.rem(y + near + 1 + h + i, NY))

    lengths = {(0, 0): 4, (0, 1): 3, (1, 0): 4, (1, 1): 3}
    ring, direct = {}, {}
    sides = []
    for way in (h, 1 - h):
        sign = 1 - 2 * way
        sides.append((sign, device(x, around(y, sign, NY), z, h)))

    def ring_step(a, step):
        for s, (sign, target) in enumerate(sides):
            n = lengths[a, s]
            if step > n:
                continue
            here = partial(a, around(y, sign * (n - step + 1), NY))
            if step > 1:
                ring[a, s].wait_recv()
                here = here + yrecv[a, s, step - 2].astype(F32)
            ysend[a, s, step - 1] = here.astype(BF16)
            ring[a, s] = copies.remote(
                ysend.at[a, s, step - 1], yrecv.at[a, s, step - 1], target
            )

    def ring_end(a):
        for s in range(2):
            ring[a, s].wait_recv()
        total = (
            partial(a, y)
            + yrecv[a, 0, lengths[a, 0] - 1].astype(F32)
            + yrecv[a, 1, lengths[a, 1] - 1].astype(F32)
        )
        zsend[a] = total.T.astype(BF16)
        direct[a] = [
            copies.remote(zsend.at[a, rows16(around(ctx, o, 16))], zrecv.at[a, o], column[o - 1])
            for o in range(1, 16)
        ]

    fill_bias(docs, bias, z)
    staged()
    feed(2)
    for copy in own_q:
        copy.wait()
    exchange[0].wait_recv()
    for slot in range(4):
        for a in range(2):
            if slot < 3:
                hop(0, a, slot + 2)
            if slot == 0:
                swapped[0, a].wait_recv()
                own_k[a].wait()
            heads(score, a, slot)
        if slot == 0:
            swap_kv(1, v)
            feed(2)
        if slot == 1:
            first_hop(1, v)
        if slot == 2:
            feed(2)
    for a in range(2):
        hop(1, a, 2)
    relay_on()
    exchange[1].wait_recv()

    @pl.loop(0, 16)
    def _(i):
        a, head = lax.div(i, 8), lax.rem(i, 8)
        for j in range(2):
            qs[j, a, rows_at(head * 256, 256)] = qg[j, :, lanes(i * HEAD, HEAD)]

    arrived(0, 0)
    heads(score, 0, 4)
    heads(weigh, 0)
    sum_heads(0, 0, 4)
    chain_step(0, 0, 1)
    arrived(0, 1)
    heads(score, 1, 4)
    for a in range(2):
        hop(1, a, 3)
    for head in range(8):
        weigh(1, head)
        if head == 1:
            sum_heads(0, 0, 3)
        elif head == 4:
            chain_step(0, 0, 2)
            sum_heads(0, 0, 2)
        elif head == 6:
            sum_heads(0, 0, 1)
    sum_heads(0, 1, 4)
    chain_step(0, 1, 1)
    for a in range(2):
        hop(1, a, 4)
    sum_heads(0, 1, 3)
    sum_heads(0, 0, 0)
    sum_heads(0, 1, 2)
    pass_own()
    chain_step(0, 0, 3)
    chain_step(0, 1, 2)

    for a in range(2):
        arrived(1, a)
        swapped[1, a].wait_recv()
        own_v[a].wait()
    order = [(a, head) for a in range(2) for head in range(8)]

    def some(n):
        for _ in range(n):
            push_back(*order.pop(0))

    sum_heads(0, 1, 1)
    sum_heads(0, 1, 0)
    some(2)
    chain_step(0, 1, 3)
    some(1)
    chain_step(0, 0, 4)
    some(3)
    chain_step(0, 1, 4)
    some(1)
    spread_dv(0)
    some(1)
    sum_heads(1, 0, 4)
    chain_step(1, 0, 1)
    sum_heads(1, 0, 3)
    some(1)
    spread_dv(1)
    sum_heads(1, 0, 2)
    sum_heads(1, 0, 1)
    sum_heads(1, 0, 0)
    some(1)
    chain_step(1, 0, 2)
    some(3)
    chain_step(1, 0, 3)
    some(3)
    sum_heads(1, 1, 4)
    chain_step(1, 1, 1)
    sum_heads(1, 1, 3)
    chain_step(1, 0, 4)
    pass_near()
    sum_heads(1, 1, 2)
    sum_heads(1, 1, 1)
    sum_heads(1, 1, 0)
    chain_step(1, 1, 2)
    pass_far()
    copies.wait_sends(8)
    wait_x()
    product(0)
    product(1)
    chain_step(1, 1, 3)
    ring_step(0, 2)
    ring_step(1, 2)
    chain_step(1, 1, 4)
    ring_step(0, 3)
    ring_step(1, 3)
    copies.wait_sends(8)
    ring_step(0, 4)
    ring_step(1, 4)
    ring_end(0)
    ring_end(1)
    copies.wait_sends(32)
    kswap[0, :, 0:HEAD] = (chain_end(1, 0) * SCALE).astype(BF16)
    kswap[0, :, HEAD : 2 * HEAD] = (chain_end(1, 1) * SCALE).astype(BF16)
    swap = copies.remote(
        kswap.at[0, rows_at((1 - h) * BLK, BLK)], kswap.at[1, pl.ds(0, BLK)], sib
    )
    key_grad[:, lanes(h * 256, 256)] = kswap[0, rows_at(h * BLK, BLK), :]
    for a in range(2):
        sums = [zsend[a, rows16(ctx), :].astype(F32), None]
        for o in range(1, 16):
            direct[a][o - 1].wait_recv()
            got = zrecv[a, o].astype(F32)
            sums[o % 2] = got if sums[o % 2] is None else sums[o % 2] + got
        wv_grad[:, lanes(h * 256 + a * HEAD, HEAD)] = sums[0]
        wv_grad[:, lanes((1 - h) * 256 + a * HEAD, HEAD)] = sums[1]
    swap.wait_recv()
    key_grad[:, lanes((1 - h) * 256, 256)] = kswap[1, pl.ds(0, BLK), :]
    copies.wait_sends()


def on_device(queries, keys, values, out_grad, layer_input, doc_blocks):
    anywhere = pl.BlockSpec(memory_space=pl.ANY)
    in_vmem = pl.BlockSpec(memory_space=pltpu.VMEM)
    key_grad, wv_grad = pl.pallas_call(
        kernel,
        out_shape=(
            jax.ShapeDtypeStruct((BLK, 512), BF16),
            jax.ShapeDtypeStruct((16, 512), F32),
        ),
        in_specs=[pl.BlockSpec(memory_space=pltpu.SMEM)] + [anywhere] * 5,
        out_specs=(in_vmem, in_vmem),
        scratch_shapes=[
            pltpu.VMEM((2, 256, 2048), BF16),
            pltpu.VMEM((2, 2, 2048, HEAD), BF16),
            pltpu.VMEM((2, 2, ROWS, HEAD), BF16),
            pltpu.VMEM((NY, NX * 256, 256), BF16),
            pltpu.VMEM((NX - 1, NY, BLK, 256), BF16),
            pltpu.VMEM((2, 4, BLK, 256), BF16),
            pltpu.VMEM((ROWS, 256), F32),
            pltpu.VMEM((2, ROWS, 2048), F32),
            pltpu.VMEM((2, ROWS, 2048), BF16),
            pltpu.VMEM((16, 8, 256), F32),
            pltpu.VMEM((16, 1, 256), F32),
            pltpu.VMEM((2, ROWS, HEAD), F32),
            pltpu.VMEM((2, ROWS, HEAD), F32),
            pltpu.VMEM((4, HOPS, 256, HEAD), BF16),
            pltpu.VMEM((4, HOPS, 256, HEAD), BF16),
            pltpu.VMEM((2, HEAD, NX * 256), BF16),
            pltpu.VMEM((2, 2, 4, HEAD, 256), BF16),
            pltpu.VMEM((2, 2, 4, HEAD, 256), BF16),
            pltpu.VMEM((2, 256, HEAD), BF16),
            pltpu.VMEM((2, 16, 16, HEAD), BF16),
            pltpu.VMEM((2, 256, 256), BF16),
            pltpu.SemaphoreType.DMA((144,)),
            pltpu.SemaphoreType.DMA((144,)),
        ],
        compiler_params=pltpu.CompilerParams(
            collective_id=0, has_side_effects=True, vmem_limit_bytes=56307712
        ),
        name="grads",
    )(doc_blocks, queries[0], out_grad[0], keys[0], values[0], layer_input[0])
    return (key_grad[None], wv_grad)


def solution(mesh):
    in_specs = (
        P("dp", "context", None),
        P("dp", "context", None),
        P("dp", "context", None),
        P("dp", "context", None),
        P("dp", "context", None),
        P("dp", None),
    )
    out_specs = (P("dp", "context", None), P(("dp", "context"), None))
    return jax.shard_map(
        on_device, mesh=mesh, in_specs=in_specs, out_specs=out_specs, check_vma=False
    )
```

```python
import math

import jax
import jax.numpy as jnp
from jax import lax
from jax.experimental import pallas as pl
from jax.experimental.pallas import tpu as pltpu
from jax.sharding import PartitionSpec as P

HEAD = 128
BLK = 128
NX, NY, NZ = 4, 8, 8
HOPS = 4
ROWS = 1152
MASKED = -1e30
SCALE = 1.0 / math.sqrt(HEAD)
MESH = pl.DeviceIdType.MESH
F32 = jnp.float32
BF16 = jnp.bfloat16


def place():
    d = lax.axis_index("dp")
    c = lax.axis_index("context")
    return lax.rem(d, NX), lax.div(d, NX), lax.div(c, 2), lax.rem(c, 2)


def device(x, y, z, h):
    return (y * NX + x, z * 2 + h)


def around(i, by, n):
    return lax.rem(i + (by + n), n)


class Lazy:
    def __init__(self, ref):
        self.ref, self.at = ref, self

    def __getitem__(self, index):
        return lambda: self.ref.at[index]


def now(ref):
    return ref() if callable(ref) else ref


class Remote:
    def __init__(self, copies, i, src, dst, target):
        self.copies, self.i, self.src, self.dst, self.target = copies, i, src, dst, target

    def copy(self):
        return pltpu.make_async_remote_copy(
            src_ref=now(self.src),
            dst_ref=now(self.dst),
            send_sem=self.copies.send.at[self.i],
            recv_sem=self.copies.recv.at[self.i],
            device_id=self.target,
            device_id_type=MESH,
        )

    def wait_recv(self):
        self.copy().wait_recv()

    def wait_send(self):
        self.copy().wait_send()


class Copies:
    def __init__(self, send, recv):
        self.send, self.recv, self.used, self.all = send, recv, 0, []

    def claim(self):
        self.used += 1
        return self.used - 1

    def remote(self, src, dst, target):
        remote = Remote(self, self.claim(), src, dst, target)
        remote.copy().start()
        self.all.append(remote)
        return remote

    def local(self, src, dst):
        copy = pltpu.make_async_copy(now(src), now(dst), self.send.at[self.claim()])
        copy.start()
        return copy

    def wait_sends(self, leave=0):
        while len(self.all) > leave:
            self.all.pop(0).wait_send()


def greet(targets):
    barrier = pltpu.get_barrier_semaphore()
    for target in targets:
        pl.semaphore_signal(barrier, inc=1, device_id=target, device_id_type=MESH)


def greeted(count):
    pl.semaphore_wait(pltpu.get_barrier_semaphore(), count)


def lanes(start, size):
    return pl.ds(pl.multiple_of(start, 128), size)


def rows_at(start, size):
    return pl.ds(pl.multiple_of(start, 128), size)


def rows16(block):
    return pl.ds(pl.multiple_of(block * 16, 16), 16)


def fill_bias(docs, bias, z):
    ends = []
    total = docs[0, 0]
    for i in range(5):
        ends.append(total)
        if i < 4:
            total = total + docs[0, i + 1]

    def doc(b):
        return sum((b >= e).astype(jnp.int32) for e in ends)

    key = lax.broadcasted_iota(jnp.int32, (BLK, BLK), 0)
    query = lax.broadcasted_iota(jnp.int32, (BLK, BLK), 1)
    for j in range(2):
        qb = 2 * z + j
        for i in range(9):
            kb = 2 * z - 2 * (i // 2) + (1 if i == 8 else i % 2)
            if i < 2 and i == j:
                block = jnp.where(key <= query, 0.0, MASKED)
            elif i == 1 and j == 0:
                block = jnp.full((BLK, BLK), MASKED, F32)
            else:
                same = (kb >= 0) & (doc(kb) == doc(qb))
                block = jnp.full((BLK, BLK), jnp.where(same, 0.0, MASKED), F32)
            bias[pl.ds(i * BLK, BLK), pl.ds(j * BLK, BLK)] = block


def kernel(
    docs, q, g, k, v, xin, key_grad, wv_grad,
    qg, qs, kv, xs, stage, relay, bias, expo, low, top, inv, dv, dk, csend, crecv, dvt, ysend, yrecv, zsend, zrecv, kswap,
    send, recv,
):
    x, y, z, h = place()
    ctx = z * 2 + h
    sib = device(x, y, z, 1 - h)
    up = device(x, y, around(z, 1, NZ), h)
    down = device(x, y, around(z, -1, NZ), h)
    across = [device(around(x, dx, NX), y, z, h) for dx in range(1, NX)]
    ahead = device(x, around(y, 1, NY), z, h)
    behind = device(x, around(y, -1, NY), z, h)
    column = [(y * NX + x, around(ctx, o, 16)) for o in range(1, 16)]
    mine = rows_at(h * BLK, BLK)
    copies = Copies(send, recv)
    partners = column + across + [ahead, behind]
    greet(partners)

    near_rows = [rows_at((1 + 2 * way) * 256 + h * BLK, BLK) for way in (h, 1 - h)]
    static_rows = [rows_at(dx * 256 + h * BLK, BLK) for dx in range(NX)]

    def x_rows(dx):
        return static_rows[dx]

    own_k, own_v = [
        [
            copies.local(Lazy(src).at[:, lanes((2 * h + a) * HEAD, HEAD)], Lazy(kv).at[a, j, mine])
            for a in range(2)
        ]
        for j, src in enumerate((k, v))
    ]
    own_q = [
        copies.local(Lazy(src).at[:, lanes(h * 2048, 2048)], Lazy(qg).at[j, mine])
        for j, src in enumerate((q, g))
    ]
    stage_sem, own_x_sem = send.at[copies.claim()], send.at[copies.claim()]
    for dx in (2, 1, 3, 0):
        to = around(x, dx, NX)
        for c in range(NY):
            src = xin.at[:, lanes(c * 1024 + to * 256, 256)]
            if dx == 0:
                pltpu.make_async_copy(src, xs.at[c, x_rows(0)], own_x_sem).start()
            else:
                pltpu.make_async_copy(src, stage.at[dx - 1, c], stage_sem).start()

    def staged():
        pltpu.make_async_copy(stage, stage, stage_sem).wait()
        own = xs.at[:, x_rows(0)]
        pltpu.make_async_copy(own, own, own_x_sem).wait()

    greeted(len(partners))

    up_other = device(x, y, around(z, 1, NZ), 1 - h)
    hops, swapped = {}, {}

    def first_hop(j, src):
        for a in range(2):
            own = Lazy(src).at[:, lanes((2 * h + a) * HEAD, HEAD)]
            other = Lazy(src).at[:, lanes((2 * (1 - h) + a) * HEAD, HEAD)]
            dst = Lazy(kv).at[a, j, rows_at(256 + h * BLK, BLK)]
            hops[j, a] = [copies.remote(own, dst, up), copies.remote(other, dst, up_other)]

    def swap_kv(j, src):
        for a in range(2):
            other = Lazy(src).at[:, lanes((2 * (1 - h) + a) * HEAD, HEAD)]
            swapped[j, a] = copies.remote(other, Lazy(kv).at[a, j, mine], sib)

    def arrived(j, a):
        for copy in hops[j, a]:
            copy.wait_recv()

    def hop(j, a, step):
        arrived(j, a)
        lo, size = (768 + 128, 128) if step == 4 else ((step - 1) * 256, 256)
        hops[j, a] = [
            copies.remote(Lazy(kv).at[a, j, pl.ds(lo, size)], Lazy(kv).at[a, j, pl.ds(step * 256, size)], up)
        ]

    first_hop(0, k)
    swap_kv(0, k)
    exchange = [
        copies.remote(Lazy(src).at[:, lanes((1 - h) * 2048, 2048)], Lazy(qg).at[j, mine], sib)
        for j, src in enumerate((q, g))
    ]

    own_x, spread_x, relays, second, pieces = [], [], [], [], []
    ways = []
    for way in (h, 1 - h):
        dx = 1 + 2 * way
        ways.append((way, dx, device(around(x, dx, NX), y, z, h)))

    def x_part(rows, lo=0, size=NY):
        return Lazy(xs).at[pl.ds(lo, size), rows]

    for way, dx, target in ways:
        far = pl.ds(way * 4, 4)
        pieces.append((Lazy(stage).at[1, far], Lazy(relay).at[way], target, relays))
    for lo in (0, 4):
        for way, dx, target in ways:
            rows = near_rows[len(pieces) % 2]
            pieces.append((Lazy(stage).at[dx - 1, pl.ds(lo, 4)], x_part(rows, lo, 4), target, spread_x))

    def feed(n):
        for _ in range(n):
            src, dst, target, group = pieces.pop(0)
            group.append(copies.remote(src, dst, target))

    def relay_on():
        for i, (way, dx, target) in enumerate(ways):
            relays[i].wait_recv()
            second.append(copies.remote(Lazy(relay).at[way], x_part(x_rows(2), way * 4, 4), target))

    passed = {}

    parcels = [x_part(rows) for rows in (x_rows(0), *near_rows, x_rows(2))]

    def pass_on(n):
        passed[n] = copies.remote(parcels[n], parcels[n], sib)

    def pass_own():
        pass_on(0)

    def pass_near():
        for copy in spread_x:
            copy.wait_recv()
        pass_on(1)
        pass_on(2)

    def pass_far():
        for copy in second:
            copy.wait_recv()
        pass_on(3)

    contract = (((1,), (1,)), ((), ()))

    def slot_rows(slot):
        return pl.ds(slot * 256, 128 if slot == 4 else 256)

    def heads(one, first, last, *args):
        @pl.loop(first // 2, last // 2)
        def _(i):
            for j in range(2):
                head = 2 * i + j
                a = first // 8 if last - first <= 8 else lax.div(head, 8)
                one(a, head - 8 * a, *args)

    def score(a, head, slot):
        rows = slot_rows(slot)
        col = lanes((a * 8 + head) * HEAD, HEAD)
        s = lax.dot_general(kv[a, 0, rows], qg[0, :, col], contract, preferred_element_type=F32)
        t = s * (SCALE * math.log2(math.e)) + bias[rows, :]
        expo[a, rows, lanes(head * 256, 256)] = t
        highest = jnp.max(t.reshape(-1, 8, 256), axis=0)
        if slot > 0:
            highest = jnp.maximum(highest, top[a * 8 + head])
        top[a * 8 + head] = highest

    def weigh(a, head):
        cols = lanes(head * 256, 256)
        m = jnp.max(top[a * 8 + head], axis=0, keepdims=True)
        e = jnp.exp2(expo[a, :, cols] - m)
        expo[a, :, cols] = e
        r = 1.0 / jnp.sum(e, axis=0, keepdims=True)
        inv[a * 8 + head] = r
        low[a, :, cols] = (e * r).astype(BF16)

    def push_back(a, head):
        cols = lanes(head * 256, 256)
        col = lanes((a * 8 + head) * HEAD, HEAD)
        dp = lax.dot_general(kv[a, 1], qg[1, :, col], contract, preferred_element_type=F32)
        p = expo[a, :, cols] * inv[a * 8 + head]
        delta = jnp.sum(p * dp, axis=0, keepdims=True)
        low[a, :, cols] = (p * (dp - delta)).astype(BF16)

    def sum_heads(w, a, slot):
        rows = slot_rows(slot)
        parts[w][a, rows] = jnp.dot(low[a, rows], qs[1 - w, a], preferred_element_type=F32)

    parts = (dv, dk)
    chain = {}

    def chain_step(w, a, step):
        i = 2 * w + a
        if step > 1:
            chain[i].wait_recv()
        if step == 1:
            csend[i, 0, pl.ds(0, 128)] = parts[w][a, pl.ds(1024, 128)].astype(BF16)
            src, dst = Lazy(csend).at[i, 0, pl.ds(0, 128)], Lazy(crecv).at[i, 0, pl.ds(0, 128)]
        else:
            here = parts[w][a, pl.ds((5 - step) * 256, 256)]
            if step == 2:
                csend[i, 1, pl.ds(0, 128)] = here[:128].astype(BF16)
                csend[i, 1, pl.ds(128, 128)] = (
                    here[128:] + crecv[i, 0, pl.ds(0, 128)].astype(F32)
                ).astype(BF16)
            else:
                csend[i, step - 1] = (here + crecv[i, step - 2].astype(F32)).astype(BF16)
            src, dst = Lazy(csend).at[i, step - 1], Lazy(crecv).at[i, step - 1]
        chain[i] = copies.remote(src, dst, down)

    def chain_end(w, a):
        i = 2 * w + a
        chain[i].wait_recv()
        return parts[w][a, pl.ds(0, 256)] + crecv[i, 3].astype(F32)

    spread = {}

    def spread_dv(a):
        dvt[a, :, 0:256] = chain_end(0, a).T.astype(BF16)
        for dx in (2, 1, 3):
            spread[a, dx] = copies.remote(
                Lazy(dvt).at[a, :, pl.ds(0, 256)], Lazy(dvt).at[a, :, pl.ds(dx * 256, 256)], across[dx - 1]
            )

    def wait_x():
        for n in range(NX):
            passed[n].wait_recv()

    part = expo.at[0]

    def partial(a, c):
        return part[rows_at(c * HEAD, HEAD), a * 256 : (a + 1) * 256]

    def product(a):
        for dx in range(1, NX):
            spread[a, dx].wait_recv()

        def chunk(c):
            part[rows_at(c * HEAD, HEAD), a * 256 : (a + 1) * 256] = jnp.dot(
                dvt[a], xs[c], preferred_element_type=F32
            )

        near = 3 + 2 * (1 - h)
        chunk(around(y, 4, NY))
        chunk(around(y, near, NY))
        ring_step(a, 1)

        @pl.loop(0, 6)
        def _(i):
            chunk(lax.rem(y + near + 1 + h + i, NY))

    lengths = {(0, 0): 4, (0, 1): 3, (1, 0): 4, (1, 1): 3}
    ring, direct = {}, {}
    sides = []
    for way in (h, 1 - h):
        sign = 1 - 2 * way
        sides.append((sign, device(x, around(y, sign, NY), z, h)))

    def ring_step(a, step):
        for s, (sign, target) in enumerate(sides):
            n = lengths[a, s]
            if step > n:
                continue
            here = partial(a, around(y, sign * (n - step + 1), NY))
            if step > 1:
                ring[a, s].wait_recv()
                here = here + yrecv[a, s, step - 2].astype(F32)
            ysend[a, s, step - 1] = here.astype(BF16)
            ring[a, s] = copies.remote(
                Lazy(ysend).at[a, s, step - 1], Lazy(yrecv).at[a, s, step - 1], target
            )

    def ring_end(a):
        for s in range(2):
            ring[a, s].wait_recv()
        total = (
            partial(a, y)
            + yrecv[a, 0, lengths[a, 0] - 1].astype(F32)
            + yrecv[a, 1, lengths[a, 1] - 1].astype(F32)
        )
        zsend[a] = total.T.astype(BF16)
        direct[a] = [
            copies.remote(Lazy(zsend).at[a, rows16(around(ctx, o, 16))], Lazy(zrecv).at[a, o], column[o - 1])
            for o in range(1, 16)
        ]

    fill_bias(docs, bias, z)
    staged()
    feed(2)
    for copy in own_q:
        copy.wait()
    exchange[0].wait_recv()
    for slot in range(4):
        for a in range(2):
            if slot < 3:
                hop(0, a, slot + 2)
            if slot == 0:
                swapped[0, a].wait_recv()
                own_k[a].wait()
        if slot == 0:
            swap_kv(1, v)
            feed(2)
        if slot == 2:
            first_hop(1, v)
            feed(2)
        heads(score, 0, 16, slot)
    for a in range(2):
        hop(1, a, 2)
    relay_on()
    exchange[1].wait_recv()

    @pl.loop(0, 16)
    def _(i):
        a, head = lax.div(i, 8), lax.rem(i, 8)
        for j in range(2):
            qs[j, a, rows_at(head * 256, 256)] = qg[j, :, lanes(i * HEAD, HEAD)]

    for a in range(2):
        arrived(0, a)
    heads(score, 0, 16, 4)
    heads(weigh, 0, 8)
    sum_heads(0, 0, 4)
    chain_step(0, 0, 1)
    sum_heads(0, 0, 3)
    for a in range(2):
        hop(1, a, 3)
    heads(weigh, 8, 16)
    sum_heads(0, 1, 4)
    chain_step(0, 1, 1)
    chain_step(0, 0, 2)
    for a in range(2):
        hop(1, a, 4)
    sum_heads(0, 1, 3)
    sum_heads(0, 0, 2)
    sum_heads(0, 0, 1)
    sum_heads(0, 0, 0)
    sum_heads(0, 1, 2)
    pass_own()
    chain_step(0, 0, 3)
    chain_step(0, 1, 2)
    sum_heads(0, 1, 1)
    sum_heads(0, 1, 0)

    for a in range(2):
        arrived(1, a)
        swapped[1, a].wait_recv()
        own_v[a].wait()

    def after(i):
        if i == 0:
            chain_step(0, 1, 3)
        elif i == 1:
            chain_step(0, 0, 4)
        elif i == 2:
            chain_step(0, 1, 4)
        elif i == 3:
            spread_dv(0)
            pass_near()
            sum_heads(1, 0, 4)
            chain_step(1, 0, 1)
            sum_heads(1, 0, 3)
        elif i == 4:
            spread_dv(1)
            sum_heads(1, 0, 2)
            sum_heads(1, 0, 1)
            sum_heads(1, 0, 0)
            pass_far()
        elif i == 5:
            chain_step(1, 0, 2)
            wait_x()
            product(0)
        elif i == 6:
            chain_step(1, 0, 3)
            ring_step(0, 2)
            product(1)

    @pl.loop(0, 8)
    def _(i):
        a = lax.div(i, 4)
        for j in range(2):
            push_back(a, 2 * i + j - 8 * a)
        for n in range(7):
            pl.when(i == n)(lambda n=n: after(n))

    ring_step(0, 3)
    ring_step(1, 2)
    sum_heads(1, 1, 4)
    chain_step(1, 1, 1)
    chain_step(1, 0, 4)
    for slot in (3, 2, 1, 0):
        sum_heads(1, 1, slot)
    ring_step(0, 4)
    ring_step(1, 3)
    chain_step(1, 1, 2)
    copies.wait_sends(8)
    ring_step(1, 4)
    ring_end(0)
    chain_step(1, 1, 3)
    ring_end(1)
    chain_step(1, 1, 4)
    copies.wait_sends(32)
    kswap[0, :, 0:HEAD] = (chain_end(1, 0) * SCALE).astype(BF16)
    kswap[0, :, HEAD : 2 * HEAD] = (chain_end(1, 1) * SCALE).astype(BF16)
    swap = copies.remote(
        Lazy(kswap).at[0, rows_at((1 - h) * BLK, BLK)], Lazy(kswap).at[1, pl.ds(0, BLK)], sib
    )
    key_grad[:, lanes(h * 256, 256)] = kswap[0, rows_at(h * BLK, BLK), :]
    for a in range(2):
        sums = [zsend[a, rows16(ctx), :].astype(F32), None]
        for o in range(1, 16):
            direct[a][o - 1].wait_recv()
            got = zrecv[a, o].astype(F32)
            sums[o % 2] = got if sums[o % 2] is None else sums[o % 2] + got
        wv_grad[:, lanes(h * 256 + a * HEAD, HEAD)] = sums[0]
        wv_grad[:, lanes((1 - h) * 256 + a * HEAD, HEAD)] = sums[1]
    swap.wait_recv()
    key_grad[:, lanes((1 - h) * 256, 256)] = kswap[1, pl.ds(0, BLK), :]
    copies.wait_sends()


def on_device(queries, keys, values, out_grad, layer_input, doc_blocks):
    anywhere = pl.BlockSpec(memory_space=pl.ANY)
    in_vmem = pl.BlockSpec(memory_space=pltpu.VMEM)
    key_grad, wv_grad = pl.pallas_call(
        kernel,
        out_shape=(
            jax.ShapeDtypeStruct((BLK, 512), BF16),
            jax.ShapeDtypeStruct((16, 512), F32),
        ),
        in_specs=[pl.BlockSpec(memory_space=pltpu.SMEM)] + [anywhere] * 5,
        out_specs=(in_vmem, in_vmem),
        scratch_shapes=[
            pltpu.VMEM((2, 256, 2048), BF16),
            pltpu.VMEM((2, 2, 2048, HEAD), BF16),
            pltpu.VMEM((2, 2, ROWS, HEAD), BF16),
            pltpu.VMEM((NY, NX * 256, 256), BF16),
            pltpu.VMEM((NX - 1, NY, BLK, 256), BF16),
            pltpu.VMEM((2, 4, BLK, 256), BF16),
            pltpu.VMEM((ROWS, 256), F32),
            pltpu.VMEM((2, ROWS, 2048), F32),
            pltpu.VMEM((2, ROWS, 2048), BF16),
            pltpu.VMEM((16, 8, 256), F32),
            pltpu.VMEM((16, 1, 256), F32),
            pltpu.VMEM((2, ROWS, HEAD), F32),
            pltpu.VMEM((2, ROWS, HEAD), F32),
            pltpu.VMEM((4, HOPS, 256, HEAD), BF16),
            pltpu.VMEM((4, HOPS, 256, HEAD), BF16),
            pltpu.VMEM((2, HEAD, NX * 256), BF16),
            pltpu.VMEM((2, 2, 4, HEAD, 256), BF16),
            pltpu.VMEM((2, 2, 4, HEAD, 256), BF16),
            pltpu.VMEM((2, 256, HEAD), BF16),
            pltpu.VMEM((2, 16, 16, HEAD), BF16),
            pltpu.VMEM((2, 256, 256), BF16),
            pltpu.SemaphoreType.DMA((144,)),
            pltpu.SemaphoreType.DMA((144,)),
        ],
        compiler_params=pltpu.CompilerParams(
            collective_id=0, has_side_effects=True, vmem_limit_bytes=56307712
        ),
        name="grads",
    )(doc_blocks, queries[0], out_grad[0], keys[0], values[0], layer_input[0])
    return (key_grad[None], wv_grad)


def solution(mesh):
    in_specs = (
        P("dp", "context", None),
        P("dp", "context", None),
        P("dp", "context", None),
        P("dp", "context", None),
        P("dp", "context", None),
        P("dp", None),
    )
    out_specs = (P("dp", "context", None), P(("dp", "context"), None))
    return jax.shard_map(
        on_device, mesh=mesh, in_specs=in_specs, out_specs=out_specs, check_vma=False
    )
```

```python
import math

import jax
import jax.numpy as jnp
from jax import lax
from jax.experimental import pallas as pl
from jax.experimental.pallas import tpu as pltpu
from jax.sharding import PartitionSpec as P

HEAD = 128
BLK = 128
NX, NY, NZ = 4, 8, 8
HOPS = 4
ROWS = 1152
MASKED = -1e30
SCALE = 1.0 / math.sqrt(HEAD)
MESH = pl.DeviceIdType.MESH
F32 = jnp.float32
BF16 = jnp.bfloat16


def place():
    d = lax.axis_index("dp")
    c = lax.axis_index("context")
    return lax.rem(d, NX), lax.div(d, NX), lax.div(c, 2), lax.rem(c, 2)


def device(x, y, z, h):
    return (y * NX + x, z * 2 + h)


def around(i, by, n):
    return lax.rem(i + (by + n), n)


class Copies:
    def __init__(self, send, recv):
        self.send, self.recv, self.used, self.all = send, recv, 0, []

    def claim(self):
        self.used += 1
        return self.used - 1

    def make(self, i, src, dst, target):
        return pltpu.make_async_remote_copy(
            src_ref=src,
            dst_ref=dst,
            send_sem=self.send.at[i],
            recv_sem=self.recv.at[i],
            device_id=target,
            device_id_type=MESH,
        )

    def remote(self, src, dst, target):
        copy = self.make(self.claim(), src, dst, target)
        copy.start()
        self.all.append(copy)
        return copy

    def local(self, src, dst):
        copy = pltpu.make_async_copy(src, dst, self.send.at[self.claim()])
        copy.start()
        return copy

    def wait_sends(self, leave=0):
        while len(self.all) > leave:
            self.all.pop(0).wait_send()


def greet(targets):
    barrier = pltpu.get_barrier_semaphore()
    for target in targets:
        pl.semaphore_signal(barrier, inc=1, device_id=target, device_id_type=MESH)


def greeted(count):
    pl.semaphore_wait(pltpu.get_barrier_semaphore(), count)


def lanes(start, size):
    return pl.ds(pl.multiple_of(start, 128), size)


def rows_at(start, size):
    return pl.ds(pl.multiple_of(start, 128), size)


def rows16(block):
    return pl.ds(pl.multiple_of(block * 16, 16), 16)


def fill_bias(docs, bias, z):
    ends = []
    total = docs[0, 0]
    for i in range(5):
        ends.append(total)
        if i < 4:
            total = total + docs[0, i + 1]

    def doc(b):
        return sum((b >= e).astype(jnp.int32) for e in ends)

    key = lax.broadcasted_iota(jnp.int32, (BLK, BLK), 0)
    query = lax.broadcasted_iota(jnp.int32, (BLK, BLK), 1)
    for j in range(2):
        qb = 2 * z + j
        for i in range(9):
            kb = 2 * z - 2 * (i // 2) + (1 if i == 8 else i % 2)
            if i < 2 and i == j:
                block = jnp.where(key <= query, 0.0, MASKED)
            elif i == 1 and j == 0:
                block = jnp.full((BLK, BLK), MASKED, F32)
            else:
                same = (kb >= 0) & (doc(kb) == doc(qb))
                block = jnp.full((BLK, BLK), jnp.where(same, 0.0, MASKED), F32)
            bias[pl.ds(i * BLK, BLK), pl.ds(j * BLK, BLK)] = block


def kernel(
    docs, q, g, k, v, xin, key_grad, wv_grad,
    qg, qs, kv, xs, stage, relay, bias, expo, low, top, inv, dv, dk, csend, crecv, dvt, ysend, yrecv, zsend, zrecv, kswap,
    send, recv,
):
    x, y, z, h = place()
    ctx = z * 2 + h
    sib = device(x, y, z, 1 - h)
    up = device(x, y, around(z, 1, NZ), h)
    down = device(x, y, around(z, -1, NZ), h)
    across = [device(around(x, dx, NX), y, z, h) for dx in range(1, NX)]
    ahead = device(x, around(y, 1, NY), z, h)
    behind = device(x, around(y, -1, NY), z, h)
    column = [(y * NX + x, around(ctx, o, 16)) for o in range(1, 16)]
    mine = rows_at(h * BLK, BLK)
    copies = Copies(send, recv)
    partners = column + across + [ahead, behind]
    greet(partners)

    def x_rows(dx):
        return rows_at(dx * 256 + h * BLK, BLK)

    own_k, own_v = [
        [
            copies.local(src.at[:, lanes((2 * h + a) * HEAD, HEAD)], kv.at[a, j, mine])
            for a in range(2)
        ]
        for j, src in enumerate((k, v))
    ]
    own_q = [
        copies.local(src.at[:, lanes(h * 2048, 2048)], qg.at[j, mine])
        for j, src in enumerate((q, g))
    ]
    stage_sem, own_x_sem = send.at[copies.claim()], send.at[copies.claim()]
    for dx in (2, 1, 3, 0):
        to = around(x, dx, NX)
        for c in range(NY):
            src = xin.at[:, lanes(c * 1024 + to * 256, 256)]
            if dx == 0:
                pltpu.make_async_copy(src, xs.at[c, x_rows(0)], own_x_sem).start()
            else:
                pltpu.make_async_copy(src, stage.at[dx - 1, c], stage_sem).start()

    def staged():
        pltpu.make_async_copy(stage, stage, stage_sem).wait()
        own = xs.at[:, x_rows(0)]
        pltpu.make_async_copy(own, own, own_x_sem).wait()

    greeted(len(partners))

    up_other = device(x, y, around(z, 1, NZ), 1 - h)
    hops, swapped = {}, {}

    def first_hop(j, src):
        for a in range(2):
            own = src.at[:, lanes((2 * h + a) * HEAD, HEAD)]
            other = src.at[:, lanes((2 * (1 - h) + a) * HEAD, HEAD)]
            dst = kv.at[a, j, rows_at(256 + h * BLK, BLK)]
            hops[j, a] = [copies.remote(own, dst, up), copies.remote(other, dst, up_other)]

    def swap_kv(j, src):
        for a in range(2):
            other = src.at[:, lanes((2 * (1 - h) + a) * HEAD, HEAD)]
            swapped[j, a] = copies.remote(other, kv.at[a, j, mine], sib)

    def arrived(j, a):
        for copy in hops[j, a]:
            copy.wait_recv()

    def hop(j, a, step):
        arrived(j, a)
        lo, size = (768 + 128, 128) if step == 4 else ((step - 1) * 256, 256)
        hops[j, a] = [
            copies.remote(kv.at[a, j, pl.ds(lo, size)], kv.at[a, j, pl.ds(step * 256, size)], up)
        ]

    first_hop(0, k)
    swap_kv(0, k)
    exchange = [
        copies.remote(src.at[:, lanes((1 - h) * 2048, 2048)], qg.at[j, mine], sib)
        for j, src in enumerate((q, g))
    ]

    own_x, spread_x, relays, second, pieces = [], [], [], [], []
    ways = []
    for way in (h, 1 - h):
        dx = 1 + 2 * way
        ways.append((way, dx, device(around(x, dx, NX), y, z, h)))

    def x_part(dx, lo=0, size=NY):
        return xs.at[pl.ds(lo, size), x_rows(dx)]

    for way, dx, target in ways:
        far = pl.ds(way * 4, 4)
        pieces.append((stage.at[1, far], relay.at[way], target, relays))
    for lo in (0, 4):
        for way, dx, target in ways:
            pieces.append((stage.at[dx - 1, pl.ds(lo, 4)], x_part(dx, lo, 4), target, spread_x))

    def feed(n):
        for _ in range(n):
            src, dst, target, group = pieces.pop(0)
            group.append(copies.remote(src, dst, target))

    def relay_on():
        for i, (way, dx, target) in enumerate(ways):
            relays[i].wait_recv()
            second.append(copies.remote(relay.at[way], x_part(2, way * 4, 4), target))

    passed = {}

    def pass_on(dx):
        passed[len(passed)] = copies.remote(x_part(dx), x_part(dx), sib)

    def pass_own():
        pass_on(0)

    def pass_near():
        for copy in spread_x:
            copy.wait_recv()
        for way, dx, target in ways:
            pass_on(dx)

    def pass_far():
        for copy in second:
            copy.wait_recv()
        pass_on(2)

    contract = (((1,), (1,)), ((), ()))

    def slot_rows(slot):
        return pl.ds(slot * 256, 128 if slot == 4 else 256)

    def heads(one, *args):
        @pl.loop(0, 2)
        def _(i):
            for j in range(4):
                one(*args, 4 * i + j)

    def score(a, slot, head):
        rows = slot_rows(slot)
        col = lanes((a * 8 + head) * HEAD, HEAD)
        s = lax.dot_general(kv[a, 0, rows], qg[0, :, col], contract, preferred_element_type=F32)
        t = s * (SCALE * math.log2(math.e)) + bias[rows, :]
        expo[a, rows, lanes(head * 256, 256)] = t
        highest = jnp.max(t.reshape(-1, 8, 256), axis=0)
        if slot > 0:
            highest = jnp.maximum(highest, top[a * 8 + head])
        top[a * 8 + head] = highest

    def weigh(a, head):
        cols = lanes(head * 256, 256)
        col = lanes((a * 8 + head) * HEAD, HEAD)
        m = jnp.max(top[a * 8 + head], axis=0, keepdims=True)
        e = jnp.exp2(expo[a, :, cols] - m)
        expo[a, :, cols] = e
        low[a, :, cols] = e.astype(BF16)
        r = 1.0 / jnp.sum(e, axis=0, keepdims=True)
        inv[a * 8 + head] = r
        by_row = jnp.broadcast_to(r, (HEAD, 256)).T
        for j in range(2):
            qs[j, a, rows_at(head * 256, 256)] = (qg[j, :, col].astype(F32) * by_row).astype(BF16)

    def push_back(a, head):
        cols = lanes(head * 256, 256)
        col = lanes((a * 8 + head) * HEAD, HEAD)
        dp = lax.dot_general(kv[a, 1], qg[1, :, col], contract, preferred_element_type=F32)
        e = expo[a, :, cols]
        delta = jnp.sum(e * dp, axis=0, keepdims=True) * inv[a * 8 + head]
        low[a, :, cols] = (e * (dp - delta)).astype(BF16)

    def sum_heads(w, a, slot):
        rows = slot_rows(slot)
        parts[w][a, rows] = jnp.dot(low[a, rows], qs[1 - w, a], preferred_element_type=F32)

    parts = (dv, dk)
    chain = {}

    def chain_step(w, a, step):
        i = 2 * w + a
        if step > 1:
            chain[i].wait_recv()
        if step == 1:
            csend[i, 0, pl.ds(0, 128)] = parts[w][a, pl.ds(1024, 128)].astype(BF16)
            src, dst = csend.at[i, 0, pl.ds(0, 128)], crecv.at[i, 0, pl.ds(0, 128)]
        else:
            here = parts[w][a, pl.ds((5 - step) * 256, 256)]
            if step == 2:
                csend[i, 1, pl.ds(0, 128)] = here[:128].astype(BF16)
                csend[i, 1, pl.ds(128, 128)] = (
                    here[128:] + crecv[i, 0, pl.ds(0, 128)].astype(F32)
                ).astype(BF16)
            else:
                csend[i, step - 1] = (here + crecv[i, step - 2].astype(F32)).astype(BF16)
            src, dst = csend.at[i, step - 1], crecv.at[i, step - 1]
        chain[i] = copies.remote(src, dst, down)

    def chain_end(w, a):
        i = 2 * w + a
        chain[i].wait_recv()
        return parts[w][a, pl.ds(0, 256)] + crecv[i, 3].astype(F32)

    spread = {}

    def spread_dv(a):
        dvt[a, :, 0:256] = chain_end(0, a).T.astype(BF16)
        for dx in (2, 1, 3):
            spread[a, dx] = copies.remote(
                dvt.at[a, :, pl.ds(0, 256)], dvt.at[a, :, pl.ds(dx * 256, 256)], across[dx - 1]
            )

    def wait_x():
        for n in range(NX):
            passed[n].wait_recv()

    part = expo.at[0]

    def partial(a, c):
        return part[rows_at(c * HEAD, HEAD), a * 256 : (a + 1) * 256]

    def product(a):
        for dx in range(1, NX):
            spread[a, dx].wait_recv()

        def chunk(c):
            part[rows_at(c * HEAD, HEAD), a * 256 : (a + 1) * 256] = jnp.dot(
                dvt[a], xs[c], preferred_element_type=F32
            )

        near = 3 + 2 * (1 - h)
        chunk(around(y, 4, NY))
        chunk(around(y, near, NY))
        ring_step(a, 1)

        @pl.loop(0, 6)
        def _(i):
            chunk(lax.rem(y + near + 1 + h + i, NY))

    lengths = {(0, 0): 4, (0, 1): 3, (1, 0): 4, (1, 1): 3}
    ring, direct = {}, {}
    sides = []
    for way in (h, 1 - h):
        sign = 1 - 2 * way
        sides.append((sign, device(x, around(y, sign, NY), z, h)))

    def ring_step(a, step):
        for s, (sign, target) in enumerate(sides):
            n = lengths[a, s]
            if step > n:
                continue
            here = partial(a, around(y, sign * (n - step + 1), NY))
            if step > 1:
                ring[a, s].wait_recv()
                here = here + yrecv[a, s, step - 2].astype(F32)
            ysend[a, s, step - 1] = here.astype(BF16)
            ring[a, s] = copies.remote(
                ysend.at[a, s, step - 1], yrecv.at[a, s, step - 1], target
            )

    def ring_end(a):
        for s in range(2):
            ring[a, s].wait_recv()
        total = (
            partial(a, y)
            + yrecv[a, 0, lengths[a, 0] - 1].astype(F32)
            + yrecv[a, 1, lengths[a, 1] - 1].astype(F32)
        )
        zsend[a] = total.T.astype(BF16)
        direct[a] = [
            copies.remote(zsend.at[a, rows16(around(ctx, o, 16))], zrecv.at[a, o], column[o - 1])
            for o in range(1, 16)
        ]

    fill_bias(docs, bias, z)
    staged()
    feed(2)
    for copy in own_q:
        copy.wait()
    exchange[0].wait_recv()
    for slot in range(4):
        for a in range(2):
            if slot < 3:
                hop(0, a, slot + 2)
            if slot == 0:
                swapped[0, a].wait_recv()
                own_k[a].wait()
            heads(score, a, slot)
        if slot == 0:
            swap_kv(1, v)
            feed(2)
        if slot == 1:
            first_hop(1, v)
        if slot == 2:
            feed(2)
    for a in range(2):
        hop(1, a, 2)
    relay_on()
    exchange[1].wait_recv()

    arrived(0, 0)
    heads(score, 0, 4)
    heads(weigh, 0)
    sum_heads(0, 0, 4)
    chain_step(0, 0, 1)
    arrived(0, 1)
    heads(score, 1, 4)
    for a in range(2):
        hop(1, a, 3)
    for head in range(8):
        weigh(1, head)
        if head == 1:
            sum_heads(0, 0, 3)
        elif head == 4:
            chain_step(0, 0, 2)
            sum_heads(0, 0, 2)
        elif head == 6:
            sum_heads(0, 0, 1)
    sum_heads(0, 1, 4)
    chain_step(0, 1, 1)
    for a in range(2):
        hop(1, a, 4)
    sum_heads(0, 1, 3)
    sum_heads(0, 0, 0)
    sum_heads(0, 1, 2)
    pass_own()
    chain_step(0, 0, 3)
    chain_step(0, 1, 2)

    for a in range(2):
        arrived(1, a)
        swapped[1, a].wait_recv()
        own_v[a].wait()
    order = [(a, head) for a in range(2) for head in range(8)]

    def some(n):
        for _ in range(n):
            push_back(*order.pop(0))

    sum_heads(0, 1, 1)
    sum_heads(0, 1, 0)
    some(2)
    chain_step(0, 1, 3)
    some(1)
    chain_step(0, 0, 4)
    some(3)
    chain_step(0, 1, 4)
    some(1)
    spread_dv(0)
    pass_near()
    some(1)
    sum_heads(1, 0, 4)
    chain_step(1, 0, 1)
    sum_heads(1, 0, 3)
    some(1)
    spread_dv(1)
    sum_heads(1, 0, 2)
    sum_heads(1, 0, 1)
    sum_heads(1, 0, 0)
    some(1)
    pass_far()
    chain_step(1, 0, 2)
    some(2)
    copies.wait_sends(8)
    wait_x()
    product(0)
    chain_step(1, 0, 3)
    some(2)
    ring_step(0, 2)
    product(1)
    some(2)
    ring_step(0, 3)
    ring_step(1, 2)
    sum_heads(1, 1, 4)
    chain_step(1, 1, 1)
    chain_step(1, 0, 4)
    for slot in (3, 2, 1, 0):
        sum_heads(1, 1, slot)
    ring_step(0, 4)
    ring_step(1, 3)
    chain_step(1, 1, 2)
    copies.wait_sends(8)
    ring_step(1, 4)
    ring_end(0)
    chain_step(1, 1, 3)
    ring_end(1)
    chain_step(1, 1, 4)
    copies.wait_sends(32)
    kswap[0, :, 0:HEAD] = (chain_end(1, 0) * SCALE).astype(BF16)
    kswap[0, :, HEAD : 2 * HEAD] = (chain_end(1, 1) * SCALE).astype(BF16)
    swap = copies.remote(
        kswap.at[0, rows_at((1 - h) * BLK, BLK)], kswap.at[1, pl.ds(0, BLK)], sib
    )
    key_grad[:, lanes(h * 256, 256)] = kswap[0, rows_at(h * BLK, BLK), :]
    for a in range(2):
        sums = [zsend[a, rows16(ctx), :].astype(F32), None]
        for o in range(1, 16):
            direct[a][o - 1].wait_recv()
            got = zrecv[a, o].astype(F32)
            sums[o % 2] = got if sums[o % 2] is None else sums[o % 2] + got
        wv_grad[:, lanes(h * 256 + a * HEAD, HEAD)] = sums[0]
        wv_grad[:, lanes((1 - h) * 256 + a * HEAD, HEAD)] = sums[1]
    swap.wait_recv()
    key_grad[:, lanes((1 - h) * 256, 256)] = kswap[1, pl.ds(0, BLK), :]
    copies.wait_sends()


def on_device(queries, keys, values, out_grad, layer_input, doc_blocks):
    anywhere = pl.BlockSpec(memory_space=pl.ANY)
    in_vmem = pl.BlockSpec(memory_space=pltpu.VMEM)
    key_grad, wv_grad = pl.pallas_call(
        kernel,
        out_shape=(
            jax.ShapeDtypeStruct((BLK, 512), BF16),
            jax.ShapeDtypeStruct((16, 512), F32),
        ),
        in_specs=[pl.BlockSpec(memory_space=pltpu.SMEM)] + [anywhere] * 5,
        out_specs=(in_vmem, in_vmem),
        scratch_shapes=[
            pltpu.VMEM((2, 256, 2048), BF16),
            pltpu.VMEM((2, 2, 2048, HEAD), BF16),
            pltpu.VMEM((2, 2, ROWS, HEAD), BF16),
            pltpu.VMEM((NY, NX * 256, 256), BF16),
            pltpu.VMEM((NX - 1, NY, BLK, 256), BF16),
            pltpu.VMEM((2, 4, BLK, 256), BF16),
            pltpu.VMEM((ROWS, 256), F32),
            pltpu.VMEM((2, ROWS, 2048), F32),
            pltpu.VMEM((2, ROWS, 2048), BF16),
            pltpu.VMEM((16, 8, 256), F32),
            pltpu.VMEM((16, 1, 256), F32),
            pltpu.VMEM((2, ROWS, HEAD), F32),
            pltpu.VMEM((2, ROWS, HEAD), F32),
            pltpu.VMEM((4, HOPS, 256, HEAD), BF16),
            pltpu.VMEM((4, HOPS, 256, HEAD), BF16),
            pltpu.VMEM((2, HEAD, NX * 256), BF16),
            pltpu.VMEM((2, 2, 4, HEAD, 256), BF16),
            pltpu.VMEM((2, 2, 4, HEAD, 256), BF16),
            pltpu.VMEM((2, 256, HEAD), BF16),
            pltpu.VMEM((2, 16, 16, HEAD), BF16),
            pltpu.VMEM((2, 256, 256), BF16),
            pltpu.SemaphoreType.DMA((144,)),
            pltpu.SemaphoreType.DMA((144,)),
        ],
        compiler_params=pltpu.CompilerParams(
            collective_id=0, has_side_effects=True, vmem_limit_bytes=56307712
        ),
        name="grads",
    )(doc_blocks, queries[0], out_grad[0], keys[0], values[0], layer_input[0])
    return (key_grad[None], wv_grad)


def solution(mesh):
    in_specs = (
        P("dp", "context", None),
        P("dp", "context", None),
        P("dp", "context", None),
        P("dp", "context", None),
        P("dp", "context", None),
        P("dp", None),
    )
    out_specs = (P("dp", "context", None), P(("dp", "context"), None))
    return jax.shard_map(
        on_device, mesh=mesh, in_specs=in_specs, out_specs=out_specs, check_vma=False
    )
```

```python
import math

import jax
import jax.numpy as jnp
from jax import lax
from jax.experimental import pallas as pl
from jax.experimental.pallas import tpu as pltpu
from jax.sharding import PartitionSpec as P

HEAD = 128
BLK = 128
NX, NY, NZ = 4, 8, 8
HOPS = 4
ROWS = 1152
MASKED = -1e30
SCALE = 1.0 / math.sqrt(HEAD)
MESH = pl.DeviceIdType.MESH
F32 = jnp.float32
BF16 = jnp.bfloat16


def place():
    d = lax.axis_index("dp")
    c = lax.axis_index("context")
    return lax.rem(d, NX), lax.div(d, NX), lax.div(c, 2), lax.rem(c, 2)


def device(x, y, z, h):
    return (y * NX + x, z * 2 + h)


def around(i, by, n):
    return lax.rem(i + (by + n), n)


class Copies:
    def __init__(self, send, recv):
        self.send, self.recv, self.used, self.all = send, recv, 0, []

    def claim(self):
        self.used += 1
        return self.used - 1

    def make(self, i, src, dst, target):
        return pltpu.make_async_remote_copy(
            src_ref=src,
            dst_ref=dst,
            send_sem=self.send.at[i],
            recv_sem=self.recv.at[i],
            device_id=target,
            device_id_type=MESH,
        )

    def remote(self, src, dst, target):
        copy = self.make(self.claim(), src, dst, target)
        copy.start()
        self.all.append(copy)
        return copy

    def local(self, src, dst):
        copy = pltpu.make_async_copy(src, dst, self.send.at[self.claim()])
        copy.start()
        return copy

    def wait_sends(self, leave=0):
        while len(self.all) > leave:
            self.all.pop(0).wait_send()


def greet(targets):
    barrier = pltpu.get_barrier_semaphore()
    for target in targets:
        pl.semaphore_signal(barrier, inc=1, device_id=target, device_id_type=MESH)


def greeted(count):
    pl.semaphore_wait(pltpu.get_barrier_semaphore(), count)


def lanes(start, size):
    return pl.ds(pl.multiple_of(start, 128), size)


def rows_at(start, size):
    return pl.ds(pl.multiple_of(start, 128), size)


def rows16(block):
    return pl.ds(pl.multiple_of(block * 16, 16), 16)


def fill_bias(docs, bias, z):
    ends = []
    total = docs[0, 0]
    for i in range(5):
        ends.append(total)
        if i < 4:
            total = total + docs[0, i + 1]

    def doc(b):
        return sum((b >= e).astype(jnp.int32) for e in ends)

    key = lax.broadcasted_iota(jnp.int32, (BLK, BLK), 0)
    query = lax.broadcasted_iota(jnp.int32, (BLK, BLK), 1)
    for j in range(2):
        qb = 2 * z + j
        for i in range(9):
            kb = 2 * z - 2 * (i // 2) + (1 if i == 8 else i % 2)
            if i < 2 and i == j:
                block = jnp.where(key <= query, 0.0, MASKED)
            elif i == 1 and j == 0:
                block = jnp.full((BLK, BLK), MASKED, F32)
            else:
                same = (kb >= 0) & (doc(kb) == doc(qb))
                block = jnp.full((BLK, BLK), jnp.where(same, 0.0, MASKED), F32)
            bias[pl.ds(i * BLK, BLK), pl.ds(j * BLK, BLK)] = block


def kernel(
    docs, q, g, k, v, xin, key_grad, wv_grad,
    qg, qs, kv, xs, stage, relay, bias, expo, low, top, inv, dv, dk, csend, crecv, dvt, ysend, yrecv, zsend, zrecv, kswap,
    send, recv,
):
    x, y, z, h = place()
    ctx = z * 2 + h
    sib = device(x, y, z, 1 - h)
    up = device(x, y, around(z, 1, NZ), h)
    down = device(x, y, around(z, -1, NZ), h)
    across = [device(around(x, dx, NX), y, z, h) for dx in range(1, NX)]
    ahead = device(x, around(y, 1, NY), z, h)
    behind = device(x, around(y, -1, NY), z, h)
    column = [(y * NX + x, around(ctx, o, 16)) for o in range(1, 16)]
    mine = rows_at(h * BLK, BLK)
    copies = Copies(send, recv)
    partners = column + across + [ahead, behind]
    greet(partners)

    def x_rows(dx):
        return rows_at(dx * 256 + h * BLK, BLK)

    own_k, own_v = [
        [
            copies.local(src.at[:, lanes((2 * h + a) * HEAD, HEAD)], kv.at[a, j, mine])
            for a in range(2)
        ]
        for j, src in enumerate((k, v))
    ]
    own_q = [
        copies.local(src.at[:, lanes(h * 2048, 2048)], qg.at[j, mine])
        for j, src in enumerate((q, g))
    ]
    stage_sem, own_x_sem = send.at[copies.claim()], send.at[copies.claim()]
    for dx in (2, 1, 3, 0):
        to = around(x, dx, NX)
        for c in range(NY):
            src = xin.at[:, lanes(c * 1024 + to * 256, 256)]
            if dx == 0:
                pltpu.make_async_copy(src, xs.at[c, x_rows(0)], own_x_sem).start()
            else:
                pltpu.make_async_copy(src, stage.at[dx - 1, c], stage_sem).start()

    def staged():
        pltpu.make_async_copy(stage, stage, stage_sem).wait()
        own = xs.at[:, x_rows(0)]
        pltpu.make_async_copy(own, own, own_x_sem).wait()

    greeted(len(partners))

    up_other = device(x, y, around(z, 1, NZ), 1 - h)
    hops, swapped = {}, {}

    def first_hop(j, src):
        for a in range(2):
            own = src.at[:, lanes((2 * h + a) * HEAD, HEAD)]
            other = src.at[:, lanes((2 * (1 - h) + a) * HEAD, HEAD)]
            dst = kv.at[a, j, rows_at(256 + h * BLK, BLK)]
            hops[j, a] = [copies.remote(own, dst, up), copies.remote(other, dst, up_other)]

    def swap_kv(j, src):
        for a in range(2):
            other = src.at[:, lanes((2 * (1 - h) + a) * HEAD, HEAD)]
            swapped[j, a] = copies.remote(other, kv.at[a, j, mine], sib)

    def arrived(j, a):
        for copy in hops[j, a]:
            copy.wait_recv()

    def hop(j, a, step):
        arrived(j, a)
        lo, size = (768 + 128, 128) if step == 4 else ((step - 1) * 256, 256)
        hops[j, a] = [
            copies.remote(kv.at[a, j, pl.ds(lo, size)], kv.at[a, j, pl.ds(step * 256, size)], up)
        ]

    first_hop(0, k)
    swap_kv(0, k)
    exchange = [
        copies.remote(src.at[:, lanes((1 - h) * 2048, 2048)], qg.at[j, mine], sib)
        for j, src in enumerate((q, g))
    ]

    own_x, spread_x, relays, second, pieces = [], [], [], [], []
    ways = []
    for way in (h, 1 - h):
        dx = 1 + 2 * way
        ways.append((way, dx, device(around(x, dx, NX), y, z, h)))

    def x_part(dx, lo=0, size=NY):
        return xs.at[pl.ds(lo, size), x_rows(dx)]

    for way, dx, target in ways:
        far = pl.ds(way * 4, 4)
        pieces.append((stage.at[1, far], relay.at[way], target, relays))
    for lo in (0, 4):
        for way, dx, target in ways:
            pieces.append((stage.at[dx - 1, pl.ds(lo, 4)], x_part(dx, lo, 4), target, spread_x))

    def feed(n):
        for _ in range(n):
            src, dst, target, group = pieces.pop(0)
            group.append(copies.remote(src, dst, target))

    def relay_on():
        for i, (way, dx, target) in enumerate(ways):
            relays[i].wait_recv()
            second.append(copies.remote(relay.at[way], x_part(2, way * 4, 4), target))

    passed = {}

    def pass_on(dx):
        passed[len(passed)] = copies.remote(x_part(dx), x_part(dx), sib)

    def pass_own():
        pass_on(0)

    def pass_near():
        for copy in spread_x:
            copy.wait_recv()
        for way, dx, target in ways:
            pass_on(dx)

    def pass_far():
        for copy in second:
            copy.wait_recv()
        pass_on(2)

    contract = (((1,), (1,)), ((), ()))

    def slot_rows(slot):
        return pl.ds(slot * 256, 128 if slot == 4 else 256)

    def heads(one, *args):
        @pl.loop(0, 2)
        def _(i):
            for j in range(4):
                one(*args, 4 * i + j)

    def hops_of_values(step):
        for a in range(2):
            hop(1, a, step)

    def score(a, slot, head):
        rows = slot_rows(slot)
        col = lanes((a * 8 + head) * HEAD, HEAD)
        s = lax.dot_general(kv[a, 0, rows], qg[0, :, col], contract, preferred_element_type=F32)
        t = s * (SCALE * math.log2(math.e)) + bias[rows, :]
        expo[a, rows, lanes(head * 256, 256)] = t
        highest = jnp.max(t.reshape(-1, 8, 256), axis=0)
        if slot > 0:
            highest = jnp.maximum(highest, top[a * 8 + head])
        top[a * 8 + head] = highest

    def weigh(a, head):
        cols = lanes(head * 256, 256)
        col = lanes((a * 8 + head) * HEAD, HEAD)
        m = jnp.max(top[a * 8 + head], axis=0, keepdims=True)
        e = jnp.exp2(expo[a, :, cols] - m)
        expo[a, :, cols] = e
        low[a, :, cols] = e.astype(BF16)
        r = 1.0 / jnp.sum(e, axis=0, keepdims=True)
        inv[a * 8 + head] = r
        by_row = jnp.broadcast_to(r, (HEAD, 256)).T
        for j in range(2):
            qs[j, a, rows_at(head * 256, 256)] = (qg[j, :, col].astype(F32) * by_row).astype(BF16)

    def push_back(a, head):
        cols = lanes(head * 256, 256)
        col = lanes((a * 8 + head) * HEAD, HEAD)
        dp = lax.dot_general(kv[a, 1], qg[1, :, col], contract, preferred_element_type=F32)
        e = expo[a, :, cols]
        delta = jnp.sum(e * dp, axis=0, keepdims=True) * inv[a * 8 + head]
        low[a, :, cols] = (e * (dp - delta)).astype(BF16)

    def sum_heads(w, a, slot):
        rows = slot_rows(slot)
        parts[w][a, rows] = jnp.dot(low[a, rows], qs[1 - w, a], preferred_element_type=F32)

    parts = (dv, dk)
    chain = {}

    def chain_step(w, a, step):
        i = 2 * w + a
        if step > 1:
            chain[i].wait_recv()
        if step == 1:
            csend[i, 0, pl.ds(0, 128)] = parts[w][a, pl.ds(1024, 128)].astype(BF16)
            src, dst = csend.at[i, 0, pl.ds(0, 128)], crecv.at[i, 0, pl.ds(0, 128)]
        else:
            here = parts[w][a, pl.ds((5 - step) * 256, 256)]
            if step == 2:
                csend[i, 1, pl.ds(0, 128)] = here[:128].astype(BF16)
                csend[i, 1, pl.ds(128, 128)] = (
                    here[128:] + crecv[i, 0, pl.ds(0, 128)].astype(F32)
                ).astype(BF16)
            else:
                csend[i, step - 1] = (here + crecv[i, step - 2].astype(F32)).astype(BF16)
            src, dst = csend.at[i, step - 1], crecv.at[i, step - 1]
        chain[i] = copies.remote(src, dst, down)

    def chain_end(w, a):
        i = 2 * w + a
        chain[i].wait_recv()
        return parts[w][a, pl.ds(0, 256)] + crecv[i, 3].astype(F32)

    spread = {}

    def spread_dv(a):
        dvt[a, :, 0:256] = chain_end(0, a).T.astype(BF16)
        for dx in (2, 1, 3):
            spread[a, dx] = copies.remote(
                dvt.at[a, :, pl.ds(0, 256)], dvt.at[a, :, pl.ds(dx * 256, 256)], across[dx - 1]
            )

    def wait_x():
        for n in range(NX):
            passed[n].wait_recv()

    part = expo.at[0]

    def partial(a, c):
        return part[rows_at(c * HEAD, HEAD), a * 256 : (a + 1) * 256]

    def product(a):
        for dx in range(1, NX):
            spread[a, dx].wait_recv()

        def chunk(c):
            part[rows_at(c * HEAD, HEAD), a * 256 : (a + 1) * 256] = jnp.dot(
                dvt[a], xs[c], preferred_element_type=F32
            )

        near = 3 + 2 * (1 - h)
        chunk(around(y, 4, NY))
        chunk(around(y, near, NY))
        ring_step(a, 1)

        @pl.loop(0, 6)
        def _(i):
            chunk(lax.rem(y + near + 1 + h + i, NY))

    lengths = {(0, 0): 4, (0, 1): 3, (1, 0): 4, (1, 1): 3}
    ring, direct = {}, {}
    sides = []
    for way in (h, 1 - h):
        sign = 1 - 2 * way
        sides.append((sign, device(x, around(y, sign, NY), z, h)))

    def ring_step(a, step):
        for s, (sign, target) in enumerate(sides):
            n = lengths[a, s]
            if step > n:
                continue
            here = partial(a, around(y, sign * (n - step + 1), NY))
            if step > 1:
                ring[a, s].wait_recv()
                here = here + yrecv[a, s, step - 2].astype(F32)
            ysend[a, s, step - 1] = here.astype(BF16)
            ring[a, s] = copies.remote(
                ysend.at[a, s, step - 1], yrecv.at[a, s, step - 1], target
            )

    def ring_end(a):
        for s in range(2):
            ring[a, s].wait_recv()
        total = (
            partial(a, y)
            + yrecv[a, 0, lengths[a, 0] - 1].astype(F32)
            + yrecv[a, 1, lengths[a, 1] - 1].astype(F32)
        )
        zsend[a] = total.T.astype(BF16)
        direct[a] = [
            copies.remote(zsend.at[a, rows16(around(ctx, o, 16))], zrecv.at[a, o], column[o - 1])
            for o in range(1, 16)
        ]

    fill_bias(docs, bias, z)
    staged()
    feed(2)
    for copy in own_q:
        copy.wait()
    exchange[0].wait_recv()
    for slot in range(4):
        for a in range(2):
            if slot < 3:
                hop(0, a, slot + 2)
            if slot == 0:
                swapped[0, a].wait_recv()
                own_k[a].wait()
            heads(score, a, slot)
        if slot == 0:
            swap_kv(1, v)
            feed(2)
        if slot == 1:
            first_hop(1, v)
        if slot == 2:
            feed(2)
    for a in range(2):
        hop(1, a, 2)
    relay_on()
    exchange[1].wait_recv()

    arrived(0, 0)
    heads(score, 0, 4)
    for head in range(8):
        weigh(0, head)
        if head == 4:
            hops_of_values(3)
    sum_heads(0, 0, 4)
    chain_step(0, 0, 1)
    arrived(0, 1)
    heads(score, 1, 4)
    for head in range(8):
        weigh(1, head)
        if head == 1:
            sum_heads(0, 0, 3)
        elif head == 4:
            chain_step(0, 0, 2)
            sum_heads(0, 0, 2)
        elif head == 5:
            hops_of_values(4)
        elif head == 6:
            sum_heads(0, 0, 1)
    sum_heads(0, 1, 4)
    chain_step(0, 1, 1)
    sum_heads(0, 1, 3)
    sum_heads(0, 0, 0)
    sum_heads(0, 1, 2)
    pass_own()
    chain_step(0, 0, 3)
    chain_step(0, 1, 2)

    def values_here(a):
        arrived(1, a)
        swapped[1, a].wait_recv()
        own_v[a].wait()

    values_here(0)
    order = [(a, head) for a in range(2) for head in range(8)]

    def some(n):
        for _ in range(n):
            push_back(*order.pop(0))

    sum_heads(0, 1, 1)
    sum_heads(0, 1, 0)
    some(2)
    chain_step(0, 1, 3)
    some(1)
    chain_step(0, 0, 4)
    some(3)
    chain_step(0, 1, 4)
    some(1)
    spread_dv(0)
    pass_near()
    some(1)
    sum_heads(1, 0, 4)
    chain_step(1, 0, 1)
    sum_heads(1, 0, 3)
    values_here(1)
    some(1)
    spread_dv(1)
    sum_heads(1, 0, 2)
    sum_heads(1, 0, 1)
    sum_heads(1, 0, 0)
    some(1)
    pass_far()
    chain_step(1, 0, 2)
    some(2)
    copies.wait_sends(8)
    wait_x()
    product(0)
    chain_step(1, 0, 3)
    some(2)
    ring_step(0, 2)
    product(1)
    some(2)
    ring_step(0, 3)
    ring_step(1, 2)
    sum_heads(1, 1, 4)
    chain_step(1, 1, 1)
    chain_step(1, 0, 4)
    for slot in (3, 2, 1, 0):
        sum_heads(1, 1, slot)
    ring_step(0, 4)
    ring_step(1, 3)
    chain_step(1, 1, 2)
    copies.wait_sends(8)
    ring_step(1, 4)
    ring_end(0)
    chain_step(1, 1, 3)
    ring_end(1)
    chain_step(1, 1, 4)
    copies.wait_sends(32)
    kswap[0, :, 0:HEAD] = (chain_end(1, 0) * SCALE).astype(BF16)
    kswap[0, :, HEAD : 2 * HEAD] = (chain_end(1, 1) * SCALE).astype(BF16)
    swap = copies.remote(
        kswap.at[0, rows_at((1 - h) * BLK, BLK)], kswap.at[1, pl.ds(0, BLK)], sib
    )
    key_grad[:, lanes(h * 256, 256)] = kswap[0, rows_at(h * BLK, BLK), :]
    for a in range(2):
        sums = [zsend[a, rows16(ctx), :].astype(F32), None]
        for o in range(1, 16):
            direct[a][o - 1].wait_recv()
            got = zrecv[a, o].astype(F32)
            sums[o % 2] = got if sums[o % 2] is None else sums[o % 2] + got
        wv_grad[:, lanes(h * 256 + a * HEAD, HEAD)] = sums[0]
        wv_grad[:, lanes((1 - h) * 256 + a * HEAD, HEAD)] = sums[1]
    swap.wait_recv()
    key_grad[:, lanes((1 - h) * 256, 256)] = kswap[1, pl.ds(0, BLK), :]
    copies.wait_sends()


def on_device(queries, keys, values, out_grad, layer_input, doc_blocks):
    anywhere = pl.BlockSpec(memory_space=pl.ANY)
    in_vmem = pl.BlockSpec(memory_space=pltpu.VMEM)
    key_grad, wv_grad = pl.pallas_call(
        kernel,
        out_shape=(
            jax.ShapeDtypeStruct((BLK, 512), BF16),
            jax.ShapeDtypeStruct((16, 512), F32),
        ),
        in_specs=[pl.BlockSpec(memory_space=pltpu.SMEM)] + [anywhere] * 5,
        out_specs=(in_vmem, in_vmem),
        scratch_shapes=[
            pltpu.VMEM((2, 256, 2048), BF16),
            pltpu.VMEM((2, 2, 2048, HEAD), BF16),
            pltpu.VMEM((2, 2, ROWS, HEAD), BF16),
            pltpu.VMEM((NY, NX * 256, 256), BF16),
            pltpu.VMEM((NX - 1, NY, BLK, 256), BF16),
            pltpu.VMEM((2, 4, BLK, 256), BF16),
            pltpu.VMEM((ROWS, 256), F32),
            pltpu.VMEM((2, ROWS, 2048), F32),
            pltpu.VMEM((2, ROWS, 2048), BF16),
            pltpu.VMEM((16, 8, 256), F32),
            pltpu.VMEM((16, 1, 256), F32),
            pltpu.VMEM((2, ROWS, HEAD), F32),
            pltpu.VMEM((2, ROWS, HEAD), F32),
            pltpu.VMEM((4, HOPS, 256, HEAD), BF16),
            pltpu.VMEM((4, HOPS, 256, HEAD), BF16),
            pltpu.VMEM((2, HEAD, NX * 256), BF16),
            pltpu.VMEM((2, 2, 4, HEAD, 256), BF16),
            pltpu.VMEM((2, 2, 4, HEAD, 256), BF16),
            pltpu.VMEM((2, 256, HEAD), BF16),
            pltpu.VMEM((2, 16, 16, HEAD), BF16),
            pltpu.VMEM((2, 256, 256), BF16),
            pltpu.SemaphoreType.DMA((144,)),
            pltpu.SemaphoreType.DMA((144,)),
        ],
        compiler_params=pltpu.CompilerParams(
            collective_id=0, has_side_effects=True, vmem_limit_bytes=56307712
        ),
        name="grads",
    )(doc_blocks, queries[0], out_grad[0], keys[0], values[0], layer_input[0])
    return (key_grad[None], wv_grad)


def solution(mesh):
    in_specs = (
        P("dp", "context", None),
        P("dp", "context", None),
        P("dp", "context", None),
        P("dp", "context", None),
        P("dp", "context", None),
        P("dp", None),
    )
    out_specs = (P("dp", "context", None), P(("dp", "context"), None))
    return jax.shard_map(
        on_device, mesh=mesh, in_specs=in_specs, out_specs=out_specs, check_vma=False
    )
```
